32 devices in a mesh: groups: 2 (over y), dp: 8 (over z, x), tensor: 2 (over core).
Axes of the slice: x: 2, y: 2, z: 4, core: 2. Of those that a mesh axis runs over, the one named last changes fastest.
Arguments:
- tokens: bfloat16 [16384, 8192], P(('groups', 'dp'), 'tensor'), parts along dimension 0, may hold values from -6 to 6
- key_weight: bfloat16 [8192, 1024], P('tensor'), may hold values from -0.0625 to 0.0625
- down_pool: bfloat16 [80, 64, 8192], P('dp', None, 'tensor'), may hold values from -0.0625 to 0.0625
- up_pool: bfloat16 [80, 64, 1024], P('dp', None, 'tensor'), may hold values from -0.75 to 0.75
- adapter_ids: int32 [16, 4], P('groups'), parts along dimension 0, may hold values from 0 to 79, as said below
- lengths: int32 [16, 4], P(('groups', 'dp')), parts along dimension 0, may hold values from 1 to 512, 1024 in all within a row
- owner_map: int32 [160], P('groups'), parts along dimension 0, may hold values from 0 to 79, as said below
Outputs:
- keys: bfloat16 [16384, 1024], P(('groups', 'dp'), 'tensor'), parts along dimension 0
The draws below stay inside these ranges and needn't reach their ends.
There are 2 independent parts, one for each index of `groups`. The reference program is written for one: setup_inputs(seed, part) draws one part's arguments, and reference() takes and returns one part's arrays. A program takes and returns all parts, laid end to end along the dimension named above; an argument that names none is the same for every part. Nothing has to cross between parts.
Inputs may be any that keep to these rules, and one draw needn't show every extreme that they name: A permutation: adapter a sits in pool slot owner_map[a], held by dp index owner_map[a] // 10. `adapter_ids`: the 4 requests of one row name adapters held by 4 different dp indices.
All inputs are finite; a program needn't handle non-finite values.
Results may differ from the reference program's by a relative error of at most 0.001.
Values may be sent and summed in bfloat16 or wider, within the bound.
No kernel may reach another device: no remote copies, remote signals or barrier semaphores. Data moves between devices by JAX's collectives and lax.ppermute only.
A program may use at most 128 MiB of HBM per device.

```python
import math
import jax
import jax.numpy as jnp
import numpy as np
from jax import lax

D = 8192
KEY_WIDTH = 1024
RANK = 64
ADP_DEV = 10
TOK_DEV = 1024
ADAPTERS = 80
REQ = 4
PROMPT_TOKENS = 8192
N_DP = 8


def placement(key):
    return jax.random.permutation(key, ADAPTERS).astype(jnp.int32)


def draw_owner_map(key, part):
    return placement(key)


def place_target(slots, row_index, target):
    row_slots = slots[row_index]
    match_owner = row_slots // ADP_DEV == target // ADP_DEV
    position = jnp.where(jnp.any(match_owner), jnp.argmax(match_owner.astype(jnp.int32)), 0).astype(jnp.int32)
    return slots.at[row_index, position].set(target)


def draw_adapter_ids(key, part):
    table = placement(key)
    key = jax.random.fold_in(key, 11)
    owner_count_total = ADAPTERS // ADP_DEV
    first, runner_up, third, fourth = jax.random.split(key, 4)
    popularity = jax.random.permutation(first, owner_count_total)
    extra_score = jnp.where(popularity < max(owner_count_total // 8, 1), 65536, 0).astype(jnp.int32)
    owner_scores = jax.random.randint(runner_up, (owner_count_total, owner_count_total), 0, 65536).astype(jnp.int32) + extra_score[None, :]
    owner_scores = owner_scores * owner_count_total + jnp.arange(owner_count_total, dtype=jnp.int32)[None, :]
    unused, chosen = lax.top_k(owner_scores, REQ)
    left_draw = jax.random.randint(third, (owner_count_total, REQ), 0, ADP_DEV)
    right_draw = jax.random.randint(fourth, (owner_count_total, REQ), 0, ADP_DEV)
    within = jnp.minimum(left_draw, right_draw)
    slots = chosen.astype(jnp.int32) * ADP_DEV + within.astype(jnp.int32)
    slots = place_target(slots, 0, table[ADAPTERS - 1])
    slots = place_target(slots, 1, table[0])
    inverse = jnp.argsort(table, stable=True).astype(jnp.int32)
    return inverse[slots].astype(jnp.int32)


def block_scale(key, shape, cuts, least, largest):
    def one(dim, parts):
        steps = jax.random.uniform(jax.random.fold_in(jax.random.fold_in(key, 6), dim), (parts,), jnp.float32, least / len(cuts), largest / len(cuts))
        return jnp.repeat(jnp.exp(steps), shape[dim] // parts).reshape((-1,) + (1,) * (len(shape) - dim - 1))

    gain = one(*cuts[0])
    for cut in cuts[1:]:
        gain = gain * one(*cut)
    return gain


def split_up(amount, total, bound, skew):
    portions = [(1 << 20) // math.isqrt(grade ** skew) + 1 for grade in range(2, amount + 1)]
    spare, given = total - bound - (amount - 1), [1] * (amount - 1)
    while spare > 0:
        candidates = [i for i in range(amount - 1) if given[i] < bound]
        pool, left = sum([portions[i] for i in candidates]), spare
        for i in candidates:
            extra = min(bound - given[i], max(1, left * portions[i] // pool), spare)
            given[i] = given[i] + extra
            spare = spare - extra
    return np.array([bound] + given)


def ragged_sizes(stream_key, number_of, total, bound, skew):
    if number_of == 2:
        one = jax.random.randint(stream_key, (), max(1, total - bound), min(bound, total - 1) + 1)
        return jnp.stack([one, total - one])
    tallies = jnp.asarray(split_up(number_of, total, bound, skew), jnp.int32)
    couples = (number_of - 1) // 2
    source_of, sink = tallies[1:1 + 2 * couples:2], tallies[2:2 + 2 * couples:2]
    room = jnp.minimum(source_of - 1, bound - sink)
    moved = jax.random.randint(jax.random.fold_in(stream_key, 1), (couples,), 0, 1 << 20) % (room + 1)
    tallies = tallies.at[1:1 + 2 * couples:2].set(source_of - moved).at[2:2 + 2 * couples:2].set(sink + moved)
    return tallies[jax.random.permutation(jax.random.fold_in(stream_key, 2), number_of)]


def normal_values(key, dims, scale, reach, cuts=(), kind=jnp.bfloat16):
    values = jax.random.normal(key, dims, jnp.float32) * scale
    if len(cuts) > 0:
        values = block_scale(key, dims, cuts, -0.22, 0.18) * values
    return jnp.clip(values, min=-reach, max=reach).astype(kind)


def setup_inputs(seed: int = 0, part: int = 0) -> dict:
    key_of = jax.random.split(jax.random.key(seed), 8)
    part_splits = jax.random.split(jax.random.fold_in(key_of[7], part), 8)
    return {
        "tokens": normal_values(part_splits[0], (PROMPT_TOKENS, D), 1.0, 6.0, ((0, 8), (1, 2))),
        "key_weight": normal_values(key_of[1], (D, KEY_WIDTH), D ** -0.5, 0.0625, ((0, 2),)),
        "down_pool": normal_values(key_of[2], (ADAPTERS, RANK, D), D ** -0.5, 0.0625, ((0, 8), (2, 2))),
        "up_pool": normal_values(key_of[3], (ADAPTERS, RANK, KEY_WIDTH), RANK ** -0.5, 0.75, ((0, 8), (2, 2))),
        "adapter_ids": draw_adapter_ids(jax.random.fold_in(jax.random.fold_in(key_of[7], part), 71), part),
        "lengths": jax.vmap(lambda own: ragged_sizes(own, REQ, TOK_DEV, TOK_DEV // 2, 2))(jax.random.split(part_splits[5], N_DP)).reshape((N_DP, REQ)).astype(jnp.int32),
        "owner_map": draw_owner_map(jax.random.fold_in(jax.random.fold_in(key_of[7], part), 71), part),
    }


ADAPTER_SCALE = 2.0


def reference(tokens, key_weight, down_pool, up_pool, adapter_ids, lengths, owner_map):
    def one_block(items):
        rows, names, sizes = items
        slots = owner_map[names]
        down = jnp.swapaxes(down_pool[slots], 1, 2)
        code = lax.ragged_dot(rows, down, sizes.astype(jnp.int32), preferred_element_type=jnp.float32)
        upper = up_pool[slots].astype(jnp.float32)
        return lax.ragged_dot(code, upper, sizes.astype(jnp.int32), precision=lax.Precision.HIGHEST, preferred_element_type=jnp.float32)

    delta_rows = lax.map(one_block, (tokens.reshape(N_DP, TOK_DEV, D), adapter_ids, lengths))
    base_output = jnp.dot(tokens, key_weight, preferred_element_type=jnp.float32)
    return (base_output + ADAPTER_SCALE * delta_rows.reshape(PROMPT_TOKENS, KEY_WIDTH)).astype(jnp.bfloat16)
```

```python
import functools

import jax
import jax.numpy as jnp
from jax import lax
from jax.experimental import pallas as pl
from jax.experimental.pallas import tpu as pltpu
from jax.sharding import PartitionSpec as P

ADAPTER_SCALE = 2.0
MIB = 1 << 20


def pick_kernel(index, down, up, out):
    width = down.shape[2]
    out[:, :, :width] = down[...]
    out[:, :, width:] = up[...]


def pick(index, down_pool, up_pool):
    rank, width = down_pool.shape[1:]
    out_width = up_pool.shape[2]
    many = index.shape[0]
    return pl.pallas_call(
        pick_kernel,
        grid_spec=pltpu.PrefetchScalarGridSpec(
            num_scalar_prefetch=1,
            grid=(many,),
            in_specs=[
                pl.BlockSpec((1, rank, width), lambda j, index: (index[j], 0, 0)),
                pl.BlockSpec((1, rank, out_width), lambda j, index: (index[j], 0, 0)),
            ],
            out_specs=pl.BlockSpec((1, rank, width + out_width), lambda j, index: (j, 0, 0)),
        ),
        out_shape=jax.ShapeDtypeStruct((many, rank, width + out_width), down_pool.dtype),
        name="pick",
    )(index, down_pool, up_pool)


def request_of_rows(ends, count, first, rows):
    at = first + lax.broadcasted_iota(jnp.int32, (rows, 1), 0)
    which = jnp.zeros((rows, 1), jnp.int32)
    for r in range(count - 1):
        which += (at >= ends[r]).astype(jnp.int32)
    return which


def code_kernel(count, place, ends, tokens, *refs):
    blocks, out, down = refs[:count], refs[count], refs[count + 1]
    rank = out.shape[1]

    @pl.when(pl.program_id(0) == 0)
    def _():
        for r in range(count):
            down[r * rank : (r + 1) * rank, :] = blocks[r][0]

    rows = tokens.shape[0]
    full = lax.dot_general(
        tokens[...], down[...], (((1,), (1,)), ((), ())), preferred_element_type=jnp.float32
    )
    which = request_of_rows(ends, count, pl.program_id(0) * rows, rows)
    code = jnp.zeros((rows, rank), jnp.float32)
    for r in range(count):
        code = jnp.where(which == r, full[:, r * rank : (r + 1) * rank], code)
    out[...] = code


def codes(place, ends, tokens, blocks, width):
    many, features = tokens.shape
    count = place.shape[0]
    rank = blocks.shape[1]
    tile = min(256, many)
    return pl.pallas_call(
        functools.partial(code_kernel, count),
        grid_spec=pltpu.PrefetchScalarGridSpec(
            num_scalar_prefetch=2,
            grid=(many // tile,),
            in_specs=[pl.BlockSpec((tile, features), lambda i, place, ends: (i, 0))]
            + [
                pl.BlockSpec((1, rank, width), lambda i, place, ends, r=r: (place[r], 0, 0))
                for r in range(count)
            ],
            out_specs=pl.BlockSpec((tile, rank), lambda i, place, ends: (i, 0)),
            scratch_shapes=[pltpu.VMEM((count * rank, width), blocks.dtype)],
        ),
        out_shape=jax.ShapeDtypeStruct((many, rank), jnp.float32),
        compiler_params=pltpu.CompilerParams(vmem_limit_bytes=40 * MIB),
        name="codes",
    )(place, ends, tokens, *([blocks] * count))


def finish_kernel(count, parts, place, ends, *refs):
    code_parts, base_parts = refs[:parts], refs[parts : 2 * parts]
    blocks = refs[2 * parts : 2 * parts + count]
    out = refs[2 * parts + count]
    up = refs[2 * parts + count + 1]
    rank = blocks[0].shape[1]

    @pl.when(pl.program_id(0) == 0)
    def _():
        for r in range(count):
            up[r * rank : (r + 1) * rank, :] = blocks[r][0]

    rows = out.shape[0]
    code = code_parts[0][...]
    base = base_parts[0][...]
    for p in range(1, parts):
        code = code + code_parts[p][...]
        base = base + base_parts[p][...]
    which = request_of_rows(ends, count, pl.program_id(0) * rows, rows)
    zero = jnp.zeros_like(code)
    wide = jnp.concatenate([jnp.where(which == r, code, zero) for r in range(count)], axis=1)
    delta = None
    for _ in range(3):
        part = wide.astype(jnp.bfloat16)
        wide = wide - part.astype(jnp.float32)
        term = jnp.dot(part, up[...], preferred_element_type=jnp.float32)
        delta = term if delta is None else delta + term
    out[...] = (base + ADAPTER_SCALE * delta).astype(out.dtype)


def finish(place, ends, code_parts, base_parts, blocks, width):
    many, rank = code_parts[0].shape
    columns = base_parts[0].shape[1]
    count = place.shape[0]
    parts = len(code_parts)
    tile = min(256, many)
    return pl.pallas_call(
        functools.partial(finish_kernel, count, parts),
        grid_spec=pltpu.PrefetchScalarGridSpec(
            num_scalar_prefetch=2,
            grid=(many // tile,),
            in_specs=[pl.BlockSpec((tile, rank), lambda i, place, ends: (i, 0))] * parts
            + [pl.BlockSpec((tile, columns), lambda i, place, ends: (i, 0))] * parts
            + [
                pl.BlockSpec(
                    (1, rank, columns),
                    lambda i, place, ends, r=r: (place[r], 0, width // columns),
                )
                for r in range(count)
            ],
            out_specs=pl.BlockSpec((tile, columns), lambda i, place, ends: (i, 0)),
            scratch_shapes=[pltpu.VMEM((count * rank, columns), blocks.dtype)],
        ),
        out_shape=jax.ShapeDtypeStruct((many, columns), jnp.bfloat16),
        compiler_params=pltpu.CompilerParams(vmem_limit_bytes=32 * MIB),
        name="finish",
    )(place, ends, *code_parts, *base_parts, *([blocks] * count))


def gathered(parts, axis, sizes):
    held = [parts]
    for step in range(1, sizes):
        held.append(lax.ppermute(parts, axis, [(i, (i + step) % sizes) for i in range(sizes)]))
    return held


def shards(n_tensor, tokens, key_weight, down_pool, up_pool, adapter_ids, lengths, owner_map):
    member = lax.axis_index("dp")
    held, _, width = down_pool.shape
    columns = up_pool.shape[2]
    slots = owner_map[adapter_ids]
    owners = slots // held
    within = slots % held
    send_index = jnp.sum(jnp.where(owners == member, within, 0), axis=1).astype(jnp.int32)
    my_owners = lax.dynamic_index_in_dim(owners, member, 0, keepdims=False)
    ends = jnp.cumsum(lengths[0]).astype(jnp.int32)

    send = pick(send_index, down_pool, up_pool)
    blocks = lax.all_to_all(send, "dp", split_axis=0, concat_axis=0, tiled=True)

    me = lax.axis_index("tensor")
    base_parts = []
    for step in range(n_tensor):
        to = lax.rem(me + step, n_tensor)
        weight = lax.dynamic_slice_in_dim(key_weight, to * columns, columns, 1)
        part = jnp.dot(tokens, weight, preferred_element_type=jnp.float32)
        if step:
            part = lax.ppermute(
                part, "tensor", [(i, (i + step) % n_tensor) for i in range(n_tensor)]
            )
        base_parts.append(part)

    code = codes(my_owners, ends, tokens, blocks, width)
    code_parts = gathered(code, "tensor", n_tensor)
    return finish(my_owners, ends, code_parts, base_parts, blocks, width)


def solution(mesh):
    placed = (
        P(("groups", "dp"), "tensor"),
        P("tensor", None),
        P("dp", None, "tensor"),
        P("dp", None, "tensor"),
        P("groups", None),
        P(("groups", "dp"), None),
        P("groups"),
    )
    return jax.shard_map(
        functools.partial(shards, mesh.shape["tensor"]),
        mesh=mesh,
        in_specs=placed,
        out_specs=P(("groups", "dp"), "tensor"),
        check_vma=False,
    )
```

```python
import functools

import jax
import jax.numpy as jnp
from jax import lax
from jax.experimental import pallas as pl
from jax.experimental.pallas import tpu as pltpu
from jax.sharding import PartitionSpec as P

ADAPTER_SCALE = 2.0
MIB = 1 << 20


def pick_kernel(index, down, up, out):
    width = down.shape[2]
    out[:, :, :width] = down[...]
    out[:, :, width:] = up[...]


def pick(index, down_pool, up_pool):
    rank, width = down_pool.shape[1:]
    out_width = up_pool.shape[2]
    many = index.shape[0]
    return pl.pallas_call(
        pick_kernel,
        grid_spec=pltpu.PrefetchScalarGridSpec(
            num_scalar_prefetch=1,
            grid=(many,),
            in_specs=[
                pl.BlockSpec((1, rank, width), lambda j, index: (index[j], 0, 0)),
                pl.BlockSpec((1, rank, out_width), lambda j, index: (index[j], 0, 0)),
            ],
            out_specs=pl.BlockSpec((1, rank, width + out_width), lambda j, index: (j, 0, 0)),
        ),
        out_shape=jax.ShapeDtypeStruct((many, rank, width + out_width), down_pool.dtype),
        name="pick",
    )(index, down_pool, up_pool)


def request_of_rows(ends, count, first, rows):
    at = first + lax.broadcasted_iota(jnp.int32, (rows, 1), 0)
    which = jnp.zeros((rows, 1), jnp.int32)
    for r in range(count - 1):
        which += (at >= ends[r]).astype(jnp.int32)
    return which


def code_kernel(count, place, ends, tokens, *refs):
    blocks, out, down = refs[:count], refs[count], refs[count + 1]
    rank = out.shape[1]

    @pl.when(pl.program_id(0) == 0)
    def _():
        for r in range(count):
            down[r * rank : (r + 1) * rank, :] = blocks[r][0]

    rows = tokens.shape[0]
    full = lax.dot_general(
        tokens[...], down[...], (((1,), (1,)), ((), ())), preferred_element_type=jnp.float32
    )
    which = request_of_rows(ends, count, pl.program_id(0) * rows, rows)
    code = jnp.zeros((rows, rank), jnp.float32)
    for r in range(count):
        code = jnp.where(which == r, full[:, r * rank : (r + 1) * rank], code)
    out[...] = code


def codes(place, ends, tokens, blocks, width):
    many, features = tokens.shape
    count = place.shape[0]
    rank = blocks.shape[1]
    tile = min(256, many)
    return pl.pallas_call(
        functools.partial(code_kernel, count),
        grid_spec=pltpu.PrefetchScalarGridSpec(
            num_scalar_prefetch=2,
            grid=(many // tile,),
            in_specs=[pl.BlockSpec((tile, features), lambda i, place, ends: (i, 0))]
            + [
                pl.BlockSpec((1, rank, width), lambda i, place, ends, r=r: (place[r], 0, 0))
                for r in range(count)
            ],
            out_specs=pl.BlockSpec((tile, rank), lambda i, place, ends: (i, 0)),
            scratch_shapes=[pltpu.VMEM((count * rank, width), blocks.dtype)],
        ),
        out_shape=jax.ShapeDtypeStruct((many, rank), jnp.float32),
        compiler_params=pltpu.CompilerParams(vmem_limit_bytes=40 * MIB),
        name="codes",
    )(place, ends, tokens, *([blocks] * count))


def finish_kernel(count, parts, place, ends, *refs):
    code_parts, base_parts = refs[:parts], refs[parts : 2 * parts]
    blocks = refs[2 * parts : 2 * parts + count]
    out = refs[2 * parts + count]
    up = refs[2 * parts + count + 1]
    rank = blocks[0].shape[1]

    @pl.when(pl.program_id(0) == 0)
    def _():
        for r in range(count):
            up[r * rank : (r + 1) * rank, :] = blocks[r][0]

    rows = out.shape[0]
    code = code_parts[0][...]
    base = base_parts[0][...]
    for p in range(1, parts):
        code = code + code_parts[p][...]
        base = base + base_parts[p][...]
    which = request_of_rows(ends, count, pl.program_id(0) * rows, rows)
    zero = jnp.zeros_like(code)
    wide = jnp.concatenate([jnp.where(which == r, code, zero) for r in range(count)], axis=1)
    delta = None
    for _ in range(3):
        part = wide.astype(jnp.bfloat16)
        wide = wide - part.astype(jnp.float32)
        term = jnp.dot(part, up[...], preferred_element_type=jnp.float32)
        delta = term if delta is None else delta + term
    out[...] = (base + ADAPTER_SCALE * delta).astype(out.dtype)


def finish(place, ends, code_parts, base_parts, blocks, width):
    many, rank = code_parts[0].shape
    columns = base_parts[0].shape[1]
    count = place.shape[0]
    parts = len(code_parts)
    tile = min(256, many)
    return pl.pallas_call(
        functools.partial(finish_kernel, count, parts),
        grid_spec=pltpu.PrefetchScalarGridSpec(
            num_scalar_prefetch=2,
            grid=(many // tile,),
            in_specs=[pl.BlockSpec((tile, rank), lambda i, place, ends: (i, 0))] * parts
            + [pl.BlockSpec((tile, columns), lambda i, place, ends: (i, 0))] * parts
            + [
                pl.BlockSpec(
                    (1, rank, columns),
                    lambda i, place, ends, r=r: (place[r], 0, width // columns),
                )
                for r in range(count)
            ],
            out_specs=pl.BlockSpec((tile, columns), lambda i, place, ends: (i, 0)),
            scratch_shapes=[pltpu.VMEM((count * rank, columns), blocks.dtype)],
        ),
        out_shape=jax.ShapeDtypeStruct((many, columns), jnp.bfloat16),
        compiler_params=pltpu.CompilerParams(vmem_limit_bytes=32 * MIB),
        name="finish",
    )(place, ends, *code_parts, *base_parts, *([blocks] * count))


def gathered(parts, axis, sizes):
    held = [parts]
    for step in range(1, sizes):
        held.append(lax.ppermute(parts, axis, [(i, (i + step) % sizes) for i in range(sizes)]))
    return held


Z_STEPS = 10
X_STEPS = 11


def route(slots, held, planes):
    rows, req = slots.shape
    n = rows * req
    item = jnp.arange(n, dtype=jnp.int32)
    slot = slots.reshape(n)
    row = item // req
    dest, side = row // 2, row % 2
    owner = slot // held
    src, col = owner // 2, owner % 2
    same = slot[:, None] == slot[None, :]
    far = dest != src
    xkey = jnp.where(far, jnp.abs(dest - src) * n + (n - 1 - item), -1)
    slot_key = jnp.max(jnp.where(same, xkey[None, :], -1), axis=1)
    xlead = far & (xkey == slot_key)
    ahead = xlead[None, :] & (owner[None, :] == owner[:, None]) & (xkey[None, :] > slot_key[:, None])
    xpos = jnp.sum(ahead.astype(jnp.int32), axis=1)
    d_dest = jnp.stack([dest, planes - 1 - dest])
    d_src = jnp.stack([src, planes - 1 - src])
    going = d_dest > d_src
    zkey = jnp.where(going, d_dest * n + (n - 1 - item)[None, :], -1)
    lead = going & (zkey == jnp.max(jnp.where(same[None], zkey[:, None, :], -1), axis=2))
    columns = jnp.arange(2, dtype=jnp.int32)[:, None]
    first = jnp.where(col[None, :] == columns, 0, xpos[None, :] + 1)[:, None, :]
    links, arrivals = [], []
    for p in range(planes - 1):
        on = (lead & (d_src <= p) & (d_dest > p))[None]
        starts = (d_src == p)[None]
        ready = first if p == 0 else jnp.where(starts, first, links[-1][1] + 1)
        key = (ready * planes + (planes - d_dest)[None]) * n + item
        before = on[:, :, None, :] & (key[:, :, None, :] <= key[:, :, :, None])
        rank = jnp.sum(before.astype(jnp.int32), axis=3)
        pos = jnp.max(
            jnp.where(before, ready[:, :, None, :] - rank[:, :, None, :], -n), axis=3
        ) + rank
        links.append((jnp.broadcast_to(on, pos.shape), pos))
        arrivals.append(
            jnp.max(jnp.where(on[:, :, None, :] & same, pos[:, :, None, :], -1), axis=3)
        )
    arrival = arrivals[0]
    for p in range(1, planes - 1):
        arrival = jnp.where((d_dest == p + 1)[None], arrivals[p], arrival)
    arrival = jnp.where(going[0], arrival[:, 0], arrival[:, 1])
    shape = (rows, req)
    partner_col = 1 - jnp.arange(rows, dtype=jnp.int32)[:, None] % 2
    partner = jnp.arange(rows, dtype=jnp.int32)[:, None] // 2 * 2 + partner_col
    sent = jnp.max(
        jnp.where(xlead[None, :] & (owner[None, :] == partner), xpos[None, :] + 1, 0), axis=1
    )[:, None]
    by_partner = jnp.where(side == 0, arrival[1], arrival[0]).reshape(shape)
    near = ~far.reshape(shape)
    from_partner = near & (col.reshape(shape) == partner_col)
    ready = jnp.where(near, sent, jnp.maximum(sent, by_partner + 1))
    ready = jnp.stack([ready, ready], axis=2).reshape(rows, 2 * req)
    valid = jnp.stack([from_partner | ~near, from_partner], axis=2).reshape(rows, 2 * req)
    key = ready * (2 * req) + jnp.arange(2 * req, dtype=jnp.int32)[None, :]
    before = valid[:, None, :] & (key[:, None, :] <= key[:, :, None])
    rank = jnp.sum(before.astype(jnp.int32), axis=2)
    dpos = jnp.max(jnp.where(before, ready[:, None, :] - rank[:, None, :], -n), axis=2) + rank
    need_x = jnp.max(jnp.maximum(jnp.where(valid, dpos + 1, 0), sent))
    need_z = functools.reduce(
        jnp.maximum, [jnp.max(jnp.where(on, pos + 1, 0)) for on, pos in links]
    )
    return dict(
        row=row, dest=dest, owner=owner, src=src, col=col, far=far, within=slot % held,
        going=going, lead=lead, d_src=d_src, xpos=xpos, links=links, arrival=arrival,
        dpos=dpos, valid=valid, need_x=need_x, need_z=need_z,
    )


def tables(slots, held, planes, member):
    rows, req = slots.shape
    plan = route(slots, held, planes)
    plane, column = member // 2, member % 2
    over_x, from_z = 2 * held, 2 * held + X_STEPS
    pool = 2 * plan["within"]
    arrived = jnp.where(column == 0, plan["arrival"][0], plan["arrival"][1])
    via_z = from_z + jnp.where(plan["going"][0], 0, Z_STEPS) + arrived

    def table(steps, *entries):
        step = jnp.arange(steps, dtype=jnp.int32)[:, None]
        best = jnp.full((steps,), -1, jnp.int32)
        for on, pos, source in entries:
            hit = on[None, :] & (pos[None, :] == step)
            best = jnp.maximum(best, jnp.max(jnp.where(hit, source[None, :], -1), axis=1))
        return best

    mine = plan["far"] & (plan["owner"] == member)
    other = member + 1 - 2 * column
    to_other = plan["row"] == other
    dpos = plan["dpos"].reshape(-1, 2)
    valid = plan["valid"].reshape(-1, 2)
    x_send = table(
        X_STEPS,
        (mine, plan["xpos"], pool + 1 - column),
        (to_other & valid[:, 0], dpos[:, 0], jnp.where(plan["far"], via_z, pool)),
        (to_other & valid[:, 1], dpos[:, 1], pool + 1),
    )
    z_send = []
    for d in range(2):
        at = plane if d == 0 else planes - 1 - plane
        source = jnp.where(plan["col"] == column, pool + column, over_x + plan["xpos"])
        on = jnp.zeros_like(plan["far"])
        pos = jnp.zeros_like(plan["xpos"])
        for p in range(planes - 1):
            link_on = plan["links"][p][0][:, d]
            link_pos = plan["links"][p][1][:, d]
            here = at == p
            on = jnp.where(here, jnp.where(column == 0, link_on[0], link_on[1]), on)
            pos = jnp.where(here, jnp.where(column == 0, link_pos[0], link_pos[1]), pos)
            if p:
                last = plan["links"][p - 1][1][:, d]
                last = jnp.where(column == 0, last[0], last[1])
                passing = here & (plan["d_src"][d] < p)
                source = jnp.where(passing, from_z + d * Z_STEPS + last, source)
        z_send.append(table(Z_STEPS, (on, pos, source)))
    halves = []
    for h in range(2):
        near = jnp.where(plan["col"] == column, pool + h, over_x + dpos[:, h])
        far = jnp.where(column == h, via_z, over_x + dpos[:, 0])
        halves.append(jnp.where(plan["far"], far, near))
    place = jnp.stack(halves, axis=1).reshape(rows, 2 * req)
    place = lax.dynamic_index_in_dim(place, member, 0, keepdims=False)
    fits = (plan["need_x"] <= X_STEPS) & (plan["need_z"] <= Z_STEPS)
    x_send, up_send, down_send = [jnp.where(fits, t, -1) for t in (x_send, *z_send)]
    return x_send, up_send, down_send, place, fits


def copies(code, base_code, down, up, arrays, out, rows, sem):
    width = down.shape[2]
    lo, size = rows
    held = down.shape[0]
    slot, half = code // 2, code % 2
    start = pl.multiple_of(half * (down.shape[1] // 2) + lo, size)
    slot = jnp.clip(slot, 0, held - 1)
    pool = [
        pltpu.make_async_copy(
            down.at[slot, pl.ds(start, size), :], out.at[:, pl.ds(0, width)], sem
        ),
        pltpu.make_async_copy(
            up.at[slot, pl.ds(start, size), :], out.at[:, pl.ds(width, up.shape[2])], sem
        ),
    ]
    pairs = [((code >= 0) & (code < 2 * held), pool)]
    for number, array in arrays:
        pairs.append((code == number, [pltpu.make_async_copy(array, out, sem)]))
    return pairs


def send_kernel(step, sub, size, codes, down, up, *refs):
    n = 3 * step
    x_in, up_in, down_in = refs[:step], refs[step : 2 * step], refs[2 * step : n]
    outs = refs[n:-1]
    sem = refs[-1]
    base = 2 * down.shape[0]
    from_x = [(base + s, r) for s, r in enumerate(x_in)]
    from_below = [(base + X_STEPS + s, r) for s, r in enumerate(up_in)]
    from_above = [(base + X_STEPS + Z_STEPS + s, r) for s, r in enumerate(down_in)]
    sources = [from_below + from_above, from_x + from_below, from_x + from_above]
    rows = (sub * size, size)
    for i, out in enumerate(outs):
        for on, list_of in copies(codes[i], base, down, up, sources[i], out, rows, sem.at[i]):

            @pl.when(on)
            def _(list_of=list_of):
                for c in list_of:
                    c.start()

    for i, out in enumerate(outs):

        @pl.when(codes[i] >= 0)
        def _(i=i, out=out):
            pltpu.make_async_copy(out, out, sem.at[i]).wait()


ANY = pl.BlockSpec(memory_space=pl.ANY)


def pick_step(step, sub, size, codes, down, up, got):
    width = down.shape[2] + up.shape[2]
    outs = 3 if step < Z_STEPS else 1
    return pl.pallas_call(
        functools.partial(send_kernel, step, sub, size),
        grid_spec=pltpu.PrefetchScalarGridSpec(
            num_scalar_prefetch=1,
            grid=(),
            in_specs=[ANY] * (2 + 3 * step),
            out_specs=[ANY] * outs,
            scratch_shapes=[pltpu.SemaphoreType.DMA((3,))],
        ),
        out_shape=[jax.ShapeDtypeStruct((size, width), down.dtype)] * outs,
        name="pick_step",
    )(codes, down, up, *got[0], *got[1], *got[2])


def collect_kernel(req, size, n_x, n_z, codes, down, up, *refs):
    n = n_x + 2 * n_z
    a_in, b_in, out, sem = refs[:n], refs[n : 2 * n], refs[2 * n], refs[2 * n + 1]
    base = 2 * down.shape[0]
    half_rows = down.shape[1] // 2
    for r in range(req):
        for h in range(2):
            code = codes[2 * r + h]
            todo = []
            for sub, arrays in enumerate((a_in, b_in)):
                target = out.at[r, pl.ds(h * half_rows + sub * size, size), :]
                sources = [(base + k, a) for k, a in enumerate(arrays)]
                todo.append(
                    copies(code, base, down, up, sources, target, (sub * size, size), sem.at[r])
                )
            for (on, first), (_, second) in zip(*todo):

                @pl.when(on)
                def _(first=first, second=second):
                    for c in first + second:
                        c.start()

    for r in range(req):
        pltpu.make_async_copy(out.at[r], out.at[r], sem.at[r]).wait()


def collect(size, codes, down, up, got_a, got_b):
    req = codes.shape[0] // 2
    rank = down.shape[1]
    width = down.shape[2] + up.shape[2]
    flat = [a for got in (got_a, got_b) for stream in got for a in stream]
    return pl.pallas_call(
        functools.partial(collect_kernel, req, size, len(got_a[0]), len(got_a[1])),
        grid_spec=pltpu.PrefetchScalarGridSpec(
            num_scalar_prefetch=1,
            grid=(),
            in_specs=[ANY] * (2 + len(flat)),
            out_specs=ANY,
            scratch_shapes=[pltpu.SemaphoreType.DMA((req,))],
        ),
        out_shape=jax.ShapeDtypeStruct((req, rank, width), down.dtype),
        name="collect",
    )(codes, down, up, *flat)


def dense(slots, held, member, down_pool, up_pool):
    owners = slots // held
    index = jnp.sum(jnp.where(owners == member, slots % held, 0), axis=1).astype(jnp.int32)
    my_owners = lax.dynamic_index_in_dim(owners, member, 0, keepdims=False)
    send = pick(index, down_pool, up_pool)
    blocks = lax.all_to_all(send, "dp", split_axis=0, concat_axis=0, tiled=True)
    return jnp.take(blocks, my_owners, axis=0, mode="clip")


def routed(n_groups, slots, held, planes, member, down_pool, up_pool, work):
    rank = down_pool.shape[1]
    size = rank // 4
    x_send, up_send, down_send, place, fits = tables(slots, held, planes, member)
    misfit = 1 - fits.astype(jnp.int32).reshape(1)
    for other in gathered(misfit, "groups", n_groups)[1:]:
        misfit = jnp.maximum(misfit, other)
    n = 2 * planes
    pairs = (
        [(i, i ^ 1) for i in range(n)],
        [(i, i + 2) for i in range(n - 2)],
        [(i + 2, i) for i in range(n - 2)],
    )
    got = [([], [], []), ([], [], [])]
    for step in range(X_STEPS):
        codes = [x_send[step]]
        if step < Z_STEPS:
            codes += [up_send[step], down_send[step]]
        codes = jnp.stack(codes)
        for sub in range(2):
            known = [s[:step] for s in got[sub]]
            sends = pick_step(step, sub, size, codes, down_pool, up_pool, known)
            for stream, send, pair in zip(got[sub], sends, pairs):
                stream.append(lax.ppermute(send, "dp", pair))
    flat = [a for g in got for s in g for a in s]

    def fast():
        return collect(size, place, down_pool, up_pool, got[0], got[1])

    def slow():
        return dense(slots, held, member, down_pool, up_pool)

    return lax.cond(misfit[0] == 0, fast, slow)


def shards(sizes, tokens, key_weight, down_pool, up_pool, adapter_ids, lengths, owner_map):
    n_groups, n_dp, n_tensor = sizes
    member = lax.axis_index("dp")
    held, rank, width = down_pool.shape
    columns = up_pool.shape[2]
    slots = owner_map[adapter_ids]
    ends = jnp.cumsum(lengths[0]).astype(jnp.int32)

    me = lax.axis_index("tensor")
    base_parts = []
    for step in range(n_tensor):
        to = lax.rem(me + step, n_tensor)
        weight = lax.dynamic_slice_in_dim(key_weight, to * columns, columns, 1)
        part = jnp.dot(tokens, weight, preferred_element_type=jnp.float32)
        if step:
            part = lax.ppermute(
                part, "tensor", [(i, (i + step) % n_tensor) for i in range(n_tensor)]
            )
        base_parts.append(part)

    if n_dp == 8 and rank % 64 == 0:
        blocks = routed(n_groups, slots, held, n_dp // 2, member, down_pool, up_pool, None)
    else:
        blocks = dense(slots, held, member, down_pool, up_pool)
    place = jnp.arange(slots.shape[1], dtype=jnp.int32)
    code = codes(place, ends, tokens, blocks, width)
    code_parts = gathered(code, "tensor", n_tensor)
    return finish(place, ends, code_parts, base_parts, blocks, width)


def solution(mesh):
    placed = (
        P(("groups", "dp"), "tensor"),
        P("tensor", None),
        P("dp", None, "tensor"),
        P("dp", None, "tensor"),
        P("groups", None),
        P(("groups", "dp"), None),
        P("groups"),
    )
    sizes = tuple(mesh.shape[name] for name in ("groups", "dp", "tensor"))
    return jax.shard_map(
        functools.partial(shards, sizes),
        mesh=mesh,
        in_specs=placed,
        out_specs=P(("groups", "dp"), "tensor"),
        check_vma=False,
    )
```

```python
import functools

import jax
import jax.numpy as jnp
from jax import lax
from jax.experimental import pallas as pl
from jax.experimental.pallas import tpu as pltpu
from jax.sharding import PartitionSpec as P

ADAPTER_SCALE = 2.0
MIB = 1 << 20
ANY = pl.BlockSpec(memory_space=pl.ANY)
VMEM = pl.BlockSpec(memory_space=pltpu.VMEM)


def in_hbm(x):
    return pltpu.with_memory_space_constraint(x, pltpu.HBM)


def pick_kernel(rows, req, ids, owner_map, down, up, out, wanted, sem):
    held, _, width = down.shape
    first = lax.axis_index("dp") * held

    def fetch(j, carry):
        wanted[j] = 0
        for r in range(req):
            slot = owner_map[ids[j * req + r]] - first

            @pl.when((slot >= 0) & (slot < held))
            def _(slot=slot):
                wanted[j] = 1
                to = out.at[j]
                pltpu.make_async_copy(down.at[slot], to.at[:, pl.ds(0, width)], sem.at[j]).start()
                pltpu.make_async_copy(
                    up.at[slot], to.at[:, pl.ds(width, up.shape[2])], sem.at[j]
                ).start()

        return carry

    def drain(j, carry):
        @pl.when(wanted[j] == 1)
        def _():
            pltpu.make_async_copy(out.at[j], out.at[j], sem.at[j]).wait()

        return carry

    for body in (fetch, drain):
        lax.fori_loop(0, rows, body, 0)


def pick(adapter_ids, owner_map, down_pool, up_pool):
    rows, req = adapter_ids.shape
    rank, width = down_pool.shape[1:]
    wide = width + up_pool.shape[2]
    return pl.pallas_call(
        functools.partial(pick_kernel, rows, req),
        grid_spec=pltpu.PrefetchScalarGridSpec(
            num_scalar_prefetch=2,
            grid=(),
            in_specs=[ANY, ANY],
            out_specs=ANY,
            scratch_shapes=[
                pltpu.SMEM((rows,), jnp.int32),
                pltpu.SemaphoreType.DMA((rows,)),
            ],
        ),
        out_shape=pltpu.VMEM((rows, rank, wide), down_pool.dtype),
        compiler_params=pltpu.CompilerParams(vmem_limit_bytes=24 * MIB),
        name="pick",
    )(adapter_ids.reshape(-1), owner_map, in_hbm(down_pool), in_hbm(up_pool))


def stage_kernel(source, out, sem):
    copy = pltpu.make_async_copy(source, out, sem)
    copy.start()
    copy.wait()


def stage(x):
    return pl.pallas_call(
        stage_kernel,
        in_specs=[ANY],
        out_specs=VMEM,
        out_shape=pltpu.VMEM(x.shape, x.dtype),
        scratch_shapes=[pltpu.SemaphoreType.DMA],
        compiler_params=pltpu.CompilerParams(vmem_limit_bytes=24 * MIB),
        cost_estimate=pl.CostEstimate(flops=0, bytes_accessed=2 * x.size * x.dtype.itemsize, transcendentals=0),
        name="stage",
    )(in_hbm(x))


def request_of_rows(ends, count, first, rows):
    at = first + lax.broadcasted_iota(jnp.int32, (rows, 1), 0)
    which = jnp.zeros((rows, 1), jnp.int32)
    for r in range(count - 1):
        which += (at >= ends[r]).astype(jnp.int32)
    return which


def code_kernel(count, tile, place, ends, tokens, blocks, out, down, sem):
    rank, width = blocks.shape[1], tokens.shape[1]
    for r in range(count):
        pltpu.make_async_copy(
            blocks.at[place[r], :, pl.ds(0, width)], down.at[pl.ds(r * rank, rank), :], sem
        ).start()
    pltpu.make_async_copy(down, down, sem).wait()
    for i in range(out.shape[0] // tile):
        parts = []
        for side in range(2):
            first = side * out.shape[0] + i * tile
            full = lax.dot_general(
                tokens[first : first + tile, :],
                down[...],
                (((1,), (1,)), ((), ())),
                preferred_element_type=jnp.float32,
            )
            which = request_of_rows(ends, count, first, tile)
            code = jnp.zeros((tile, rank), jnp.float32)
            for r in range(count):
                code = jnp.where(which == r, full[:, r * rank : (r + 1) * rank], code)
            parts.append(code)
        out[i * tile : (i + 1) * tile, :] = jnp.concatenate(parts, axis=1)


def codes(place, ends, tokens, blocks):
    many, features = tokens.shape
    count = place.shape[0]
    rank = blocks.shape[1]
    return pl.pallas_call(
        functools.partial(code_kernel, count, min(256, many // 2)),
        grid_spec=pltpu.PrefetchScalarGridSpec(
            num_scalar_prefetch=2,
            grid=(),
            in_specs=[VMEM, ANY],
            out_specs=VMEM,
            scratch_shapes=[
                pltpu.VMEM((count * rank, features), blocks.dtype),
                pltpu.SemaphoreType.DMA,
            ],
        ),
        out_shape=jax.ShapeDtypeStruct((many // 2, 2 * rank), jnp.float32),
        compiler_params=pltpu.CompilerParams(vmem_limit_bytes=32 * MIB),
        cost_estimate=pl.CostEstimate(
            flops=2 * many * features * count * rank,
            bytes_accessed=count * rank * features * 2,
            transcendentals=0,
        ),
        name="codes",
    )(place, ends, pltpu.with_memory_space_constraint(tokens, pltpu.VMEM), blocks)


def finish_kernel(count, parts, place, ends, *refs):
    code_parts, base = refs[:parts], refs[parts]
    blocks = refs[parts + 1 : parts + 1 + count]
    out, up = refs[parts + 1 + count :]
    rank = blocks[0].shape[1]
    step = pl.program_id(0)

    @pl.when(step == 0)
    def _():
        for r in range(count):
            up[r * rank : (r + 1) * rank, :] = blocks[r][0]

    rows = out.shape[0]
    code = code_parts[0][...]
    for p in range(1, parts):
        code = code + code_parts[p][...]
    code = jnp.where(step < pl.num_programs(0) // 2, code[:, :rank], code[:, rank:])
    which = request_of_rows(ends, count, step * rows, rows)
    zero = jnp.zeros_like(code)
    wide = jnp.concatenate([jnp.where(which == r, code, zero) for r in range(count)], axis=1)
    delta = None
    for _ in range(3):
        part = wide.astype(jnp.bfloat16)
        wide = wide - part.astype(jnp.float32)
        term = jnp.dot(part, up[...], preferred_element_type=jnp.float32)
        delta = term if delta is None else delta + term
    out[...] = (base[...] + ADAPTER_SCALE * delta).astype(out.dtype)


def finish(place, ends, code_parts, base, blocks, width):
    many, columns = base.shape
    rank = blocks.shape[1]
    count = place.shape[0]
    parts = len(code_parts)
    tile = min(256, many // 2)
    half = many // tile // 2
    return pl.pallas_call(
        functools.partial(finish_kernel, count, parts),
        grid_spec=pltpu.PrefetchScalarGridSpec(
            num_scalar_prefetch=2,
            grid=(many // tile,),
            in_specs=[pl.BlockSpec((tile, 2 * rank), lambda i, place, ends: (i % half, 0))] * parts
            + [pl.BlockSpec((tile, columns), lambda i, place, ends: (i, 0))]
            + [
                pl.BlockSpec(
                    (1, rank, columns),
                    lambda i, place, ends, r=r: (place[r], 0, width // columns),
                )
                for r in range(count)
            ],
            out_specs=pl.BlockSpec((tile, columns), lambda i, place, ends: (i, 0)),
            scratch_shapes=[pltpu.VMEM((count * rank, columns), blocks.dtype)],
        ),
        out_shape=jax.ShapeDtypeStruct((many, columns), jnp.bfloat16),
        compiler_params=pltpu.CompilerParams(vmem_limit_bytes=24 * MIB),
        name="finish",
    )(place, ends, *code_parts, base, *([blocks] * count))


def gathered(part, axis, size):
    held = [part]
    for step in range(1, size):
        held.append(lax.ppermute(part, axis, [(i, (i + step) % size) for i in range(size)]))
    return held


def shards(sizes, tokens, key_weight, down_pool, up_pool, adapter_ids, lengths, owner_map):
    n_groups, n_dp, n_tensor = sizes
    held, _, width = down_pool.shape
    columns = up_pool.shape[2]

    send = pick(adapter_ids, owner_map, down_pool, up_pool)
    send, late_tokens = lax.optimization_barrier((send, tokens))
    blocks = lax.all_to_all(send, "dp", split_axis=0, concat_axis=0, tiled=True)

    me = lax.axis_index("tensor")
    base = None
    for step in reversed(range(n_tensor)):
        to = lax.rem(me + step, n_tensor)
        weight = lax.dynamic_slice_in_dim(key_weight, to * columns, columns, 1)
        part = jnp.dot(late_tokens, weight, preferred_element_type=jnp.float32)
        if step:
            part = lax.ppermute(
                part, "tensor", [(i, (i + step) % n_tensor) for i in range(n_tensor)]
            )
        base = part if base is None else base + part
    at_hand = stage(late_tokens)
    my_ids = lax.dynamic_index_in_dim(adapter_ids, lax.axis_index("dp"), 0, keepdims=False)
    place = owner_map[my_ids] // held
    ends = jnp.cumsum(lengths[0]).astype(jnp.int32)

    blocks, base, at_hand, place, ends = lax.optimization_barrier(
        (blocks, base, at_hand, place, ends)
    )
    code = codes(place, ends, at_hand, blocks)
    code_parts = gathered(code, "tensor", n_tensor)
    return finish(place, ends, code_parts, base, blocks, width)


def solution(mesh):
    placed = (
        P(("groups", "dp"), "tensor"),
        P("tensor", None),
        P("dp", None, "tensor"),
        P("dp", None, "tensor"),
        P("groups", None),
        P(("groups", "dp"), None),
        P("groups"),
    )
    sizes = tuple(mesh.shape[name] for name in ("groups", "dp", "tensor"))
    return jax.shard_map(
        functools.partial(shards, sizes),
        mesh=mesh,
        in_specs=placed,
        out_specs=P(("groups", "dp"), "tensor"),
        check_vma=False,
    )
```

```python
import functools

import jax
import jax.numpy as jnp
from jax import lax
from jax.experimental import pallas as pl
from jax.experimental.pallas import tpu as pltpu
from jax.sharding import PartitionSpec as P

ADAPTER_SCALE = 2.0
MIB = 1 << 20
ANY = pl.BlockSpec(memory_space=pl.ANY)
VMEM = pl.BlockSpec(memory_space=pltpu.VMEM)


def in_hbm(x):
    return pltpu.with_memory_space_constraint(x, pltpu.HBM)


def pick_kernel(swaps, req, ids, owner_map, down, up, *refs):
    outs, (hold, wanted, in_sem, out_sem) = refs[: len(swaps)], refs[len(swaps) :]
    held, _, width = down.shape
    member = lax.axis_index("dp")
    for i, swap in enumerate(swaps):
        wanted[i] = 0
        for r in range(req):
            slot = owner_map[ids[r, member ^ swap]] - member * held

            @pl.when((slot >= 0) & (slot < held))
            def _(i=i, slot=slot):
                wanted[i] = 1
                to = hold.at[i]
                pltpu.make_async_copy(
                    down.at[slot], to.at[:, pl.ds(0, width)], in_sem.at[i]
                ).start()
                pltpu.make_async_copy(
                    up.at[slot], to.at[:, pl.ds(width, up.shape[2])], in_sem.at[i]
                ).start()

    for i, out in enumerate(outs):

        @pl.when(wanted[i] == 1)
        def _(i=i, out=out):
            pltpu.make_async_copy(hold.at[i], hold.at[i], in_sem.at[i]).wait()
            pltpu.make_async_copy(hold.at[i], out, out_sem.at[i]).start()

    for i, out in enumerate(outs):

        @pl.when(wanted[i] == 1)
        def _(i=i, out=out):
            pltpu.make_async_copy(hold.at[i], out, out_sem.at[i]).wait()


def pick(swaps, adapter_ids, owner_map, down_pool, up_pool):
    rows, req = adapter_ids.shape
    rank, width = down_pool.shape[1:]
    block = (rank, width + up_pool.shape[2])
    many = len(swaps)
    return pl.pallas_call(
        functools.partial(pick_kernel, swaps, req),
        grid_spec=pltpu.PrefetchScalarGridSpec(
            num_scalar_prefetch=2,
            grid=(),
            in_specs=[ANY, ANY],
            out_specs=[ANY] * many,
            scratch_shapes=[
                pltpu.VMEM((many, *block), down_pool.dtype),
                pltpu.SMEM((many,), jnp.int32),
                pltpu.SemaphoreType.DMA((many,)),
                pltpu.SemaphoreType.DMA((many,)),
            ],
        ),
        out_shape=[jax.ShapeDtypeStruct(block, down_pool.dtype)] * many,
        compiler_params=pltpu.CompilerParams(vmem_limit_bytes=48 * MIB),
        name="pick",
    )(adapter_ids.T, owner_map, in_hbm(down_pool), in_hbm(up_pool))


def dense_kernel(index, down, up, out):
    width = down.shape[2]
    out[:, :, :width] = down[...]
    out[:, :, width:] = up[...]


def dense(adapter_ids, owner_map, down_pool, up_pool):
    held, rank, width = down_pool.shape
    columns = up_pool.shape[2]
    slots = owner_map[adapter_ids] - lax.axis_index("dp") * held
    here = (slots >= 0) & (slots < held)
    index = jnp.sum(jnp.where(here, slots, 0), axis=1).astype(jnp.int32)
    many = index.shape[0]
    send = pl.pallas_call(
        dense_kernel,
        grid_spec=pltpu.PrefetchScalarGridSpec(
            num_scalar_prefetch=1,
            grid=(many,),
            in_specs=[
                pl.BlockSpec((1, rank, width), lambda j, index: (index[j], 0, 0)),
                pl.BlockSpec((1, rank, columns), lambda j, index: (index[j], 0, 0)),
            ],
            out_specs=pl.BlockSpec((1, rank, width + columns), lambda j, index: (j, 0, 0)),
        ),
        out_shape=jax.ShapeDtypeStruct((many, rank, width + columns), down_pool.dtype),
        name="pick_all",
    )(index, down_pool, up_pool)
    return lax.all_to_all(send, "dp", split_axis=0, concat_axis=0, tiled=True)


def request_of_rows(ends, count, first, rows):
    at = first + lax.broadcasted_iota(jnp.int32, (rows, 1), 0)
    which = jnp.zeros((rows, 1), jnp.int32)
    for r in range(count - 1):
        which += (at >= ends[r]).astype(jnp.int32)
    return which


def code_kernel(count, chunks, place, ends, tokens, *refs):
    n = len(refs) - 7
    blocks, (out, up, down, rows, total, block_sem, row_sem) = refs[:n], refs[n:]
    rank, features = out.shape[1] // 2, tokens.shape[1]
    columns = up.shape[1]
    step = features // chunks

    def parts(block):
        cuts = [(k * step, step) for k in range(chunks)]
        return [block.at[:, pl.ds(*cut)] for cut in cuts] + [block.at[:, pl.ds(features, columns)]]

    def targets(r):
        mine = pl.ds(r * rank, rank)
        return [down.at[k, mine, :] for k in range(chunks)] + [up.at[mine, :]]

    def load(r, block):
        for k, (source, target) in enumerate(zip(parts(block), targets(r))):
            pltpu.make_async_copy(source, target, block_sem.at[k]).start()

    for r in range(count):
        if n == 1:
            load(r, blocks[0].at[place[r]])
        else:
            for s, block in enumerate(blocks):

                @pl.when(place[r] == s)
                def _(r=r, block=block):
                    load(r, block)

    for k in range(chunks):
        pltpu.make_async_copy(
            tokens.at[:, pl.ds(k * step, step)], rows.at[k], row_sem.at[k]
        ).start()
    for k in range(chunks):
        pltpu.make_async_copy(down.at[k], down.at[k], block_sem.at[k]).wait()
        pltpu.make_async_copy(rows.at[k], rows.at[k], row_sem.at[k]).wait()
        part = lax.dot_general(
            rows[k], down[k], (((1,), (1,)), ((), ())), preferred_element_type=jnp.float32
        )
        if k == 0:
            total[...] = part
        elif k < chunks - 1:
            total[...] += part
        else:
            full = total[...] + part
    pltpu.make_async_copy(up, up, block_sem.at[chunks]).wait()
    which = request_of_rows(ends, count, 0, full.shape[0])
    code = full[:, :rank]
    for r in range(1, count):
        code = jnp.where(which == r, full[:, r * rank : (r + 1) * rank], code)
    half = full.shape[0] // 2
    out[...] = jnp.concatenate([code[:half], code[half:]], axis=1)


def codes(place, ends, tokens, blocks, columns):
    many, features = tokens.shape
    count = place.shape[0]
    rank = blocks[0].shape[-2]
    chunks = 4
    return pl.pallas_call(
        functools.partial(code_kernel, count, chunks),
        grid_spec=pltpu.PrefetchScalarGridSpec(
            num_scalar_prefetch=2,
            grid=(),
            in_specs=[ANY] * (1 + len(blocks)),
            out_specs=[VMEM, VMEM],
            scratch_shapes=[
                pltpu.VMEM((chunks, count * rank, features // chunks), tokens.dtype),
                pltpu.VMEM((chunks, many, features // chunks), tokens.dtype),
                pltpu.VMEM((many, count * rank), jnp.float32),
                pltpu.SemaphoreType.DMA((chunks + 1,)),
                pltpu.SemaphoreType.DMA((chunks,)),
            ],
        ),
        out_shape=[
            jax.ShapeDtypeStruct((many // 2, 2 * rank), jnp.float32),
            jax.ShapeDtypeStruct((count * rank, columns), tokens.dtype),
        ],
        compiler_params=pltpu.CompilerParams(vmem_limit_bytes=48 * MIB),
        name="codes",
    )(place, ends, in_hbm(tokens), *blocks)


def finish_kernel(count, parts, tile, ends, *refs):
    code_parts, (base, up, out, hold, sem) = refs[:parts], refs[parts:]
    rank = up.shape[0] // count
    code = code_parts[0][...]
    for p in range(1, parts):
        code = code + code_parts[p][...]
    half = code.shape[0]
    copies = []
    for i in range(out.shape[0] // tile):
        first = i * tile
        side, at = first // half, first % half
        mine = code[at : at + tile, side * rank : (side + 1) * rank]
        which = request_of_rows(ends, count, first, tile)
        zero = jnp.zeros_like(mine)
        wide = jnp.concatenate([jnp.where(which == r, mine, zero) for r in range(count)], axis=1)
        delta = None
        for _ in range(3):
            part = wide.astype(jnp.bfloat16)
            wide = wide - part.astype(jnp.float32)
            term = jnp.dot(part, up[...], preferred_element_type=jnp.float32)
            delta = term if delta is None else delta + term
        rows = pl.ds(first, tile)
        hold[rows, :] = (base[rows, :] + ADAPTER_SCALE * delta).astype(hold.dtype)
        copies.append(pltpu.make_async_copy(hold.at[rows, :], out.at[rows, :], sem.at[i]))
        copies[-1].start()
    for copy in copies:
        copy.wait()


def finish(ends, code_parts, base, up):
    many, columns = base.shape
    count = ends.shape[0]
    parts = len(code_parts)
    tile = min(256, many // 2)
    return pl.pallas_call(
        functools.partial(finish_kernel, count, parts, tile),
        grid_spec=pltpu.PrefetchScalarGridSpec(
            num_scalar_prefetch=1,
            grid=(),
            in_specs=[VMEM] * (parts + 2),
            out_specs=ANY,
            scratch_shapes=[
                pltpu.VMEM((many, columns), jnp.bfloat16),
                pltpu.SemaphoreType.DMA((many // tile,)),
            ],
        ),
        out_shape=jax.ShapeDtypeStruct((many, columns), jnp.bfloat16),
        compiler_params=pltpu.CompilerParams(vmem_limit_bytes=24 * MIB),
        name="finish",
    )(ends, *code_parts, pltpu.with_memory_space_constraint(base, pltpu.VMEM), up)


def gathered(part, axis, size):
    held = [part]
    for step in range(1, size):
        held.append(lax.ppermute(part, axis, [(i, (i + step) % size) for i in range(size)]))
    return held


def shards(sizes, tokens, key_weight, down_pool, up_pool, adapter_ids, lengths, owner_map):
    n_groups, n_dp, n_tensor = sizes
    held, _, width = down_pool.shape
    columns = up_pool.shape[2]

    member = lax.axis_index("dp")
    if n_dp == 8:
        swaps = [4, 5, 6, 7, 2, 3, 1]
        sends = pick(swaps, adapter_ids, owner_map, down_pool, up_pool)
        *sends, late_tokens = lax.optimization_barrier((*sends, tokens))
        got = {}
        for swap, send in zip(swaps, sends):
            got[swap] = lax.ppermute(send, "dp", [(i, i ^ swap) for i in range(n_dp)])
        blocks = [got[swap] for swap in range(1, n_dp)]
    else:
        late_tokens = tokens
        blocks = [dense(adapter_ids, owner_map, down_pool, up_pool)]

    me = lax.axis_index("tensor")
    base = None
    for step in reversed(range(n_tensor)):
        to = lax.rem(me + step, n_tensor)
        weight = lax.dynamic_slice_in_dim(key_weight, to * columns, columns, 1)
        part = jnp.dot(late_tokens, weight, preferred_element_type=jnp.float32)
        if step:
            part = lax.ppermute(
                part, "tensor", [(i, (i + step) % n_tensor) for i in range(n_tensor)]
            )
        base = part if base is None else base + part
    my_ids = lax.dynamic_index_in_dim(adapter_ids, member, 0, keepdims=False)
    my_slots = owner_map[my_ids]
    place = my_slots // held
    ends = jnp.cumsum(lengths[0]).astype(jnp.int32)
    if n_dp == 8:
        place = place ^ member
        own = jnp.clip(jnp.max(jnp.where(place == 0, my_slots % held, 0)), 0, held - 1)
        own_down = lax.dynamic_index_in_dim(down_pool, own, 0, keepdims=False)
        own_up = lax.dynamic_index_in_dim(up_pool, own, 0, keepdims=False)
        blocks = [jnp.concatenate([own_down, own_up], axis=1)] + blocks

    *blocks, base, place, ends = lax.optimization_barrier((*blocks, base, place, ends))
    code, up = codes(place, ends, tokens, blocks, columns)
    code_parts = gathered(code, "tensor", n_tensor)
    return finish(ends, code_parts, base, up)


def solution(mesh):
    placed = (
        P(("groups", "dp"), "tensor"),
        P("tensor", None),
        P("dp", None, "tensor"),
        P("dp", None, "tensor"),
        P("groups", None),
        P(("groups", "dp"), None),
        P("groups"),
    )
    sizes = tuple(mesh.shape[name] for name in ("groups", "dp", "tensor"))
    return jax.shard_map(
        functools.partial(shards, sizes),
        mesh=mesh,
        in_specs=placed,
        out_specs=P(("groups", "dp"), "tensor"),
        check_vma=False,
    )
```

```python
import functools

import jax
import jax.numpy as jnp
from jax import lax
from jax.experimental import pallas as pl
from jax.experimental.pallas import tpu as pltpu
from jax.sharding import PartitionSpec as P

ADAPTER_SCALE = 2.0
MIB = 1 << 20
ANY = pl.BlockSpec(memory_space=pl.ANY)
VMEM = pl.BlockSpec(memory_space=pltpu.VMEM)


def in_hbm(x):
    return pltpu.with_memory_space_constraint(x, pltpu.HBM)


def pick_kernel(pieces, req, ids, owner_map, down, up, *refs):
    n = len(pieces)
    outs, holds = refs[:n], refs[n : 2 * n]
    wanted, in_sem, out_sem = refs[2 * n :]
    held = down.shape[0]
    member = lax.axis_index("dp")
    for i, (swap, lo, hi, with_up) in enumerate(pieces):
        wanted[i] = 0
        for r in range(req):
            slot = owner_map[ids[r, member ^ swap]] - member * held

            @pl.when((slot >= 0) & (slot < held))
            def _(i=i, slot=slot, lo=lo, hi=hi, with_up=with_up):
                wanted[i] = 1
                pltpu.make_async_copy(
                    down.at[slot, :, pl.ds(lo, hi - lo)],
                    holds[i].at[:, pl.ds(0, hi - lo)],
                    in_sem.at[i],
                ).start()
                if with_up:
                    pltpu.make_async_copy(
                        up.at[slot], holds[i].at[:, pl.ds(hi - lo, up.shape[2])], in_sem.at[i]
                    ).start()

    for i in range(n):

        @pl.when(wanted[i] == 1)
        def _(i=i):
            pltpu.make_async_copy(holds[i], holds[i], in_sem.at[i]).wait()
            pltpu.make_async_copy(holds[i], outs[i], out_sem.at[i]).start()

    for i in range(n):

        @pl.when(wanted[i] == 1)
        def _(i=i):
            pltpu.make_async_copy(holds[i], outs[i], out_sem.at[i]).wait()


def pick(pieces, adapter_ids, owner_map, down_pool, up_pool):
    rows, req = adapter_ids.shape
    rank = down_pool.shape[1]
    shapes = [(rank, hi - lo + up_pool.shape[2] * with_up) for _, lo, hi, with_up in pieces]
    many = len(pieces)
    return pl.pallas_call(
        functools.partial(pick_kernel, pieces, req),
        grid_spec=pltpu.PrefetchScalarGridSpec(
            num_scalar_prefetch=2,
            grid=(),
            in_specs=[ANY, ANY],
            out_specs=[ANY] * many,
            scratch_shapes=[pltpu.VMEM(shape, down_pool.dtype) for shape in shapes]
            + [
                pltpu.SMEM((many,), jnp.int32),
                pltpu.SemaphoreType.DMA((many,)),
                pltpu.SemaphoreType.DMA((many,)),
            ],
        ),
        out_shape=[jax.ShapeDtypeStruct(shape, down_pool.dtype) for shape in shapes],
        compiler_params=pltpu.CompilerParams(vmem_limit_bytes=48 * MIB),
        name="pick",
    )(adapter_ids.T, owner_map, in_hbm(down_pool), in_hbm(up_pool))


def dense_kernel(index, down, up, out):
    width = down.shape[2]
    out[:, :, :width] = down[...]
    out[:, :, width:] = up[...]


def dense(adapter_ids, owner_map, down_pool, up_pool):
    held, rank, width = down_pool.shape
    columns = up_pool.shape[2]
    slots = owner_map[adapter_ids] - lax.axis_index("dp") * held
    here = (slots >= 0) & (slots < held)
    index = jnp.sum(jnp.where(here, slots, 0), axis=1).astype(jnp.int32)
    many = index.shape[0]
    send = pl.pallas_call(
        dense_kernel,
        grid_spec=pltpu.PrefetchScalarGridSpec(
            num_scalar_prefetch=1,
            grid=(many,),
            in_specs=[
                pl.BlockSpec((1, rank, width), lambda j, index: (index[j], 0, 0)),
                pl.BlockSpec((1, rank, columns), lambda j, index: (index[j], 0, 0)),
            ],
            out_specs=pl.BlockSpec((1, rank, width + columns), lambda j, index: (j, 0, 0)),
        ),
        out_shape=jax.ShapeDtypeStruct((many, rank, width + columns), down_pool.dtype),
        name="pick_all",
    )(index, down_pool, up_pool)
    return lax.all_to_all(send, "dp", split_axis=0, concat_axis=0, tiled=True)


def request_of_rows(ends, count, first, rows):
    at = first + lax.broadcasted_iota(jnp.int32, (rows, 1), 0)
    which = jnp.zeros((rows, 1), jnp.int32)
    for r in range(count - 1):
        which += (at >= ends[r]).astype(jnp.int32)
    return which


def code_kernel(count, cut, step, kinds, has_up, has_before, index, ends, tokens, *refs):
    lo, hi = cut
    chunks = (hi - lo) // step
    n = sum(2 if kind == "pool" else 1 for kind, _, _ in kinds)
    arrays, refs = list(refs[:n]), list(refs[n:])
    before = refs.pop(0) if has_before else None
    out = refs.pop(0)
    up = refs.pop(0) if has_up else None
    down, rows, total, block_sem, row_sem = refs
    rank = out.shape[1] // 2

    def load(r, down_block, first, up_block):
        mine = pl.ds(r * rank, rank)
        for k in range(chunks):
            pltpu.make_async_copy(
                down_block.at[:, pl.ds(first + k * step, step)],
                down.at[k, mine, :],
                block_sem.at[k],
            ).start()
        if has_up:
            pltpu.make_async_copy(up_block, up.at[mine, :], block_sem.at[chunks]).start()

    def load_from(r, kind, first, up_first, held):
        block = held[0]
        if kind != "plain":
            block = block.at[index[count + r]]
        up_block = None
        if has_up:
            width = up.shape[1]
            if kind == "pool":
                up_block = held[1].at[index[count + r]]
            else:
                up_block = block.at[:, pl.ds(up_first, width)]
        load(r, block, first, up_block)

    for r in range(count):
        at = 0
        for s, (kind, first, up_first) in enumerate(kinds):
            width = 2 if kind == "pool" else 1
            held, at = arrays[at : at + width], at + width
            if len(kinds) == 1:
                load_from(r, kind, first, up_first, held)
            else:

                @pl.when(index[r] == s)
                def _(r=r, kind=kind, first=first, up_first=up_first, held=held):
                    load_from(r, kind, first, up_first, held)

    for k in range(chunks):
        pltpu.make_async_copy(
            tokens.at[:, pl.ds(lo + k * step, step)], rows.at[k], row_sem.at[k]
        ).start()
    for k in range(chunks):
        pltpu.make_async_copy(down.at[k], down.at[k], block_sem.at[k]).wait()
        pltpu.make_async_copy(rows.at[k], rows.at[k], row_sem.at[k]).wait()
        full = lax.dot_general(
            rows[k], down[k], (((1,), (1,)), ((), ())), preferred_element_type=jnp.float32
        )
        if k:
            full = total[...] + full
        if k < chunks - 1:
            total[...] = full
    if has_up:
        pltpu.make_async_copy(up, up, block_sem.at[chunks]).wait()
    which = request_of_rows(ends, count, 0, full.shape[0])
    code = full[:, :rank]
    for r in range(1, count):
        code = jnp.where(which == r, full[:, r * rank : (r + 1) * rank], code)
    half = full.shape[0] // 2
    code = jnp.concatenate([code[:half], code[half:]], axis=1)
    out[...] = code + before[...] if has_before else code


def codes(index, ends, tokens, sources, cut, step, columns=0, before=None):
    many = tokens.shape[0]
    count = ends.shape[0]
    rank = sources[0][1][0].shape[-2]
    chunks = (cut[1] - cut[0]) // step
    kinds = [(kind, first, up_first) for kind, _, first, up_first in sources]
    arrays = [array for _, held, _, _ in sources for array in held]
    out_shape = [jax.ShapeDtypeStruct((many // 2, 2 * rank), jnp.float32)]
    if columns:
        out_shape.append(jax.ShapeDtypeStruct((count * rank, columns), tokens.dtype))
    extra = [] if before is None else [before]
    return pl.pallas_call(
        functools.partial(
            code_kernel, count, cut, step, kinds, columns > 0, before is not None
        ),
        grid_spec=pltpu.PrefetchScalarGridSpec(
            num_scalar_prefetch=2,
            grid=(),
            in_specs=[ANY] * (1 + len(arrays)) + [VMEM] * len(extra),
            out_specs=[VMEM] * len(out_shape),
            scratch_shapes=[
                pltpu.VMEM((chunks, count * rank, step), tokens.dtype),
                pltpu.VMEM((chunks, many, step), tokens.dtype),
                pltpu.VMEM((many, count * rank), jnp.float32),
                pltpu.SemaphoreType.DMA((chunks + 1,)),
                pltpu.SemaphoreType.DMA((chunks,)),
            ],
        ),
        out_shape=out_shape,
        compiler_params=pltpu.CompilerParams(vmem_limit_bytes=40 * MIB),
        cost_estimate=pl.CostEstimate(
            flops=2 * many * (cut[1] - cut[0]) * count * rank,
            bytes_accessed=(cut[1] - cut[0]) * (many + count * rank) * 2,
            transcendentals=0,
        ),
        name="codes",
    )(index, ends, in_hbm(tokens), *arrays, *extra)


def finish_kernel(count, parts, tile, ends, *refs):
    code_parts, (base, up, out, hold, sem) = refs[:parts], refs[parts:]
    rank = up.shape[0] // count
    code = code_parts[0][...]
    for p in range(1, parts):
        code = code + code_parts[p][...]
    half = code.shape[0]
    copies = []
    for i in range(out.shape[0] // tile):
        first = i * tile
        side, at = first // half, first % half
        mine = code[at : at + tile, side * rank : (side + 1) * rank]
        which = request_of_rows(ends, count, first, tile)
        zero = jnp.zeros_like(mine)
        wide = jnp.concatenate([jnp.where(which == r, mine, zero) for r in range(count)], axis=1)
        delta = None
        for _ in range(3):
            part = wide.astype(jnp.bfloat16)
            wide = wide - part.astype(jnp.float32)
            term = jnp.dot(part, up[...], preferred_element_type=jnp.float32)
            delta = term if delta is None else delta + term
        rows = pl.ds(first, tile)
        hold[rows, :] = (base[rows, :] + ADAPTER_SCALE * delta).astype(hold.dtype)
        copies.append(pltpu.make_async_copy(hold.at[rows, :], out.at[rows, :], sem.at[i]))
        copies[-1].start()
    for copy in copies:
        copy.wait()


def finish(ends, code_parts, base, up):
    many, columns = base.shape
    count = ends.shape[0]
    parts = len(code_parts)
    tile = min(256, many // 2)
    return pl.pallas_call(
        functools.partial(finish_kernel, count, parts, tile),
        grid_spec=pltpu.PrefetchScalarGridSpec(
            num_scalar_prefetch=1,
            grid=(),
            in_specs=[VMEM] * (parts + 2),
            out_specs=ANY,
            scratch_shapes=[
                pltpu.VMEM((many, columns), jnp.bfloat16),
                pltpu.SemaphoreType.DMA((many // tile,)),
            ],
        ),
        out_shape=jax.ShapeDtypeStruct((many, columns), jnp.bfloat16),
        compiler_params=pltpu.CompilerParams(vmem_limit_bytes=24 * MIB),
        name="finish",
    )(ends, *code_parts, pltpu.with_memory_space_constraint(base, pltpu.VMEM), up)


def gathered(part, axis, size):
    held = [part]
    for step in range(1, size):
        held.append(lax.ppermute(part, axis, [(i, (i + step) % size) for i in range(size)]))
    return held


def after(x, earlier):
    return lax.optimization_barrier((x, earlier))


def exchange(adapter_ids, owner_map, down_pool, up_pool):
    rows = adapter_ids.shape[0]
    width = down_pool.shape[2]
    most = width // 4 * 3
    names = {
        "4": (4, 0, width, 1), "7a": (7, 0, most, 1), "1": (1, 0, width, 1),
        "5": (5, 0, width, 1), "6a": (6, 0, most, 1), "2": (2, 0, width, 1),
        "3": (3, 0, width, 1), "6b": (6, most, width, 0), "7b": (7, most, width, 0),
    }
    sends = pick(list(names.values()), adapter_ids, owner_map, down_pool, up_pool)
    sends = dict(zip(names, sends))
    got = {}

    def swap(name, earlier=None):
        send = sends[name]
        if earlier is not None:
            send, got[earlier] = after(send, got[earlier])
        pairs = [(i, i ^ names[name][0]) for i in range(rows)]
        got[name] = lax.ppermute(send, "dp", pairs)

    for name, earlier in (
        ("4", None), ("7a", None), ("5", "7a"), ("1", "7a"), ("6a", "4"), ("2", "1"),
        ("3", "2"), ("6b", "6a"), ("7b", "5"),
    ):
        swap(name, earlier)
    return got, most


def shards(sizes, tokens, key_weight, down_pool, up_pool, adapter_ids, lengths, owner_map):
    n_groups, n_dp, n_tensor = sizes
    held, _, width = down_pool.shape
    columns = up_pool.shape[2]
    member = lax.axis_index("dp")
    by_swaps = n_dp == 8 and width % 512 == 0

    late_tokens = tokens
    if by_swaps:
        got, most = exchange(adapter_ids, owner_map, down_pool, up_pool)
        late_tokens, got["2"] = after(tokens, got["2"])

    me = lax.axis_index("tensor")
    base = None
    for step in reversed(range(n_tensor)):
        to = lax.rem(me + step, n_tensor)
        weight = lax.dynamic_slice_in_dim(key_weight, to * columns, columns, 1)
        part = jnp.dot(late_tokens, weight, preferred_element_type=jnp.float32)
        if step:
            part = lax.ppermute(
                part, "tensor", [(i, (i + step) % n_tensor) for i in range(n_tensor)]
            )
        base = part if base is None else base + part
    my_ids = lax.dynamic_index_in_dim(adapter_ids, member, 0, keepdims=False)
    my_slots = owner_map[my_ids]
    owners = my_slots // held
    ends = jnp.cumsum(lengths[0]).astype(jnp.int32)

    if by_swaps:
        index = jnp.concatenate([owners ^ member, my_slots % held])
        base, got["7a"], index = lax.optimization_barrier((base, got["7a"], index))

        def sources(first, up_first, six, seven):
            mine = [("pool", (down_pool, up_pool), first, 0)]
            near = [("plain", (got[str(s)],), first, width) for s in range(1, 6)]
            return mine + near + [("plain", (got[name],), *at) for name, *at in (six, seven)]

        most_of = sources(0, width, ("6a", 0, most), ("7a", 0, most))
        rest_of = sources(most, width, ("6b", 0, 0), ("7b", 0, 0))
        step = width // 4
        code, up = codes(index, ends, tokens, most_of, (0, most), step, columns)
        (code,) = codes(index, ends, tokens, rest_of, (most, width), step, before=code)
    else:
        blocks = dense(adapter_ids, owner_map, down_pool, up_pool)
        index = jnp.concatenate([owners, owners])
        whole = [("several", (blocks,), 0, width)]
        code, up = codes(index, ends, tokens, whole, (0, width), width, columns)
    code_parts = gathered(code, "tensor", n_tensor)
    return finish(ends, code_parts, base, up)


def solution(mesh):
    placed = (
        P(("groups", "dp"), "tensor"),
        P("tensor", None),
        P("dp", None, "tensor"),
        P("dp", None, "tensor"),
        P("groups", None),
        P(("groups", "dp"), None),
        P("groups"),
    )
    sizes = tuple(mesh.shape[name] for name in ("groups", "dp", "tensor"))
    return jax.shard_map(
        functools.partial(shards, sizes),
        mesh=mesh,
        in_specs=placed,
        out_specs=P(("groups", "dp"), "tensor"),
        check_vma=False,
    )
```

```python
import functools

import jax
import jax.numpy as jnp
from jax import lax
from jax.experimental import pallas as pl
from jax.experimental.pallas import tpu as pltpu
from jax.sharding import PartitionSpec as P

ADAPTER_SCALE = 2.0
MIB = 1 << 20
ANY = pl.BlockSpec(memory_space=pl.ANY)
VMEM = pl.BlockSpec(memory_space=pltpu.VMEM)


def in_hbm(x):
    return pltpu.with_memory_space_constraint(x, pltpu.HBM)


X_STEPS = 4
Z_STEPS = 6
NEVER = 1000.0
E_TABLE, O_TABLE, X_TABLE, PLACE, MISFIT = range(5)


def plan_kernel(held, planes, req, ids, owner_map, out):
    n = planes * req
    member = lax.axis_index("dp")
    plane, column = member // 2, member % 2
    lane = lax.broadcasted_iota(jnp.int32, (n, 128), 1)
    sub = lax.broadcasted_iota(jnp.int32, (n, 128), 0)
    lane_f, sub_f = lane.astype(jnp.float32), sub.astype(jnp.float32)

    def row_of(at):
        return sum([(at >= q * req).astype(jnp.float32) for q in range(1, planes)])

    dest_i, dest_k = row_of(lane), row_of(sub)

    def entries(c):
        by_lane = [jnp.full((n, 128), -1.0, jnp.float32) for _ in range(5)]
        by_sub = [jnp.full((n, 128), -2.0, jnp.float32) for _ in range(5)]
        for i in range(n):
            slot = owner_map[ids[i % req, 2 * (i // req) + c]]
            owner = slot // held
            values = (slot, owner, owner // 2, owner % 2, slot - owner * held)
            for v, value in enumerate(values):
                value = value.astype(jnp.float32)
                by_lane[v] = jnp.where(lane == i, value, by_lane[v])
                by_sub[v] = jnp.where(sub == i, value, by_sub[v])
        return by_lane, by_sub

    def over_x(by_lane, by_sub, c):
        (slot_i, owner_i, src_i, col_i, _), (slot_k, owner_k, src_k, col_k, _) = by_lane, by_sub
        c = c.astype(jnp.float32)
        same = slot_i == slot_k
        key_i = jnp.where(col_i == c, -1.0, jnp.abs(dest_i - src_i) * n + (n - 1 - lane_f))
        key_k = jnp.where(col_k == c, -1.0, jnp.abs(dest_k - src_k) * n + (n - 1 - sub_f))
        best_i = jnp.max(jnp.where(same, key_k, -1.0), axis=0, keepdims=True)
        best_k = jnp.max(jnp.where(same, key_i, -1.0), axis=1, keepdims=True)
        ahead = (key_k == best_k) & (key_k >= 0) & (owner_k == owner_i) & (key_k > best_i)
        pos = jnp.sum(jnp.where(ahead, 1.0, 0.0), axis=0, keepdims=True)
        return pos, (key_i == best_i) & (key_i >= 0)

    here = column.astype(jnp.float32)
    by_lane, by_sub = entries(column)
    slot_i, _, src_i, col_i, within_i = by_lane
    same = slot_i == by_sub[0]
    xpos, _ = over_x(by_lane, by_sub, column)
    other_lane, other_sub = entries(1 - column)
    other_xpos, other_lead = over_x(other_lane, other_sub, 1 - column)

    def top(x):
        return jnp.broadcast_to(x[0:1, :], (8, 128))

    row = lax.broadcasted_iota(jnp.int32, (8, 128), 0)
    lane8 = lax.broadcasted_iota(jnp.int32, (8, 128), 1).astype(jnp.float32)
    row_f = row.astype(jnp.float32)
    links = planes - 1
    up = row < links
    last = float(planes - 1)
    dest, src = top(dest_i), top(src_i)
    d_dest, d_src = jnp.where(up, dest, last - dest), jnp.where(up, src, last - src)
    link = jnp.where(up, row_f, row_f - links)

    def beyond(sign):
        more = same & ((dest_k - dest_i) * sign > 0)
        return top(jnp.max(jnp.where(more, 1.0, 0.0), axis=0, keepdims=True)) == 0

    not_beyond = jnp.where(up, jnp.where(beyond(1.0), 1.0, 0.0), jnp.where(beyond(-1.0), 1.0, 0.0))
    valid = (row < 2 * links) & (lane8 < n)
    lead = valid & (not_beyond == 1.0) & (d_dest > d_src)
    on = lead & (d_src <= link) & (d_dest > link)
    starts = d_src == link
    local = top(col_i) == here
    first = jnp.where(local, 0.0, top(jnp.broadcast_to(xpos, (8, 128))) + 1)
    ready = jnp.where(starts, first, NEVER)
    pos = jnp.full((8, 128), NEVER, jnp.float32)
    for t in range(Z_STEPS):
        open_ = on & (ready <= t) & (pos >= NEVER)
        key = jnp.where(open_, d_dest * 128 + (127 - lane8), -1.0)
        chosen = open_ & (key == jnp.max(key, axis=1, keepdims=True))
        pos = jnp.where(chosen, float(t), pos)
        before = jnp.concatenate([pos[7:8, :], pos[0:7, :]], axis=0)
        ready = jnp.where(starts, first, before + 1)
    misfit = jnp.max(jnp.where(on & (pos >= NEVER), 1.0, 0.0), axis=1, keepdims=True)
    misfit = jnp.max(misfit, axis=0, keepdims=True)

    from_x = float(held)
    from_e = from_x + X_STEPS
    from_o = from_e + Z_STEPS
    own = jnp.where(local, top(within_i), from_x + top(jnp.broadcast_to(xpos, (8, 128))))

    def table(hit, source):
        return jnp.sum(jnp.where(hit, source + 1, 0.0), axis=1, keepdims=True) - 1

    def only(which, x):
        return jnp.sum(jnp.where(row == which, x, 0.0), axis=0, keepdims=True)

    def sent(which, passing_from):
        hit = only(which, jnp.where(on, 1.0, 0.0)) == 1.0
        fresh = only(which, jnp.where(starts, 1.0, 0.0)) == 1.0
        at, earlier = only(which, pos), only(which - 1, pos)
        source = jnp.where(fresh, own, passing_from + earlier)
        return table(hit & (at == row_f), source)

    e_row = jnp.where(plane % 2 == 0, plane, links + (planes - 1 - plane))
    o_row = jnp.where(plane == 1, 1, jnp.where(plane == 2, links + 1, 7))
    e_table = sent(e_row, from_o)
    o_table = sent(o_row, from_e)
    (_, owner_o, _, _, within_o) = other_lane
    mine = top(owner_o) == member.astype(jnp.float32)
    other_lead8 = top(jnp.where(other_lead, 1.0, 0.0)) == 1.0
    other_xpos8 = top(jnp.broadcast_to(other_xpos, (8, 128)))
    x_table = table(mine & other_lead8 & (other_xpos8 == row_f), top(within_o))

    arrival = jnp.zeros((8, 128), jnp.float32)
    for which in range(2 * links):
        one = jnp.broadcast_to(pos[which : which + 1, :], (n, 128))
        one_on = jnp.broadcast_to(jnp.where(on, 1.0, 0.0)[which : which + 1, :], (n, 128))
        by_k = jnp.sum(jnp.where((lane == sub) & (one_on == 1.0), one + 1, 0.0), axis=1, keepdims=True)
        arrives = jnp.max(jnp.where(same, by_k, 0.0), axis=0, keepdims=True) - 1
        if which < links:
            hit = (dest > src) & (dest == which + 1)
        else:
            hit = (dest < src) & (last - dest == which - links + 1)
        arrival = jnp.where(hit, arrives, arrival)
    odd = dest - 2 * jnp.floor(dest * 0.5)
    outer = jnp.where(dest > src, odd, 1 - odd) == 1.0
    final = jnp.where(dest == src, own, jnp.where(outer, from_e, from_o) + arrival)
    my_rows = lane8 == (plane * req).astype(jnp.float32) + row_f
    place = jnp.sum(jnp.where(my_rows & (row < req), final, 0.0), axis=1, keepdims=True)
    place = jnp.where(misfit == 1.0, 0.0, place)
    result = jnp.zeros((8, 128), jnp.float32)
    for at, values in ((E_TABLE, e_table), (O_TABLE, o_table), (X_TABLE, x_table), (PLACE, place), (MISFIT, misfit)):
        result = jnp.where(lane8 == at, values, result)
    out[...] = result.astype(jnp.int32)


def plan(held, adapter_ids, owner_map):
    rows, req = adapter_ids.shape
    return pl.pallas_call(
        functools.partial(plan_kernel, held, rows // 2, req),
        grid_spec=pltpu.PrefetchScalarGridSpec(
            num_scalar_prefetch=2, grid=(), in_specs=[], out_specs=VMEM
        ),
        out_shape=jax.ShapeDtypeStruct((8, 128), jnp.int32),
        compiler_params=pltpu.CompilerParams(vmem_limit_bytes=4 * MIB),
        name="plan",
    )(adapter_ids.T, owner_map)


def pick_kernel(step, size, lo, streams, held, table, down, up, *refs):
    at = 0
    got = []
    for many in held:
        got.append(refs[at : at + many])
        at += many
    outs, sem = refs[at:-1], refs[-1]
    slots, _, width = down.shape
    from_x, from_e, from_o = slots, slots + X_STEPS, slots + X_STEPS + Z_STEPS
    over_x = [(from_x + t, ref) for t, ref in enumerate(got[2])]
    outer = [(from_e + t, ref) for t, ref in enumerate(got[0])]
    middle = [(from_o + t, ref) for t, ref in enumerate(got[1])]
    sources = {E_TABLE: over_x + middle, O_TABLE: over_x + outer, X_TABLE: []}
    rows = pl.ds(lo, size)
    for i, stream in enumerate(streams):
        code, out = table[step, stream], outs[i]

        @pl.when((code >= 0) & (code < slots))
        def _(code=code, out=out, i=i):
            pltpu.make_async_copy(
                down.at[code, rows, :], out.at[:, pl.ds(0, width)], sem.at[i]
            ).start()
            pltpu.make_async_copy(
                up.at[code, rows, :], out.at[:, pl.ds(width, up.shape[2])], sem.at[i]
            ).start()

        for number, ref in sources[stream]:

            @pl.when(code == number)
            def _(ref=ref, out=out, i=i):
                pltpu.make_async_copy(ref, out, sem.at[i]).start()

    for i, stream in enumerate(streams):

        @pl.when(table[step, stream] >= 0)
        def _(i=i):
            pltpu.make_async_copy(outs[i], outs[i], sem.at[i]).wait()


def pick(step, lo, size, streams, table, down_pool, up_pool, got):
    wide = down_pool.shape[2] + up_pool.shape[2]
    held = [len(arrays) for arrays in got]
    return pl.pallas_call(
        functools.partial(pick_kernel, step, size, lo, streams, held),
        grid_spec=pltpu.PrefetchScalarGridSpec(
            num_scalar_prefetch=1,
            grid=(),
            in_specs=[ANY] * (2 + sum(held)),
            out_specs=[ANY] * len(streams),
            scratch_shapes=[pltpu.SemaphoreType.DMA((len(streams),))],
        ),
        out_shape=[pltpu.VMEM((size, wide), down_pool.dtype)] * len(streams),
        compiler_params=pltpu.CompilerParams(vmem_limit_bytes=2 * MIB),
        name="pick",
    )(table, in_hbm(down_pool), in_hbm(up_pool), *[a for arrays in got for a in arrays])


def dense_kernel(index, down, up, out):
    width = down.shape[2]
    out[:, :, :width] = down[...]
    out[:, :, width:] = up[...]


def dense(adapter_ids, owner_map, down_pool, up_pool):
    held, rank, width = down_pool.shape
    columns = up_pool.shape[2]
    slots = owner_map[adapter_ids] - lax.axis_index("dp") * held
    here = (slots >= 0) & (slots < held)
    index = jnp.sum(jnp.where(here, slots, 0), axis=1).astype(jnp.int32)
    many = index.shape[0]
    send = pl.pallas_call(
        dense_kernel,
        grid_spec=pltpu.PrefetchScalarGridSpec(
            num_scalar_prefetch=1,
            grid=(many,),
            in_specs=[
                pl.BlockSpec((1, rank, width), lambda j, index: (index[j], 0, 0)),
                pl.BlockSpec((1, rank, columns), lambda j, index: (index[j], 0, 0)),
            ],
            out_specs=pl.BlockSpec((1, rank, width + columns), lambda j, index: (j, 0, 0)),
        ),
        out_shape=jax.ShapeDtypeStruct((many, rank, width + columns), down_pool.dtype),
        name="pick_all",
    )(index, down_pool, up_pool)
    return lax.all_to_all(send, "dp", split_axis=0, concat_axis=0, tiled=True)


def request_of_rows(ends, count, first, rows):
    at = first + lax.broadcasted_iota(jnp.int32, (rows, 1), 0)
    which = jnp.zeros((rows, 1), jnp.int32)
    for r in range(count - 1):
        which += (at >= ends[r]).astype(jnp.int32)
    return which


def code_kernel(count, step, kinds, index, ends, tokens, *refs):
    n = sum(many for _, many in kinds)
    arrays, refs = refs[:n], refs[n:]
    out, up, down, rows, total, block_sem, row_sem = refs
    rank, columns = out.shape[1] // 2, up.shape[1]
    features = tokens.shape[1]
    chunks = features // step

    def load(r, kind, held):
        if kind == "pool":
            slot = index[r]
            parts = [(held[0].at[slot], held[1].at[slot])]
        elif kind == "several":
            block = held[0].at[index[r]]
            parts = [(block, block.at[:, pl.ds(features, columns)])]
        else:
            parts = [(ref, ref.at[:, pl.ds(features, columns)]) for ref in held]
        size = rank // len(parts)
        for p, (down_part, up_part) in enumerate(parts):
            mine = pl.ds(r * rank + p * size, size)
            for k in range(chunks):
                pltpu.make_async_copy(
                    down_part.at[:, pl.ds(k * step, step)], down.at[k, mine, :], block_sem.at[k]
                ).start()
            pltpu.make_async_copy(up_part, up.at[mine, :], block_sem.at[chunks]).start()

    for r in range(count):
        at, number = 0, 0
        for kind, many in kinds:
            held = arrays[at : at + many]
            at += many
            if kind == "several":
                load(r, kind, held)
            elif kind == "pool":
                number = held[0].shape[0]

                @pl.when(index[r] < number)
                def _(r=r, kind=kind, held=held):
                    load(r, kind, held)

            else:

                @pl.when(index[r] == number)
                def _(r=r, kind=kind, held=held):
                    load(r, kind, held)

                number += 1

    for k in range(chunks):
        pltpu.make_async_copy(
            tokens.at[:, pl.ds(k * step, step)], rows.at[k], row_sem.at[k]
        ).start()
    for k in range(chunks):
        pltpu.make_async_copy(down.at[k], down.at[k], block_sem.at[k]).wait()
        pltpu.make_async_copy(rows.at[k], rows.at[k], row_sem.at[k]).wait()
        full = lax.dot_general(
            rows[k], down[k], (((1,), (1,)), ((), ())), preferred_element_type=jnp.float32
        )
        if k:
            full = total[...] + full
        if k < chunks - 1:
            total[...] = full
    pltpu.make_async_copy(up, up, block_sem.at[chunks]).wait()
    which = request_of_rows(ends, count, 0, full.shape[0])
    code = full[:, :rank]
    for r in range(1, count):
        code = jnp.where(which == r, full[:, r * rank : (r + 1) * rank], code)
    half = full.shape[0] // 2
    out[...] = jnp.concatenate([code[:half], code[half:]], axis=1)


def codes(index, ends, tokens, sources, rank, columns):
    many, features = tokens.shape
    count = ends.shape[0]
    chunks = 4 if features % 512 == 0 else 1
    step = features // chunks
    kinds = [(kind, len(held)) for kind, held in sources]
    arrays = [array for _, held in sources for array in held]
    return pl.pallas_call(
        functools.partial(code_kernel, count, step, kinds),
        grid_spec=pltpu.PrefetchScalarGridSpec(
            num_scalar_prefetch=2,
            grid=(),
            in_specs=[ANY] * (1 + len(arrays)),
            out_specs=[VMEM, VMEM],
            scratch_shapes=[
                pltpu.VMEM((chunks, count * rank, step), tokens.dtype),
                pltpu.VMEM((chunks, many, step), tokens.dtype),
                pltpu.VMEM((many, count * rank), jnp.float32),
                pltpu.SemaphoreType.DMA((chunks + 1,)),
                pltpu.SemaphoreType.DMA((chunks,)),
            ],
        ),
        out_shape=[
            jax.ShapeDtypeStruct((many // 2, 2 * rank), jnp.float32),
            jax.ShapeDtypeStruct((count * rank, columns), tokens.dtype),
        ],
        compiler_params=pltpu.CompilerParams(vmem_limit_bytes=32 * MIB),
        name="codes",
    )(index, ends, in_hbm(tokens), *arrays)


def finish_kernel(count, parts, tile, ends, *refs):
    code_parts, (low, high, up, out, hold, sem) = refs[:parts], refs[parts:]
    rank = up.shape[0] // count
    code = code_parts[0][...]
    for p in range(1, parts):
        code = code + code_parts[p][...]
    half = code.shape[0]
    copies = []
    for i in range(out.shape[0] // tile):
        first = i * tile
        side, at = first // half, first % half
        mine = code[at : at + tile, side * rank : (side + 1) * rank]
        which = request_of_rows(ends, count, first, tile)
        zero = jnp.zeros_like(mine)
        wide = jnp.concatenate([jnp.where(which == r, mine, zero) for r in range(count)], axis=1)
        delta = None
        for _ in range(3):
            part = wide.astype(jnp.bfloat16)
            wide = wide - part.astype(jnp.float32)
            term = jnp.dot(part, up[...], preferred_element_type=jnp.float32)
            delta = term if delta is None else delta + term
        rows = pl.ds(first, tile)
        base = (low, high)[side][at : at + tile, :]
        hold[rows, :] = (base + ADAPTER_SCALE * delta).astype(hold.dtype)
        copies.append(pltpu.make_async_copy(hold.at[rows, :], out.at[rows, :], sem.at[i]))
        copies[-1].start()
    for copy in copies:
        copy.wait()


def finish(ends, code_parts, base, up):
    many, columns = 2 * base[0].shape[0], base[0].shape[1]
    count = ends.shape[0]
    parts = len(code_parts)
    tile = min(256, many // 2)
    return pl.pallas_call(
        functools.partial(finish_kernel, count, parts, tile),
        grid_spec=pltpu.PrefetchScalarGridSpec(
            num_scalar_prefetch=1,
            grid=(),
            in_specs=[VMEM] * (parts + 3),
            out_specs=ANY,
            scratch_shapes=[
                pltpu.VMEM((many, columns), jnp.bfloat16),
                pltpu.SemaphoreType.DMA((many // tile,)),
            ],
        ),
        out_shape=jax.ShapeDtypeStruct((many, columns), jnp.bfloat16),
        compiler_params=pltpu.CompilerParams(vmem_limit_bytes=24 * MIB),
        name="finish",
    )(ends, *code_parts, *base, up)


def gathered(part, axis, size):
    held = [part]
    for step in range(1, size):
        held.append(lax.ppermute(part, axis, [(i, (i + step) % size) for i in range(size)]))
    return held


def after(x, earlier):
    return lax.optimization_barrier((x, earlier))


def route(table, down_pool, up_pool, n_dp, pieces):
    rank = down_pool.shape[1]
    size = rank // 2
    outer = [(i, i ^ 2) for i in range(n_dp)]
    middle = [(i, i + 2) for i in (2, 3)] + [(i, i - 2) for i in (4, 5)]
    over_x = [(i, i ^ 1) for i in range(n_dp)]
    got = [([], [], []), ([], [], [])]
    done = []
    for step in range(Z_STEPS):
        streams = [E_TABLE, O_TABLE] + ([X_TABLE] if step < X_STEPS else [])
        for part in range(2):
            known = [list(arrays) for arrays in got[part]]
            sends = pick(step, part * size, size, streams, table, down_pool, up_pool, known)
            for stream, send in zip(streams, sends):
                pairs = (outer, middle, over_x)[stream]
                got[part][stream].append(lax.ppermute(send, "dp", pairs))
        if 1 <= step <= len(pieces):
            held = got[0][0][step - 1]
            piece, got[0][0][step - 1] = pieces[step - 1](held)
            table, piece = after(table, piece)
            done.append(piece)
    return got, done


def base_piece(tokens, weight, first, many):
    def run(arrival):
        rows, arrival = after(tokens, arrival)
        rows = lax.slice_in_dim(rows, first, first + many, axis=0)
        return jnp.dot(rows, weight, preferred_element_type=jnp.float32), arrival

    return run


def shards(sizes, tokens, key_weight, down_pool, up_pool, adapter_ids, lengths, owner_map):
    n_groups, n_dp, n_tensor = sizes
    held, rank, width = down_pool.shape
    columns = up_pool.shape[2]
    member = lax.axis_index("dp")
    me = lax.axis_index("tensor")
    half = tokens.shape[0] // 2
    ends = jnp.cumsum(lengths[0]).astype(jnp.int32)

    def weight_of(to):
        return lax.dynamic_slice_in_dim(key_weight, to * columns, columns, 1)

    def sent_on(part, step):
        pairs = [(i, (i + step) % n_tensor) for i in range(n_tensor)]
        return lax.ppermute(part, "tensor", pairs)

    def by_all_to_all():
        blocks = dense(adapter_ids, owner_map, down_pool, up_pool)
        my_ids = lax.dynamic_index_in_dim(adapter_ids, member, 0, keepdims=False)
        index = owner_map[my_ids] // held
        return tuple(codes(index, ends, tokens, [("several", (blocks,))], rank, columns))

    if n_dp == 8 and n_tensor == 2 and rank % 32 == 0 and adapter_ids.shape[1] == 4:
        table = plan(held, adapter_ids, owner_map)
        theirs, mine = weight_of(1 - me), weight_of(me)
        pieces = [
            base_piece(tokens, weight, first, half)
            for weight in (theirs, mine)
            for first in (0, half)
        ]
        got, done = route(table, down_pool, up_pool, n_dp, pieces)
        base = [here + sent_on(there, 1) for there, here in zip(done[:2], done[2:])]
        misfit = table[0, MISFIT].reshape(1)
        misfit = jnp.maximum(misfit, lax.ppermute(misfit, "dp", [(i, i ^ 1) for i in range(n_dp)]))
        for other in gathered(misfit, "groups", n_groups)[1:]:
            misfit = jnp.maximum(misfit, other)
        index = table[: adapter_ids.shape[1], PLACE]
        sources = [("pool", (down_pool, up_pool))]
        for stream in (2, 0, 1):
            sources += [("block", pair) for pair in zip(got[0][stream], got[1][stream])]
        routed = tuple(codes(index, ends, tokens, sources, rank, columns))
        code, up = lax.cond(misfit[0] == 0, lambda: routed, by_all_to_all)
    else:
        base = None
        for step in reversed(range(n_tensor)):
            weight = weight_of(lax.rem(me + step, n_tensor))
            part = jnp.dot(tokens, weight, preferred_element_type=jnp.float32)
            part = sent_on(part, step) if step else part
            base = part if base is None else base + part
        base = [base[:half], base[half:]]
        code, up = by_all_to_all()
    code_parts = gathered(code, "tensor", n_tensor)
    return finish(ends, code_parts, base, up)


def solution(mesh):
    placed = (
        P(("groups", "dp"), "tensor"),
        P("tensor", None),
        P("dp", None, "tensor"),
        P("dp", None, "tensor"),
        P("groups", None),
        P(("groups", "dp"), None),
        P("groups"),
    )
    sizes = tuple(mesh.shape[name] for name in ("groups", "dp", "tensor"))
    return jax.shard_map(
        functools.partial(shards, sizes),
        mesh=mesh,
        in_specs=placed,
        out_specs=P(("groups", "dp"), "tensor"),
        check_vma=False,
    )
```

```python
import functools

import jax
import jax.numpy as jnp
from jax import lax
from jax.experimental import pallas as pl
from jax.experimental.pallas import tpu as pltpu
from jax.sharding import PartitionSpec as P

ADAPTER_SCALE = 2.0
MIB = 1 << 20
ANY = pl.BlockSpec(memory_space=pl.ANY)
VMEM = pl.BlockSpec(memory_space=pltpu.VMEM)


def in_vmem(x):
    return pltpu.with_memory_space_constraint(x, pltpu.VMEM)


def in_hbm(x):
    return pltpu.with_memory_space_constraint(x, pltpu.HBM)


X_STEPS = 4
Z_STEPS = 6
NEVER = 1000.0
E_TABLE, O_TABLE, X_TABLE, PLACE, MISFIT = range(5)


def plan_kernel(held, planes, req, ids, owner_map, out):
    n = planes * req
    member = lax.axis_index("dp")
    plane, column = member // 2, member % 2
    lane = lax.broadcasted_iota(jnp.int32, (n, 128), 1)
    sub = lax.broadcasted_iota(jnp.int32, (n, 128), 0)
    lane_f, sub_f = lane.astype(jnp.float32), sub.astype(jnp.float32)

    def row_of(at):
        return sum([(at >= q * req).astype(jnp.float32) for q in range(1, planes)])

    dest_i, dest_k = row_of(lane), row_of(sub)

    def entries(c):
        by_lane = [jnp.full((n, 128), -1.0, jnp.float32) for _ in range(5)]
        by_sub = [jnp.full((n, 128), -2.0, jnp.float32) for _ in range(5)]
        for i in range(n):
            slot = owner_map[ids[i % req, 2 * (i // req) + c]]
            owner = slot // held
            values = (slot, owner, owner // 2, owner % 2, slot - owner * held)
            for v, value in enumerate(values):
                value = value.astype(jnp.float32)
                by_lane[v] = jnp.where(lane == i, value, by_lane[v])
                by_sub[v] = jnp.where(sub == i, value, by_sub[v])
        return by_lane, by_sub

    def over_x(by_lane, by_sub, c):
        (slot_i, owner_i, src_i, col_i, _), (slot_k, owner_k, src_k, col_k, _) = by_lane, by_sub
        c = c.astype(jnp.float32)
        same = slot_i == slot_k
        key_i = jnp.where(col_i == c, -1.0, jnp.abs(dest_i - src_i) * n + (n - 1 - lane_f))
        key_k = jnp.where(col_k == c, -1.0, jnp.abs(dest_k - src_k) * n + (n - 1 - sub_f))
        best_i = jnp.max(jnp.where(same, key_k, -1.0), axis=0, keepdims=True)
        best_k = jnp.max(jnp.where(same, key_i, -1.0), axis=1, keepdims=True)
        ahead = (key_k == best_k) & (key_k >= 0) & (owner_k == owner_i) & (key_k > best_i)
        pos = jnp.sum(jnp.where(ahead, 1.0, 0.0), axis=0, keepdims=True)
        return pos, (key_i == best_i) & (key_i >= 0)

    row = lax.broadcasted_iota(jnp.int32, (8, 128), 0)
    lane8 = lax.broadcasted_iota(jnp.int32, (8, 128), 1).astype(jnp.float32)
    row_f = row.astype(jnp.float32)
    links = planes - 1
    up = row < links
    last = float(planes - 1)
    link = jnp.where(up, row_f, row_f - links)

    def top(x):
        return jnp.broadcast_to(x[0:1, :], (8, 128))

    def schedule(by_lane, by_sub, xpos, c):
        slot_i, _, src_i, col_i, _ = by_lane
        same = slot_i == by_sub[0]
        dest, src = top(dest_i), top(src_i)
        d_dest, d_src = jnp.where(up, dest, last - dest), jnp.where(up, src, last - src)

        def beyond(sign):
            more = same & ((dest_k - dest_i) * sign > 0)
            return top(jnp.max(jnp.where(more, 1.0, 0.0), axis=0, keepdims=True))

        farther = jnp.where(up, beyond(1.0), beyond(-1.0))
        valid = (row < 2 * links) & (lane8 < n)
        lead = valid & (farther == 0.0) & (d_dest > d_src)
        on = lead & (d_src <= link) & (d_dest > link)
        starts = d_src == link
        local = top(col_i) == c.astype(jnp.float32)
        first = jnp.where(local, 0.0, top(jnp.broadcast_to(xpos, (8, 128))) + 1)
        ready = jnp.where(starts, first, NEVER)
        pos = jnp.full((8, 128), NEVER, jnp.float32)
        for t in range(Z_STEPS):
            open_ = on & (ready <= t) & (pos >= NEVER)
            key = jnp.where(open_, d_dest * 128 + (127 - lane8), -1.0)
            chosen = open_ & (key == jnp.max(key, axis=1, keepdims=True))
            pos = jnp.where(chosen, float(t), pos)
            before = jnp.concatenate([pos[7:8, :], pos[0:7, :]], axis=0)
            ready = jnp.where(starts, first, before + 1)
        misfit = jnp.max(jnp.where(on & (pos >= NEVER), 1.0, 0.0), axis=1, keepdims=True)
        return same, dest, src, local, on, starts, pos, jnp.max(misfit, axis=0, keepdims=True)

    by_lane, by_sub = entries(column)
    within_i = by_lane[4]
    xpos, _ = over_x(by_lane, by_sub, column)
    same, dest, src, local, on, starts, pos, misfit = schedule(by_lane, by_sub, xpos, column)
    other_lane, other_sub = entries(1 - column)
    other_xpos, other_lead = over_x(other_lane, other_sub, 1 - column)
    other_misfit = schedule(other_lane, other_sub, other_xpos, 1 - column)[-1]
    misfit = jnp.maximum(misfit, other_misfit)

    from_x = float(held)
    from_e = from_x + X_STEPS
    from_o = from_e + Z_STEPS
    own = jnp.where(local, top(within_i), from_x + top(jnp.broadcast_to(xpos, (8, 128))))

    def table(hit, source):
        return jnp.sum(jnp.where(hit, source + 1, 0.0), axis=1, keepdims=True) - 1

    def only(which, x):
        return jnp.sum(jnp.where(row == which, x, 0.0), axis=0, keepdims=True)

    def sent(which, passing_from):
        hit = only(which, jnp.where(on, 1.0, 0.0)) == 1.0
        fresh = only(which, jnp.where(starts, 1.0, 0.0)) == 1.0
        at, earlier = only(which, pos), only(which - 1, pos)
        source = jnp.where(fresh, own, passing_from + earlier)
        return table(hit & (at == row_f), source)

    e_row = jnp.where(plane % 2 == 0, plane, links + (planes - 1 - plane))
    o_row = jnp.where(plane == 1, 1, jnp.where(plane == 2, links + 1, 7))
    e_table = sent(e_row, from_o)
    o_table = sent(o_row, from_e)
    (_, owner_o, _, _, within_o) = other_lane
    mine = top(owner_o) == member.astype(jnp.float32)
    other_lead8 = top(jnp.where(other_lead, 1.0, 0.0)) == 1.0
    other_xpos8 = top(jnp.broadcast_to(other_xpos, (8, 128)))
    x_table = table(mine & other_lead8 & (other_xpos8 == row_f), top(within_o))

    arrival = jnp.zeros((8, 128), jnp.float32)
    for which in range(2 * links):
        one = jnp.broadcast_to(pos[which : which + 1, :], (n, 128))
        one_on = jnp.broadcast_to(jnp.where(on, 1.0, 0.0)[which : which + 1, :], (n, 128))
        by_k = jnp.sum(jnp.where((lane == sub) & (one_on == 1.0), one + 1, 0.0), axis=1, keepdims=True)
        arrives = jnp.max(jnp.where(same, by_k, 0.0), axis=0, keepdims=True) - 1
        if which < links:
            hit = (dest > src) & (dest == which + 1)
        else:
            hit = (dest < src) & (last - dest == which - links + 1)
        arrival = jnp.where(hit, arrives, arrival)
    odd = dest - 2 * jnp.floor(dest * 0.5)
    outer = jnp.where(dest > src, odd, 1 - odd) == 1.0
    final = jnp.where(dest == src, own, jnp.where(outer, from_e, from_o) + arrival)
    my_rows = lane8 == (plane * req).astype(jnp.float32) + row_f
    place = jnp.sum(jnp.where(my_rows & (row < req), final, 0.0), axis=1, keepdims=True)
    place = jnp.where(misfit == 1.0, 0.0, place)
    result = jnp.zeros((8, 128), jnp.float32)
    for at, values in ((E_TABLE, e_table), (O_TABLE, o_table), (X_TABLE, x_table), (PLACE, place), (MISFIT, misfit)):
        result = jnp.where(lane8 == at, values, result)
    out[...] = result.astype(jnp.int32)


def plan(held, adapter_ids, owner_map):
    rows, req = adapter_ids.shape
    return pl.pallas_call(
        functools.partial(plan_kernel, held, rows // 2, req),
        grid_spec=pltpu.PrefetchScalarGridSpec(
            num_scalar_prefetch=2, grid=(), in_specs=[], out_specs=VMEM
        ),
        out_shape=jax.ShapeDtypeStruct((8, 128), jnp.int32),
        compiler_params=pltpu.CompilerParams(vmem_limit_bytes=4 * MIB),
        name="plan",
    )(adapter_ids.T, owner_map)


def pick_kernel(step, size, lo, streams, held, piece, table, down, up, *refs):
    at = 0
    got = []
    for many in held:
        got.append(refs[at : at + many])
        at += many
    refs = list(refs[at:])
    if piece is not None:
        tokens, weight = refs.pop(0), refs.pop(0)
        held_weight, weight_sem = refs.pop(-2), refs.pop(-1)
        distance, shift = piece
        columns, wide = up.shape[2], held_weight.shape[1]
        to = lax.rem(lax.axis_index("tensor") + distance, 2)
        first = pl.multiple_of(to * columns + shift, 128)
        load = pltpu.make_async_copy(weight.at[:, pl.ds(first, wide)], held_weight, weight_sem)
        load.start()
    outs, sem = refs[: len(streams)], refs[-1]
    slots, _, width = down.shape
    from_x, from_e, from_o = slots, slots + X_STEPS, slots + X_STEPS + Z_STEPS
    over_x = [(from_x + t, ref) for t, ref in enumerate(got[2])]
    outer = [(from_e + t, ref) for t, ref in enumerate(got[0])]
    middle = [(from_o + t, ref) for t, ref in enumerate(got[1])]
    sources = {E_TABLE: over_x + middle, O_TABLE: over_x + outer, X_TABLE: []}
    rows = pl.ds(lo, size)
    for i, stream in enumerate(streams):
        code, out = table[step, stream], outs[i]

        @pl.when((code >= 0) & (code < slots))
        def _(code=code, out=out, i=i):
            pltpu.make_async_copy(
                down.at[code, rows, :], out.at[:, pl.ds(0, width)], sem.at[i]
            ).start()
            pltpu.make_async_copy(
                up.at[code, rows, :], out.at[:, pl.ds(width, up.shape[2])], sem.at[i]
            ).start()

        for number, ref in sources[stream]:

            @pl.when(code == number)
            def _(ref=ref, out=out, i=i):
                pltpu.make_async_copy(ref, out, sem.at[i]).start()

    if piece is not None:
        load.wait()
        product = refs[len(streams)]
        tile = min(256, product.shape[0])
        for first in range(0, product.shape[0], tile):
            product[first : first + tile, :] = jnp.dot(
                tokens[first : first + tile, :],
                held_weight[...],
                preferred_element_type=jnp.float32,
            )

    for i, stream in enumerate(streams):

        @pl.when(table[step, stream] >= 0)
        def _(i=i):
            pltpu.make_async_copy(outs[i], outs[i], sem.at[i]).wait()


def pick(step, lo, size, streams, table, down_pool, up_pool, got, piece, tokens, key_weight):
    many, features = tokens.shape
    columns = up_pool.shape[2]
    wide = down_pool.shape[2] + columns
    held = [len(arrays) for arrays in got]
    operands = [in_hbm(down_pool), in_hbm(up_pool)] + [a for arrays in got for a in arrays]
    in_specs = [ANY] * len(operands)
    out_specs = [ANY] * len(streams)
    out_shape = [pltpu.VMEM((size, wide), down_pool.dtype)] * len(streams)
    scratch = [pltpu.SemaphoreType.DMA((len(streams),))]
    if piece is not None:
        operands += [in_vmem(tokens), in_hbm(key_weight)]
        in_specs += [VMEM, ANY]
        out_specs.append(VMEM)
        out_shape.append(jax.ShapeDtypeStruct((many, columns // 2), jnp.float32))
        scratch += [
            pltpu.VMEM((features, columns // 2), key_weight.dtype),
            pltpu.SemaphoreType.DMA,
        ]
    outs = pl.pallas_call(
        functools.partial(pick_kernel, step, size, lo, streams, held, piece),
        grid_spec=pltpu.PrefetchScalarGridSpec(
            num_scalar_prefetch=1,
            grid=(),
            in_specs=in_specs,
            out_specs=out_specs,
            scratch_shapes=scratch,
        ),
        out_shape=out_shape,
        compiler_params=pltpu.CompilerParams(vmem_limit_bytes=(2 if piece is None else 8) * MIB),
        name="pick",
    )(table, *operands)
    return outs[: len(streams)], outs[len(streams) :]


def dense_kernel(index, down, up, out):
    width = down.shape[2]
    out[:, :, :width] = down[...]
    out[:, :, width:] = up[...]


def dense(adapter_ids, owner_map, down_pool, up_pool):
    held, rank, width = down_pool.shape
    columns = up_pool.shape[2]
    slots = owner_map[adapter_ids] - lax.axis_index("dp") * held
    here = (slots >= 0) & (slots < held)
    index = jnp.sum(jnp.where(here, slots, 0), axis=1).astype(jnp.int32)
    many = index.shape[0]
    send = pl.pallas_call(
        dense_kernel,
        grid_spec=pltpu.PrefetchScalarGridSpec(
            num_scalar_prefetch=1,
            grid=(many,),
            in_specs=[
                pl.BlockSpec((1, rank, width), lambda j, index: (index[j], 0, 0)),
                pl.BlockSpec((1, rank, columns), lambda j, index: (index[j], 0, 0)),
            ],
            out_specs=pl.BlockSpec((1, rank, width + columns), lambda j, index: (j, 0, 0)),
        ),
        out_shape=jax.ShapeDtypeStruct((many, rank, width + columns), down_pool.dtype),
        name="pick_all",
    )(index, down_pool, up_pool)
    return lax.all_to_all(send, "dp", split_axis=0, concat_axis=0, tiled=True)


def request_of_rows(ends, count, first, rows):
    at = first + lax.broadcasted_iota(jnp.int32, (rows, 1), 0)
    which = jnp.zeros((rows, 1), jnp.int32)
    for r in range(count - 1):
        which += (at >= ends[r]).astype(jnp.int32)
    return which


def code_kernel(count, step, kinds, index, ends, tokens, *refs):
    n = sum(many for _, many in kinds)
    arrays, refs = refs[:n], refs[n:]
    out, up, down, total, block_sem = refs
    rank, columns = out.shape[1] // 2, up.shape[1]
    features = tokens.shape[1]
    chunks = features // step

    def load(r, kind, held):
        if kind == "pool":
            slot = index[r]
            parts = [(held[0].at[slot], held[1].at[slot])]
        elif kind == "several":
            block = held[0].at[index[r]]
            parts = [(block, block.at[:, pl.ds(features, columns)])]
        else:
            parts = [(ref, ref.at[:, pl.ds(features, columns)]) for ref in held]
        size = rank // len(parts)
        for p, (down_part, up_part) in enumerate(parts):
            mine = pl.ds(r * rank + p * size, size)
            for k in range(chunks):
                pltpu.make_async_copy(
                    down_part.at[:, pl.ds(k * step, step)], down.at[k, mine, :], block_sem.at[k]
                ).start()
            pltpu.make_async_copy(up_part, up.at[mine, :], block_sem.at[chunks]).start()

    for r in range(count):
        at, number = 0, 0
        for kind, many in kinds:
            held = arrays[at : at + many]
            at += many
            if kind == "several":
                load(r, kind, held)
            elif kind == "pool":
                number = held[0].shape[0]

                @pl.when(index[r] < number)
                def _(r=r, kind=kind, held=held):
                    load(r, kind, held)

            else:

                @pl.when(index[r] == number)
                def _(r=r, kind=kind, held=held):
                    load(r, kind, held)

                number += 1

    for k in range(chunks):
        pltpu.make_async_copy(down.at[k], down.at[k], block_sem.at[k]).wait()
        full = lax.dot_general(
            tokens[:, k * step : (k + 1) * step],
            down[k],
            (((1,), (1,)), ((), ())),
            preferred_element_type=jnp.float32,
        )
        if k:
            full = total[...] + full
        if k < chunks - 1:
            total[...] = full
    pltpu.make_async_copy(up, up, block_sem.at[chunks]).wait()
    which = request_of_rows(ends, count, 0, full.shape[0])
    code = full[:, :rank]
    for r in range(1, count):
        code = jnp.where(which == r, full[:, r * rank : (r + 1) * rank], code)
    half = full.shape[0] // 2
    out[...] = jnp.concatenate([code[:half], code[half:]], axis=1)


def codes(index, ends, tokens, sources, rank, columns):
    many, features = tokens.shape
    count = ends.shape[0]
    chunks = 4 if features % 512 == 0 else 1
    step = features // chunks
    kinds = [(kind, len(held)) for kind, held in sources]
    arrays = [array for _, held in sources for array in held]
    return pl.pallas_call(
        functools.partial(code_kernel, count, step, kinds),
        grid_spec=pltpu.PrefetchScalarGridSpec(
            num_scalar_prefetch=2,
            grid=(),
            in_specs=[VMEM] + [ANY] * len(arrays),
            out_specs=[VMEM, VMEM],
            scratch_shapes=[
                pltpu.VMEM((chunks, count * rank, step), tokens.dtype),
                pltpu.VMEM((many, count * rank), jnp.float32),
                pltpu.SemaphoreType.DMA((chunks + 1,)),
            ],
        ),
        out_shape=[
            jax.ShapeDtypeStruct((many // 2, 2 * rank), jnp.float32),
            jax.ShapeDtypeStruct((count * rank, columns), tokens.dtype),
        ],
        compiler_params=pltpu.CompilerParams(vmem_limit_bytes=16 * MIB),
        name="codes",
    )(index, ends, in_vmem(tokens), *arrays)


def finish_kernel(count, parts, shares, tile, ends, *refs):
    code_parts, base_parts = refs[:parts], refs[parts : parts + sum(shares)]
    up, out, hold, sem = refs[parts + sum(shares) :]
    rank = up.shape[0] // count
    code = code_parts[0][...]
    for p in range(1, parts):
        code = code + code_parts[p][...]
    half = code.shape[0]
    copies = []
    for i in range(out.shape[0] // tile):
        first = i * tile
        side, at = first // half, first % half
        mine = code[at : at + tile, side * rank : (side + 1) * rank]
        which = request_of_rows(ends, count, first, tile)
        zero = jnp.zeros_like(mine)
        wide = jnp.concatenate([jnp.where(which == r, mine, zero) for r in range(count)], axis=1)
        delta = None
        for _ in range(3):
            part = wide.astype(jnp.bfloat16)
            wide = wide - part.astype(jnp.float32)
            term = jnp.dot(part, up[...], preferred_element_type=jnp.float32)
            delta = term if delta is None else delta + term
        rows = pl.ds(first, tile)
        left, number = 0, 0
        for share in shares:
            base = base_parts[number][rows, :]
            for p in range(1, share):
                base = base + base_parts[number + p][rows, :]
            number += share
            right = left + base.shape[1]
            total = base + ADAPTER_SCALE * delta[:, left:right]
            hold[rows, left:right] = total.astype(hold.dtype)
            left = right
        copies.append(pltpu.make_async_copy(hold.at[rows, :], out.at[rows, :], sem.at[i]))
        copies[-1].start()
    for copy in copies:
        copy.wait()


def finish(ends, code_parts, base, up):
    many = base[0][0].shape[0]
    columns = up.shape[1]
    count = ends.shape[0]
    parts = len(code_parts)
    tile = min(256, many // 2)
    shares = [len(share) for share in base]
    return pl.pallas_call(
        functools.partial(finish_kernel, count, parts, shares, tile),
        grid_spec=pltpu.PrefetchScalarGridSpec(
            num_scalar_prefetch=1,
            grid=(),
            in_specs=[VMEM] * (parts + sum(shares) + 1),
            out_specs=ANY,
            scratch_shapes=[
                pltpu.VMEM((many, columns), jnp.bfloat16),
                pltpu.SemaphoreType.DMA((many // tile,)),
            ],
        ),
        out_shape=jax.ShapeDtypeStruct((many, columns), jnp.bfloat16),
        compiler_params=pltpu.CompilerParams(vmem_limit_bytes=24 * MIB),
        name="finish",
    )(ends, *code_parts, *[part for share in base for part in share], up)


def gathered(part, axis, size):
    held = [part]
    for step in range(1, size):
        held.append(lax.ppermute(part, axis, [(i, (i + step) % size) for i in range(size)]))
    return held


def route(table, down_pool, up_pool, n_dp, tokens, key_weight):
    rank = down_pool.shape[1]
    size = rank // 2
    half = up_pool.shape[2] // 2
    outer = [(i, i ^ 2) for i in range(n_dp)]
    middle = [(i, i + 2) for i in (2, 3)] + [(i, i - 2) for i in (4, 5)]
    over_x = [(i, i ^ 1) for i in range(n_dp)]
    got = [([], [], []), ([], [], [])]
    pieces = [(1, 0), (1, half), (0, 0), (0, half)]
    done = []
    for step in range(Z_STEPS):
        streams = [E_TABLE, O_TABLE] + ([X_TABLE] if step < X_STEPS else [])
        for part in range(2):
            known = [list(arrays) for arrays in got[part]]
            piece = pieces[step] if part == 1 and step < len(pieces) else None
            sends, product = pick(
                step, part * size, size, streams, table, down_pool, up_pool, known, piece,
                tokens, key_weight,
            )
            done += product
            for stream, send in zip(streams, sends):
                pairs = (outer, middle, over_x)[stream]
                got[part][stream].append(lax.ppermute(send, "dp", pairs))
    return got, done


def shards(sizes, tokens, key_weight, down_pool, up_pool, adapter_ids, lengths, owner_map):
    n_groups, n_dp, n_tensor = sizes
    held, rank, width = down_pool.shape
    columns = up_pool.shape[2]
    member = lax.axis_index("dp")
    me = lax.axis_index("tensor")
    ends = jnp.cumsum(lengths[0]).astype(jnp.int32)

    def sent_on(part, step):
        pairs = [(i, (i + step) % n_tensor) for i in range(n_tensor)]
        return lax.ppermute(part, "tensor", pairs)

    def by_all_to_all():
        blocks = dense(adapter_ids, owner_map, down_pool, up_pool)
        my_ids = lax.dynamic_index_in_dim(adapter_ids, member, 0, keepdims=False)
        index = owner_map[my_ids] // held
        return tuple(codes(index, ends, tokens, [("several", (blocks,))], rank, columns))

    if n_dp == 8 and n_tensor == 2 and rank % 32 == 0 and adapter_ids.shape[1] == 4:
        table = plan(held, adapter_ids, owner_map)
        got, done = route(table, down_pool, up_pool, n_dp, tokens, key_weight)
        base = [[here, sent_on(there, 1)] for there, here in zip(done[:2], done[2:])]
        misfit = table[0, MISFIT].reshape(1)
        for other in gathered(misfit, "groups", n_groups)[1:]:
            misfit = jnp.maximum(misfit, other)
        index = table[: adapter_ids.shape[1], PLACE]
        sources = [("pool", (in_hbm(down_pool), in_hbm(up_pool)))]
        for stream in (2, 0, 1):
            sources += [("block", pair) for pair in zip(got[0][stream], got[1][stream])]
        routed = tuple(codes(index, ends, tokens, sources, rank, columns))
        code, up = lax.cond(misfit[0] == 0, lambda: routed, by_all_to_all)
    else:
        parts = []
        for step in range(n_tensor):
            first = lax.rem(me + step, n_tensor) * columns
            weight = lax.dynamic_slice_in_dim(key_weight, first, columns, 1)
            part = jnp.dot(tokens, weight, preferred_element_type=jnp.float32)
            parts.append(sent_on(part, step) if step else part)
        base = [parts]
        code, up = by_all_to_all()
    code_parts = gathered(code, "tensor", n_tensor)
    return finish(ends, code_parts, base, up)


def solution(mesh):
    placed = (
        P(("groups", "dp"), "tensor"),
        P("tensor", None),
        P("dp", None, "tensor"),
        P("dp", None, "tensor"),
        P("groups", None),
        P(("groups", "dp"), None),
        P("groups"),
    )
    sizes = tuple(mesh.shape[name] for name in ("groups", "dp", "tensor"))
    return jax.shard_map(
        functools.partial(shards, sizes),
        mesh=mesh,
        in_specs=placed,
        out_specs=P(("groups", "dp"), "tensor"),
        check_vma=False,
    )
```

```python
import functools

import jax
import jax.numpy as jnp
from jax import lax
from jax.experimental import pallas as pl
from jax.experimental.pallas import tpu as pltpu
from jax.sharding import PartitionSpec as P

ADAPTER_SCALE = 2.0
MIB = 1 << 20
ANY = pl.BlockSpec(memory_space=pl.ANY)
VMEM = pl.BlockSpec(memory_space=pltpu.VMEM)


def in_vmem(x):
    return pltpu.with_memory_space_constraint(x, pltpu.VMEM)


def in_hbm(x):
    return pltpu.with_memory_space_constraint(x, pltpu.HBM)


X_STEPS = 4
Z_STEPS = 6
NEVER = 1000.0
E_TABLE, O_TABLE, X_TABLE, PLACE, MISFIT = range(5)


def plan_kernel(held, planes, req, ids, owner_map, out):
    n = planes * req
    member = lax.axis_index("dp")
    plane, column = member // 2, member % 2
    lane = lax.broadcasted_iota(jnp.int32, (n, 128), 1)
    sub = lax.broadcasted_iota(jnp.int32, (n, 128), 0)
    lane_f, sub_f = lane.astype(jnp.float32), sub.astype(jnp.float32)

    def row_of(at):
        return sum([(at >= q * req).astype(jnp.float32) for q in range(1, planes)])

    dest_i, dest_k = row_of(lane), row_of(sub)

    def entries(c):
        by_lane = [jnp.full((n, 128), -1.0, jnp.float32) for _ in range(5)]
        by_sub = [jnp.full((n, 128), -2.0, jnp.float32) for _ in range(5)]
        for i in range(n):
            slot = owner_map[ids[i % req, 2 * (i // req) + c]]
            owner = slot // held
            values = (slot, owner, owner // 2, owner % 2, slot - owner * held)
            for v, value in enumerate(values):
                value = value.astype(jnp.float32)
                by_lane[v] = jnp.where(lane == i, value, by_lane[v])
                by_sub[v] = jnp.where(sub == i, value, by_sub[v])
        return by_lane, by_sub

    def over_x(by_lane, by_sub, c):
        (slot_i, owner_i, src_i, col_i, _), (slot_k, owner_k, src_k, col_k, _) = by_lane, by_sub
        c = c.astype(jnp.float32)
        same = slot_i == slot_k
        key_i = jnp.where(col_i == c, -1.0, jnp.abs(dest_i - src_i) * n + (n - 1 - lane_f))
        key_k = jnp.where(col_k == c, -1.0, jnp.abs(dest_k - src_k) * n + (n - 1 - sub_f))
        best_i = jnp.max(jnp.where(same, key_k, -1.0), axis=0, keepdims=True)
        best_k = jnp.max(jnp.where(same, key_i, -1.0), axis=1, keepdims=True)
        ahead = (key_k == best_k) & (key_k >= 0) & (owner_k == owner_i) & (key_k > best_i)
        pos = jnp.sum(jnp.where(ahead, 1.0, 0.0), axis=0, keepdims=True)
        return pos, (key_i == best_i) & (key_i >= 0)

    row = lax.broadcasted_iota(jnp.int32, (8, 128), 0)
    lane8 = lax.broadcasted_iota(jnp.int32, (8, 128), 1).astype(jnp.float32)
    row_f = row.astype(jnp.float32)
    links = planes - 1
    up = row < links
    last = float(planes - 1)
    link = jnp.where(up, row_f, row_f - links)

    def top(x):
        return jnp.broadcast_to(x[0:1, :], (8, 128))

    def schedule(by_lane, by_sub, xpos, c):
        slot_i, _, src_i, col_i, _ = by_lane
        same = slot_i == by_sub[0]
        dest, src = top(dest_i), top(src_i)
        d_dest, d_src = jnp.where(up, dest, last - dest), jnp.where(up, src, last - src)

        def beyond(sign):
            more = same & ((dest_k - dest_i) * sign > 0)
            return top(jnp.max(jnp.where(more, 1.0, 0.0), axis=0, keepdims=True))

        farther = jnp.where(up, beyond(1.0), beyond(-1.0))
        valid = (row < 2 * links) & (lane8 < n)
        lead = valid & (farther == 0.0) & (d_dest > d_src)
        on = lead & (d_src <= link) & (d_dest > link)
        starts = d_src == link
        local = top(col_i) == c.astype(jnp.float32)
        first = jnp.where(local, 0.0, top(jnp.broadcast_to(xpos, (8, 128))) + 1)
        ready = jnp.where(starts, first, NEVER)
        pos = jnp.full((8, 128), NEVER, jnp.float32)
        for t in range(Z_STEPS):
            open_ = on & (ready <= t) & (pos >= NEVER)
            key = jnp.where(open_, d_dest * 128 + (127 - lane8), -1.0)
            chosen = open_ & (key == jnp.max(key, axis=1, keepdims=True))
            pos = jnp.where(chosen, float(t), pos)
            before = jnp.concatenate([pos[7:8, :], pos[0:7, :]], axis=0)
            ready = jnp.where(starts, first, before + 1)
        misfit = jnp.max(jnp.where(on & (pos >= NEVER), 1.0, 0.0), axis=1, keepdims=True)
        return same, dest, src, local, on, starts, pos, jnp.max(misfit, axis=0, keepdims=True)

    by_lane, by_sub = entries(column)
    within_i = by_lane[4]
    xpos, _ = over_x(by_lane, by_sub, column)
    same, dest, src, local, on, starts, pos, misfit = schedule(by_lane, by_sub, xpos, column)
    other_lane, other_sub = entries(1 - column)
    other_xpos, other_lead = over_x(other_lane, other_sub, 1 - column)
    other_misfit = schedule(other_lane, other_sub, other_xpos, 1 - column)[-1]
    misfit = jnp.maximum(misfit, other_misfit)

    from_x = float(held)
    from_e = from_x + X_STEPS
    from_o = from_e + Z_STEPS
    own = jnp.where(local, top(within_i), from_x + top(jnp.broadcast_to(xpos, (8, 128))))

    def table(hit, source):
        return jnp.sum(jnp.where(hit, source + 1, 0.0), axis=1, keepdims=True) - 1

    def only(which, x):
        return jnp.sum(jnp.where(row == which, x, 0.0), axis=0, keepdims=True)

    def sent(which, passing_from):
        hit = only(which, jnp.where(on, 1.0, 0.0)) == 1.0
        fresh = only(which, jnp.where(starts, 1.0, 0.0)) == 1.0
        at, earlier = only(which, pos), only(which - 1, pos)
        source = jnp.where(fresh, own, passing_from + earlier)
        return table(hit & (at == row_f), source)

    e_row = jnp.where(plane % 2 == 0, plane, links + (planes - 1 - plane))
    o_row = jnp.where(plane == 1, 1, jnp.where(plane == 2, links + 1, 7))
    e_table = sent(e_row, from_o)
    o_table = sent(o_row, from_e)
    (_, owner_o, _, _, within_o) = other_lane
    mine = top(owner_o) == member.astype(jnp.float32)
    other_lead8 = top(jnp.where(other_lead, 1.0, 0.0)) == 1.0
    other_xpos8 = top(jnp.broadcast_to(other_xpos, (8, 128)))
    x_table = table(mine & other_lead8 & (other_xpos8 == row_f), top(within_o))

    arrival = jnp.zeros((8, 128), jnp.float32)
    for which in range(2 * links):
        one = jnp.broadcast_to(pos[which : which + 1, :], (n, 128))
        one_on = jnp.broadcast_to(jnp.where(on, 1.0, 0.0)[which : which + 1, :], (n, 128))
        by_k = jnp.sum(jnp.where((lane == sub) & (one_on == 1.0), one + 1, 0.0), axis=1, keepdims=True)
        arrives = jnp.max(jnp.where(same, by_k, 0.0), axis=0, keepdims=True) - 1
        if which < links:
            hit = (dest > src) & (dest == which + 1)
        else:
            hit = (dest < src) & (last - dest == which - links + 1)
        arrival = jnp.where(hit, arrives, arrival)
    odd = dest - 2 * jnp.floor(dest * 0.5)
    outer = jnp.where(dest > src, odd, 1 - odd) == 1.0
    final = jnp.where(dest == src, own, jnp.where(outer, from_e, from_o) + arrival)
    my_rows = lane8 == (plane * req).astype(jnp.float32) + row_f
    place = jnp.sum(jnp.where(my_rows & (row < req), final, 0.0), axis=1, keepdims=True)
    place = jnp.where(misfit == 1.0, 0.0, place)
    result = jnp.zeros((8, 128), jnp.float32)
    for at, values in ((E_TABLE, e_table), (O_TABLE, o_table), (X_TABLE, x_table), (PLACE, place), (MISFIT, misfit)):
        result = jnp.where(lane8 == at, values, result)
    out[...] = result.astype(jnp.int32)


def plan(held, adapter_ids, owner_map):
    rows, req = adapter_ids.shape
    return pl.pallas_call(
        functools.partial(plan_kernel, held, rows // 2, req),
        grid_spec=pltpu.PrefetchScalarGridSpec(
            num_scalar_prefetch=2, grid=(), in_specs=[], out_specs=VMEM
        ),
        out_shape=jax.ShapeDtypeStruct((8, 128), jnp.int32),
        compiler_params=pltpu.CompilerParams(vmem_limit_bytes=4 * MIB),
        name="plan",
    )(adapter_ids.T, owner_map)


def pick_kernel(step, size, lo, streams, held, piece, table, down, up, *refs):
    at = 0
    got = []
    for many in held:
        got.append(refs[at : at + many])
        at += many
    refs = list(refs[at:])
    if piece is not None:
        tokens, weight = refs.pop(0), refs.pop(0)
        held_weight, weight_sem = refs.pop(-2), refs.pop(-1)
        distance, shift = piece
        columns, wide = up.shape[2], held_weight.shape[1]
        to = lax.rem(lax.axis_index("tensor") + distance, 2)
        first = pl.multiple_of(to * columns + shift, 128)
        depth = held_weight.shape[0] // 4
        loads = []
        for k in range(4):
            some = pl.ds(k * depth, depth)
            loads.append(
                pltpu.make_async_copy(
                    weight.at[some, pl.ds(first, wide)], held_weight.at[some, :], weight_sem.at[k]
                )
            )
            loads[-1].start()
    outs, sem = refs[: len(streams)], refs[-1]
    slots, _, width = down.shape
    from_x, from_e, from_o = slots, slots + X_STEPS, slots + X_STEPS + Z_STEPS
    over_x = [(from_x + t, ref) for t, ref in enumerate(got[2])]
    outer = [(from_e + t, ref) for t, ref in enumerate(got[0])]
    middle = [(from_o + t, ref) for t, ref in enumerate(got[1])]
    sources = {E_TABLE: over_x + middle, O_TABLE: over_x + outer, X_TABLE: []}
    rows = pl.ds(lo, size)
    for i, stream in enumerate(streams):
        code, out = table[step, stream], outs[i]

        @pl.when((code >= 0) & (code < slots))
        def _(code=code, out=out, i=i):
            pltpu.make_async_copy(
                down.at[code, rows, :], out.at[:, pl.ds(0, width)], sem.at[i]
            ).start()
            pltpu.make_async_copy(
                up.at[code, rows, :], out.at[:, pl.ds(width, up.shape[2])], sem.at[i]
            ).start()

        for number, ref in sources[stream]:

            @pl.when(code == number)
            def _(ref=ref, out=out, i=i):
                pltpu.make_async_copy(ref, out, sem.at[i]).start()

    if piece is not None:
        product = refs[len(streams)]
        for k in range(4):
            loads[k].wait()
            some = slice(k * depth, (k + 1) * depth)
            part = jnp.dot(
                tokens[:, some], held_weight[some, :], preferred_element_type=jnp.float32
            )
            product[...] = part if k == 0 else product[...] + part

    for i, stream in enumerate(streams):

        @pl.when(table[step, stream] >= 0)
        def _(i=i):
            pltpu.make_async_copy(outs[i], outs[i], sem.at[i]).wait()


def pick(step, lo, size, streams, table, down_pool, up_pool, got, piece, tokens, key_weight):
    many, features = tokens.shape
    columns = up_pool.shape[2]
    wide = down_pool.shape[2] + columns
    held = [len(arrays) for arrays in got]
    operands = [in_hbm(down_pool), in_hbm(up_pool)] + [a for arrays in got for a in arrays]
    in_specs = [ANY] * len(operands)
    out_specs = [ANY] * len(streams)
    out_shape = [pltpu.VMEM((size, wide), down_pool.dtype)] * len(streams)
    scratch = [pltpu.SemaphoreType.DMA((len(streams),))]
    if piece is not None:
        operands += [in_vmem(tokens), in_hbm(key_weight)]
        in_specs += [VMEM, ANY]
        out_specs.append(VMEM)
        out_shape.append(jax.ShapeDtypeStruct((many, columns // 2), jnp.float32))
        scratch += [
            pltpu.VMEM((features, columns // 2), key_weight.dtype),
            pltpu.SemaphoreType.DMA((4,)),
        ]
    outs = pl.pallas_call(
        functools.partial(pick_kernel, step, size, lo, streams, held, piece),
        grid_spec=pltpu.PrefetchScalarGridSpec(
            num_scalar_prefetch=1,
            grid=(),
            in_specs=in_specs,
            out_specs=out_specs,
            scratch_shapes=scratch,
        ),
        out_shape=out_shape,
        compiler_params=pltpu.CompilerParams(vmem_limit_bytes=(2 if piece is None else 8) * MIB),
        name="pick",
    )(table, *operands)
    return outs[: len(streams)], outs[len(streams) :]


def dense_kernel(index, down, up, out):
    width = down.shape[2]
    out[:, :, :width] = down[...]
    out[:, :, width:] = up[...]


def dense(adapter_ids, owner_map, down_pool, up_pool):
    held, rank, width = down_pool.shape
    columns = up_pool.shape[2]
    slots = owner_map[adapter_ids] - lax.axis_index("dp") * held
    here = (slots >= 0) & (slots < held)
    index = jnp.sum(jnp.where(here, slots, 0), axis=1).astype(jnp.int32)
    many = index.shape[0]
    send = pl.pallas_call(
        dense_kernel,
        grid_spec=pltpu.PrefetchScalarGridSpec(
            num_scalar_prefetch=1,
            grid=(many,),
            in_specs=[
                pl.BlockSpec((1, rank, width), lambda j, index: (index[j], 0, 0)),
                pl.BlockSpec((1, rank, columns), lambda j, index: (index[j], 0, 0)),
            ],
            out_specs=pl.BlockSpec((1, rank, width + columns), lambda j, index: (j, 0, 0)),
        ),
        out_shape=jax.ShapeDtypeStruct((many, rank, width + columns), down_pool.dtype),
        name="pick_all",
    )(index, down_pool, up_pool)
    return lax.all_to_all(send, "dp", split_axis=0, concat_axis=0, tiled=True)


def request_of_rows(lengths, count, first, rows):
    at = first + lax.broadcasted_iota(jnp.int32, (rows, 1), 0)
    which = jnp.zeros((rows, 1), jnp.int32)
    end = 0
    for r in range(count - 1):
        end = end + lengths[0, r]
        which += (at >= end).astype(jnp.int32)
    return which


def code_kernel(count, step, kinds, routed, index, others, lengths, tokens, *refs):
    n = sum(many for _, many in kinds)
    arrays, refs = refs[:n], refs[n:]
    out, up, flag, down, total, block_sem = refs
    flag[0] = 0
    if routed:
        flag[0] = jnp.maximum(index[0, MISFIT], others[0, MISFIT])

    def source(r):
        return index[r, PLACE] if routed else index[r, 0]

    rank, columns = out.shape[1] // 2, up.shape[1]
    features = tokens.shape[1]
    chunks = features // step

    def load(r, kind, held):
        if kind == "pool":
            slot = source(r)
            parts = [(held[0].at[slot], held[1].at[slot])]
        elif kind == "several":
            block = held[0].at[source(r)]
            parts = [(block, block.at[:, pl.ds(features, columns)])]
        else:
            parts = [(ref, ref.at[:, pl.ds(features, columns)]) for ref in held]
        size = rank // len(parts)
        for p, (down_part, up_part) in enumerate(parts):
            mine = pl.ds(r * rank + p * size, size)
            for k in range(chunks):
                pltpu.make_async_copy(
                    down_part.at[:, pl.ds(k * step, step)], down.at[k, mine, :], block_sem.at[k]
                ).start()
            pltpu.make_async_copy(up_part, up.at[mine, :], block_sem.at[chunks]).start()

    for r in range(count):
        at, number = 0, 0
        for kind, many in kinds:
            held = arrays[at : at + many]
            at += many
            if kind == "several":
                load(r, kind, held)
            elif kind == "pool":
                number = held[0].shape[0]

                @pl.when(source(r) < number)
                def _(r=r, kind=kind, held=held):
                    load(r, kind, held)

            else:

                @pl.when(source(r) == number)
                def _(r=r, kind=kind, held=held):
                    load(r, kind, held)

                number += 1

    for k in range(chunks):
        pltpu.make_async_copy(down.at[k], down.at[k], block_sem.at[k]).wait()
        full = lax.dot_general(
            tokens[:, k * step : (k + 1) * step],
            down[k],
            (((1,), (1,)), ((), ())),
            preferred_element_type=jnp.float32,
        )
        if k:
            full = total[...] + full
        if k < chunks - 1:
            total[...] = full
    pltpu.make_async_copy(up, up, block_sem.at[chunks]).wait()
    which = request_of_rows(lengths, count, 0, full.shape[0])
    code = full[:, :rank]
    for r in range(1, count):
        code = jnp.where(which == r, full[:, r * rank : (r + 1) * rank], code)
    half = full.shape[0] // 2
    out[...] = jnp.concatenate([code[:half], code[half:]], axis=1)


def codes(index, others, lengths, tokens, sources, rank, columns):
    many, features = tokens.shape
    count = lengths.shape[1]
    routed = others is not None
    chunks = 4 if features % 512 == 0 else 1
    step = features // chunks
    kinds = [(kind, len(held)) for kind, held in sources]
    arrays = [array for _, held in sources for array in held]
    return pl.pallas_call(
        functools.partial(code_kernel, count, step, kinds, routed),
        grid_spec=pltpu.PrefetchScalarGridSpec(
            num_scalar_prefetch=3,
            grid=(),
            in_specs=[VMEM] + [ANY] * len(arrays),
            out_specs=[VMEM, VMEM, pl.BlockSpec(memory_space=pltpu.SMEM)],
            scratch_shapes=[
                pltpu.VMEM((chunks, count * rank, step), tokens.dtype),
                pltpu.VMEM((many, count * rank), jnp.float32),
                pltpu.SemaphoreType.DMA((chunks + 1,)),
            ],
        ),
        out_shape=[
            jax.ShapeDtypeStruct((many // 2, 2 * rank), jnp.float32),
            jax.ShapeDtypeStruct((count * rank, columns), tokens.dtype),
            jax.ShapeDtypeStruct((1,), jnp.int32),
        ],
        compiler_params=pltpu.CompilerParams(vmem_limit_bytes=16 * MIB),
        name="codes",
    )(index, others if routed else index, lengths, in_vmem(tokens), *arrays)


def finish_kernel(count, parts, shares, tile, lengths, *refs):
    code_parts, base_parts = refs[:parts], refs[parts : parts + sum(shares)]
    up, out, hold, sem = refs[parts + sum(shares) :]
    rank = up.shape[0] // count
    code = code_parts[0][...]
    for p in range(1, parts):
        code = code + code_parts[p][...]
    half = code.shape[0]
    copies = []
    for i in range(out.shape[0] // tile):
        first = i * tile
        side, at = first // half, first % half
        mine = code[at : at + tile, side * rank : (side + 1) * rank]
        which = request_of_rows(lengths, count, first, tile)
        zero = jnp.zeros_like(mine)
        wide = jnp.concatenate([jnp.where(which == r, mine, zero) for r in range(count)], axis=1)
        delta = None
        for _ in range(3):
            part = wide.astype(jnp.bfloat16)
            wide = wide - part.astype(jnp.float32)
            term = jnp.dot(part, up[...], preferred_element_type=jnp.float32)
            delta = term if delta is None else delta + term
        rows = pl.ds(first, tile)
        left, number = 0, 0
        for share in shares:
            base = base_parts[number][rows, :]
            for p in range(1, share):
                base = base + base_parts[number + p][rows, :]
            number += share
            right = left + base.shape[1]
            total = base + ADAPTER_SCALE * delta[:, left:right]
            hold[rows, left:right] = total.astype(hold.dtype)
            left = right
        copies.append(pltpu.make_async_copy(hold.at[rows, :], out.at[rows, :], sem.at[i]))
        copies[-1].start()
    for copy in copies:
        copy.wait()


def finish(lengths, code_parts, base, up):
    many = base[0][0].shape[0]
    columns = up.shape[1]
    count = lengths.shape[1]
    parts = len(code_parts)
    tile = min(256, many // 2)
    shares = [len(share) for share in base]
    return pl.pallas_call(
        functools.partial(finish_kernel, count, parts, shares, tile),
        grid_spec=pltpu.PrefetchScalarGridSpec(
            num_scalar_prefetch=1,
            grid=(),
            in_specs=[VMEM] * (parts + sum(shares) + 1),
            out_specs=ANY,
            scratch_shapes=[
                pltpu.VMEM((many, columns), jnp.bfloat16),
                pltpu.SemaphoreType.DMA((many // tile,)),
            ],
        ),
        out_shape=jax.ShapeDtypeStruct((many, columns), jnp.bfloat16),
        compiler_params=pltpu.CompilerParams(vmem_limit_bytes=24 * MIB),
        name="finish",
    )(lengths, *code_parts, *[part for share in base for part in share], up)


def gathered(part, axis, size):
    held = [part]
    for step in range(1, size):
        held.append(lax.ppermute(part, axis, [(i, (i + step) % size) for i in range(size)]))
    return held


def route(table, down_pool, up_pool, n_dp, tokens, key_weight):
    rank = down_pool.shape[1]
    size = rank // 2
    half = up_pool.shape[2] // 2
    outer = [(i, i ^ 2) for i in range(n_dp)]
    middle = [(i, i + 2) for i in (2, 3)] + [(i, i - 2) for i in (4, 5)]
    over_x = [(i, i ^ 1) for i in range(n_dp)]
    got = [([], [], []), ([], [], [])]
    pieces = [(1, 0), (1, half), (0, 0), (0, half)]
    done = []
    for step in range(Z_STEPS):
        streams = [E_TABLE, O_TABLE] + ([X_TABLE] if step < X_STEPS else [])
        for part in range(2):
            known = [list(arrays) for arrays in got[part]]
            piece = pieces[step - 1] if part == 1 and 1 <= step <= len(pieces) else None
            sends, product = pick(
                step, part * size, size, streams, table, down_pool, up_pool, known, piece,
                tokens, key_weight,
            )
            done += product
            for stream, send in zip(streams, sends):
                pairs = (outer, middle, over_x)[stream]
                got[part][stream].append(lax.ppermute(send, "dp", pairs))
    return got, done


def shards(sizes, tokens, key_weight, down_pool, up_pool, adapter_ids, lengths, owner_map):
    n_groups, n_dp, n_tensor = sizes
    held, rank, width = down_pool.shape
    columns = up_pool.shape[2]
    member = lax.axis_index("dp")
    me = lax.axis_index("tensor")

    def sent_on(part, step):
        pairs = [(i, (i + step) % n_tensor) for i in range(n_tensor)]
        return lax.ppermute(part, "tensor", pairs)

    def by_all_to_all():
        blocks = dense(adapter_ids, owner_map, down_pool, up_pool)
        my_ids = lax.dynamic_index_in_dim(adapter_ids, member, 0, keepdims=False)
        index = (owner_map[my_ids] // held)[:, None]
        code, up, _ = codes(index, None, lengths, tokens, [("several", (blocks,))], rank, columns)
        return code, up

    if n_dp == 8 and n_tensor == 2 and rank % 32 == 0 and adapter_ids.shape[1] == 4:
        table = plan(held, adapter_ids, owner_map)
        got, done = route(table, down_pool, up_pool, n_dp, tokens, key_weight)
        base = [[here, sent_on(there, 1)] for there, here in zip(done[:2], done[2:])]
        others = table
        for other in gathered(table, "groups", n_groups)[1:]:
            others = other if n_groups == 2 else jnp.maximum(others, other)
        sources = [("pool", (in_hbm(down_pool), in_hbm(up_pool)))]
        for stream in (2, 0, 1):
            sources += [("block", pair) for pair in zip(got[0][stream], got[1][stream])]
        code, up, misfit = codes(table, others, lengths, tokens, sources, rank, columns)
        code, up = lax.cond(misfit[0] == 0, lambda: (code, up), by_all_to_all)
    else:
        parts = []
        for step in range(n_tensor):
            first = lax.rem(me + step, n_tensor) * columns
            weight = lax.dynamic_slice_in_dim(key_weight, first, columns, 1)
            part = jnp.dot(tokens, weight, preferred_element_type=jnp.float32)
            parts.append(sent_on(part, step) if step else part)
        base = [parts]
        code, up = by_all_to_all()
    code_parts = gathered(code, "tensor", n_tensor)
    return finish(lengths, code_parts, base, up)


def solution(mesh):
    placed = (
        P(("groups", "dp"), "tensor"),
        P("tensor", None),
        P("dp", None, "tensor"),
        P("dp", None, "tensor"),
        P("groups", None),
        P(("groups", "dp"), None),
        P("groups"),
    )
    sizes = tuple(mesh.shape[name] for name in ("groups", "dp", "tensor"))
    return jax.shard_map(
        functools.partial(shards, sizes),
        mesh=mesh,
        in_specs=placed,
        out_specs=P(("groups", "dp"), "tensor"),
        check_vma=False,
    )
```

```python
import functools

import jax
import jax.numpy as jnp
from jax import lax
from jax.experimental import pallas as pl
from jax.experimental.pallas import tpu as pltpu
from jax.sharding import PartitionSpec as P

ADAPTER_SCALE = 2.0
MIB = 1 << 20
ANY = pl.BlockSpec(memory_space=pl.ANY)
VMEM = pl.BlockSpec(memory_space=pltpu.VMEM)


def in_vmem(x):
    return pltpu.with_memory_space_constraint(x, pltpu.VMEM)


def in_hbm(x):
    return pltpu.with_memory_space_constraint(x, pltpu.HBM)


X_STEPS = 4
Z_STEPS = 6
NEVER = 1000.0
E_TABLE, O_TABLE, X_TABLE, PLACE, MISFIT = range(5)


def plan_kernel(held, planes, req, ids, owner_map, out):
    n = planes * req
    member = lax.axis_index("dp")
    plane, column = member // 2, member % 2
    lane = lax.broadcasted_iota(jnp.int32, (n, 128), 1)
    sub = lax.broadcasted_iota(jnp.int32, (n, 128), 0)
    lane_f, sub_f = lane.astype(jnp.float32), sub.astype(jnp.float32)

    def row_of(at):
        return sum([(at >= q * req).astype(jnp.float32) for q in range(1, planes)])

    dest_i, dest_k = row_of(lane), row_of(sub)

    def entries(c):
        by_lane = [jnp.full((n, 128), -1.0, jnp.float32) for _ in range(5)]
        by_sub = [jnp.full((n, 128), -2.0, jnp.float32) for _ in range(5)]
        for i in range(n):
            slot = owner_map[ids[i % req, 2 * (i // req) + c]]
            owner = slot // held
            values = (slot, owner, owner // 2, owner % 2, slot - owner * held)
            for v, value in enumerate(values):
                value = value.astype(jnp.float32)
                by_lane[v] = jnp.where(lane == i, value, by_lane[v])
                by_sub[v] = jnp.where(sub == i, value, by_sub[v])
        return by_lane, by_sub

    def over_x(by_lane, by_sub, c):
        (slot_i, owner_i, src_i, col_i, _), (slot_k, owner_k, src_k, col_k, _) = by_lane, by_sub
        c = c.astype(jnp.float32)
        same = slot_i == slot_k
        key_i = jnp.where(col_i == c, -1.0, jnp.abs(dest_i - src_i) * n + (n - 1 - lane_f))
        key_k = jnp.where(col_k == c, -1.0, jnp.abs(dest_k - src_k) * n + (n - 1 - sub_f))
        best_i = jnp.max(jnp.where(same, key_k, -1.0), axis=0, keepdims=True)
        best_k = jnp.max(jnp.where(same, key_i, -1.0), axis=1, keepdims=True)
        ahead = (key_k == best_k) & (key_k >= 0) & (owner_k == owner_i) & (key_k > best_i)
        pos = jnp.sum(jnp.where(ahead, 1.0, 0.0), axis=0, keepdims=True)
        return pos, (key_i == best_i) & (key_i >= 0)

    row = lax.broadcasted_iota(jnp.int32, (8, 128), 0)
    lane8 = lax.broadcasted_iota(jnp.int32, (8, 128), 1).astype(jnp.float32)
    row_f = row.astype(jnp.float32)
    links = planes - 1
    up = row < links
    last = float(planes - 1)
    link = jnp.where(up, row_f, row_f - links)

    def top(x):
        return jnp.broadcast_to(x[0:1, :], (8, 128))

    def schedule(by_lane, by_sub, xpos, c):
        slot_i, _, src_i, col_i, _ = by_lane
        same = slot_i == by_sub[0]
        dest, src = top(dest_i), top(src_i)
        d_dest, d_src = jnp.where(up, dest, last - dest), jnp.where(up, src, last - src)

        def beyond(sign):
            more = same & ((dest_k - dest_i) * sign > 0)
            return top(jnp.max(jnp.where(more, 1.0, 0.0), axis=0, keepdims=True))

        farther = jnp.where(up, beyond(1.0), beyond(-1.0))
        valid = (row < 2 * links) & (lane8 < n)
        lead = valid & (farther == 0.0) & (d_dest > d_src)
        on = lead & (d_src <= link) & (d_dest > link)
        starts = d_src == link
        local = top(col_i) == c.astype(jnp.float32)
        first = jnp.where(local, 0.0, top(jnp.broadcast_to(xpos, (8, 128))) + 1)
        ready = jnp.where(starts, first, NEVER)
        pos = jnp.full((8, 128), NEVER, jnp.float32)
        for t in range(Z_STEPS):
            open_ = on & (ready <= t) & (pos >= NEVER)
            key = jnp.where(open_, d_dest * 128 + (127 - lane8), -1.0)
            chosen = open_ & (key == jnp.max(key, axis=1, keepdims=True))
            pos = jnp.where(chosen, float(t), pos)
            before = jnp.concatenate([pos[7:8, :], pos[0:7, :]], axis=0)
            ready = jnp.where(starts, first, before + 1)
        misfit = jnp.max(jnp.where(on & (pos >= NEVER), 1.0, 0.0), axis=1, keepdims=True)
        return same, dest, src, local, on, starts, pos, jnp.max(misfit, axis=0, keepdims=True)

    by_lane, by_sub = entries(column)
    within_i = by_lane[4]
    xpos, _ = over_x(by_lane, by_sub, column)
    same, dest, src, local, on, starts, pos, misfit = schedule(by_lane, by_sub, xpos, column)
    other_lane, other_sub = entries(1 - column)
    other_xpos, other_lead = over_x(other_lane, other_sub, 1 - column)
    other_misfit = schedule(other_lane, other_sub, other_xpos, 1 - column)[-1]
    misfit = jnp.maximum(misfit, other_misfit)

    from_x = float(held)
    from_e = from_x + X_STEPS
    from_o = from_e + Z_STEPS
    own = jnp.where(local, top(within_i), from_x + top(jnp.broadcast_to(xpos, (8, 128))))

    def table(hit, source):
        return jnp.sum(jnp.where(hit, source + 1, 0.0), axis=1, keepdims=True) - 1

    def only(which, x):
        return jnp.sum(jnp.where(row == which, x, 0.0), axis=0, keepdims=True)

    def sent(which, passing_from):
        hit = only(which, jnp.where(on, 1.0, 0.0)) == 1.0
        fresh = only(which, jnp.where(starts, 1.0, 0.0)) == 1.0
        at, earlier = only(which, pos), only(which - 1, pos)
        source = jnp.where(fresh, own, passing_from + earlier)
        return table(hit & (at == row_f), source)

    e_row = jnp.where(plane % 2 == 0, plane, links + (planes - 1 - plane))
    o_row = jnp.where(plane == 1, 1, jnp.where(plane == 2, links + 1, 7))
    e_table = sent(e_row, from_o)
    o_table = sent(o_row, from_e)
    (_, owner_o, _, _, within_o) = other_lane
    mine = top(owner_o) == member.astype(jnp.float32)
    other_lead8 = top(jnp.where(other_lead, 1.0, 0.0)) == 1.0
    other_xpos8 = top(jnp.broadcast_to(other_xpos, (8, 128)))
    x_table = table(mine & other_lead8 & (other_xpos8 == row_f), top(within_o))

    arrival = jnp.zeros((8, 128), jnp.float32)
    for which in range(2 * links):
        one = jnp.broadcast_to(pos[which : which + 1, :], (n, 128))
        one_on = jnp.broadcast_to(jnp.where(on, 1.0, 0.0)[which : which + 1, :], (n, 128))
        by_k = jnp.sum(jnp.where((lane == sub) & (one_on == 1.0), one + 1, 0.0), axis=1, keepdims=True)
        arrives = jnp.max(jnp.where(same, by_k, 0.0), axis=0, keepdims=True) - 1
        if which < links:
            hit = (dest > src) & (dest == which + 1)
        else:
            hit = (dest < src) & (last - dest == which - links + 1)
        arrival = jnp.where(hit, arrives, arrival)
    odd = dest - 2 * jnp.floor(dest * 0.5)
    outer = jnp.where(dest > src, odd, 1 - odd) == 1.0
    final = jnp.where(dest == src, own, jnp.where(outer, from_e, from_o) + arrival)
    my_rows = lane8 == (plane * req).astype(jnp.float32) + row_f
    place = jnp.sum(jnp.where(my_rows & (row < req), final, 0.0), axis=1, keepdims=True)
    place = jnp.where(misfit == 1.0, 0.0, place)
    result = jnp.zeros((8, 128), jnp.float32)
    for at, values in ((E_TABLE, e_table), (O_TABLE, o_table), (X_TABLE, x_table), (PLACE, place), (MISFIT, misfit)):
        result = jnp.where(lane8 == at, values, result)
    out[...] = result.astype(jnp.int32)


def plan(held, adapter_ids, owner_map):
    rows, req = adapter_ids.shape
    return pl.pallas_call(
        functools.partial(plan_kernel, held, rows // 2, req),
        grid_spec=pltpu.PrefetchScalarGridSpec(
            num_scalar_prefetch=2, grid=(), in_specs=[], out_specs=VMEM
        ),
        out_shape=jax.ShapeDtypeStruct((8, 128), jnp.int32),
        compiler_params=pltpu.CompilerParams(vmem_limit_bytes=4 * MIB),
        name="plan",
    )(adapter_ids.T, owner_map)


def pick_kernel(step, size, lo, streams, held, piece, table, down, up, *refs):
    at = 0
    got = []
    for many in held:
        got.append(refs[at : at + many])
        at += many
    refs = list(refs[at:])
    if piece is not None:
        tokens, weight = refs.pop(0), refs.pop(0)
        held_weight, weight_sem = refs.pop(-2), refs.pop(-1)
        distance, shift = piece
        columns, wide = up.shape[2], held_weight.shape[1]
        to = lax.rem(lax.axis_index("tensor") + distance, 2)
        first = pl.multiple_of(to * columns + shift, 128)
        load = pltpu.make_async_copy(weight.at[:, pl.ds(first, wide)], held_weight, weight_sem)
        load.start()
    outs, sem = refs[: len(streams)], refs[-1]
    slots, _, width = down.shape
    from_x, from_e, from_o = slots, slots + X_STEPS, slots + X_STEPS + Z_STEPS
    over_x = [(from_x + t, ref) for t, ref in enumerate(got[2])]
    outer = [(from_e + t, ref) for t, ref in enumerate(got[0])]
    middle = [(from_o + t, ref) for t, ref in enumerate(got[1])]
    sources = {E_TABLE: over_x + middle, O_TABLE: over_x + outer, X_TABLE: []}
    rows = pl.ds(lo, size)
    for i, stream in enumerate(streams):
        code, out = table[step, stream], outs[i]

        @pl.when((code >= 0) & (code < slots))
        def _(code=code, out=out, i=i):
            pltpu.make_async_copy(
                down.at[code, rows, :], out.at[:, pl.ds(0, width)], sem.at[i]
            ).start()
            pltpu.make_async_copy(
                up.at[code, rows, :], out.at[:, pl.ds(width, up.shape[2])], sem.at[i]
            ).start()

        for number, ref in sources[stream]:

            @pl.when(code == number)
            def _(ref=ref, out=out, i=i):
                pltpu.make_async_copy(ref, out, sem.at[i]).start()

    if piece is not None:
        load.wait()
        product = refs[len(streams)]
        tile = min(256, product.shape[0])
        for at in range(0, product.shape[0], tile):
            product[at : at + tile, :] = jnp.dot(
                tokens[at : at + tile, :],
                held_weight[...],
                preferred_element_type=jnp.float32,
            )

    for i, stream in enumerate(streams):

        @pl.when(table[step, stream] >= 0)
        def _(i=i):
            pltpu.make_async_copy(outs[i], outs[i], sem.at[i]).wait()


def pick(step, lo, size, streams, table, down_pool, up_pool, got, piece, tokens, key_weight):
    many = tokens.shape[0]
    columns = up_pool.shape[2]
    wide = down_pool.shape[2] + columns
    held = [len(arrays) for arrays in got]
    operands = [in_hbm(down_pool), in_hbm(up_pool)] + [a for arrays in got for a in arrays]
    in_specs = [ANY] * len(operands)
    out_specs = [ANY] * len(streams)
    out_shape = [pltpu.VMEM((size, wide), down_pool.dtype)] * len(streams)
    scratch = [pltpu.SemaphoreType.DMA((len(streams),))]
    if piece is not None:
        operands += [in_vmem(tokens), in_hbm(key_weight)]
        in_specs += [VMEM, ANY]
        out_specs.append(VMEM)
        out_shape.append(jax.ShapeDtypeStruct((many, columns // 2), jnp.float32))
        scratch += [
            pltpu.VMEM((tokens.shape[1], columns // 2), key_weight.dtype),
            pltpu.SemaphoreType.DMA,
        ]
    outs = pl.pallas_call(
        functools.partial(pick_kernel, step, size, lo, streams, held, piece),
        grid_spec=pltpu.PrefetchScalarGridSpec(
            num_scalar_prefetch=1,
            grid=(),
            in_specs=in_specs,
            out_specs=out_specs,
            scratch_shapes=scratch,
        ),
        out_shape=out_shape,
        compiler_params=pltpu.CompilerParams(vmem_limit_bytes=(4 if piece is None else 16) * MIB),
        name="pick",
    )(table, *operands)
    return outs[: len(streams)], outs[len(streams) :]


def dense_kernel(index, down, up, out):
    width = down.shape[2]
    out[:, :, :width] = down[...]
    out[:, :, width:] = up[...]


def dense(adapter_ids, owner_map, down_pool, up_pool):
    held, rank, width = down_pool.shape
    columns = up_pool.shape[2]
    slots = owner_map[adapter_ids] - lax.axis_index("dp") * held
    here = (slots >= 0) & (slots < held)
    index = jnp.sum(jnp.where(here, slots, 0), axis=1).astype(jnp.int32)
    many = index.shape[0]
    send = pl.pallas_call(
        dense_kernel,
        grid_spec=pltpu.PrefetchScalarGridSpec(
            num_scalar_prefetch=1,
            grid=(many,),
            in_specs=[
                pl.BlockSpec((1, rank, width), lambda j, index: (index[j], 0, 0)),
                pl.BlockSpec((1, rank, columns), lambda j, index: (index[j], 0, 0)),
            ],
            out_specs=pl.BlockSpec((1, rank, width + columns), lambda j, index: (j, 0, 0)),
        ),
        out_shape=jax.ShapeDtypeStruct((many, rank, width + columns), down_pool.dtype),
        name="pick_all",
    )(index, in_hbm(down_pool), in_hbm(up_pool))
    return lax.all_to_all(send, "dp", split_axis=0, concat_axis=0, tiled=True)


def request_of_rows(lengths, count, first, rows):
    at = first + lax.broadcasted_iota(jnp.int32, (rows, 1), 0)
    which = jnp.zeros((rows, 1), jnp.int32)
    end = 0
    for r in range(count - 1):
        end = end + lengths[0, r]
        which += (at >= end).astype(jnp.int32)
    return which


def code_kernel(count, kinds, routed, index, others, lengths, tokens, *refs):
    n = sum(many for _, many in kinds)
    arrays, refs = refs[:n], refs[n:]
    out, up, flag, down, sem, up_sem = refs
    rank, columns = out.shape[1] // 2, up.shape[1]
    features = tokens.shape[1]
    flag[0] = 0
    if routed:
        flag[0] = jnp.maximum(index[0, MISFIT], others[0, MISFIT])

    def source(r):
        return index[r, PLACE] if routed else index[r, 0]

    def load(r, kind, held):
        if kind == "pool":
            slot = source(r)
            parts = [(held[0].at[slot], held[1].at[slot])]
        elif kind == "several":
            block = held[0].at[source(r)]
            parts = [(block.at[:, pl.ds(0, features)], block.at[:, pl.ds(features, columns)])]
        else:
            parts = [
                (ref.at[:, pl.ds(0, features)], ref.at[:, pl.ds(features, columns)])
                for ref in held
            ]
        size = rank // len(parts)
        for p, (down_part, up_part) in enumerate(parts):
            mine = pl.ds(r * rank + p * size, size)
            pltpu.make_async_copy(down_part, down.at[mine, :], sem).start()
            pltpu.make_async_copy(up_part, up.at[mine, :], up_sem).start()

    for r in range(count):
        at, number = 0, 0
        for kind, many in kinds:
            held = arrays[at : at + many]
            at += many
            if kind == "several":
                load(r, kind, held)
            elif kind == "pool":
                number = held[0].shape[0]

                @pl.when(source(r) < number)
                def _(r=r, kind=kind, held=held):
                    load(r, kind, held)

            else:

                @pl.when(source(r) == number)
                def _(r=r, kind=kind, held=held):
                    load(r, kind, held)

                number += 1

    pltpu.make_async_copy(down, down, sem).wait()
    half = out.shape[0]
    tile = min(256, half)
    for i in range(half // tile):
        parts = []
        for side in range(2):
            first = side * half + i * tile
            full = lax.dot_general(
                tokens[first : first + tile, :],
                down[...],
                (((1,), (1,)), ((), ())),
                preferred_element_type=jnp.float32,
            )
            which = request_of_rows(lengths, count, first, tile)
            code = full[:, :rank]
            for r in range(1, count):
                code = jnp.where(which == r, full[:, r * rank : (r + 1) * rank], code)
            parts.append(code)
        out[i * tile : (i + 1) * tile, :] = jnp.concatenate(parts, axis=1)
    pltpu.make_async_copy(up, up, up_sem).wait()


def codes(index, others, lengths, tokens, sources, rank, columns):
    many, features = tokens.shape
    count = lengths.shape[1]
    routed = others is not None
    kinds = [(kind, len(held)) for kind, held in sources]
    arrays = [array for _, held in sources for array in held]
    return pl.pallas_call(
        functools.partial(code_kernel, count, kinds, routed),
        grid_spec=pltpu.PrefetchScalarGridSpec(
            num_scalar_prefetch=3,
            grid=(),
            in_specs=[VMEM] + [ANY] * len(arrays),
            out_specs=[VMEM, VMEM, pl.BlockSpec(memory_space=pltpu.SMEM)],
            scratch_shapes=[
                pltpu.VMEM((count * rank, features), tokens.dtype),
                pltpu.SemaphoreType.DMA,
                pltpu.SemaphoreType.DMA,
            ],
        ),
        out_shape=[
            jax.ShapeDtypeStruct((many // 2, 2 * rank), jnp.float32),
            jax.ShapeDtypeStruct((count * rank, columns), tokens.dtype),
            jax.ShapeDtypeStruct((1,), jnp.int32),
        ],
        compiler_params=pltpu.CompilerParams(vmem_limit_bytes=(16 if routed else 40) * MIB),
        name="codes",
    )(index, others if routed else index, lengths, in_vmem(tokens) if routed else tokens, *arrays)


def finish_kernel(count, parts, shares, tile, lengths, *refs):
    code_parts, base_parts = refs[:parts], refs[parts : parts + sum(shares)]
    up, out, hold, sem = refs[parts + sum(shares) :]
    rank = up.shape[0] // count
    code = code_parts[0][...]
    for p in range(1, parts):
        code = code + code_parts[p][...]
    half = code.shape[0]
    copies = []
    for i in range(out.shape[0] // tile):
        first = i * tile
        side, at = first // half, first % half
        mine = code[at : at + tile, side * rank : (side + 1) * rank]
        which = request_of_rows(lengths, count, first, tile)
        zero = jnp.zeros_like(mine)
        wide = jnp.concatenate([jnp.where(which == r, mine, zero) for r in range(count)], axis=1)
        delta = None
        for _ in range(3):
            part = wide.astype(jnp.bfloat16)
            wide = wide - part.astype(jnp.float32)
            term = jnp.dot(part, up[...], preferred_element_type=jnp.float32)
            delta = term if delta is None else delta + term
        rows = pl.ds(first, tile)
        left, number = 0, 0
        for share in shares:
            base = base_parts[number][rows, :]
            for p in range(1, share):
                base = base + base_parts[number + p][rows, :]
            number += share
            right = left + base.shape[1]
            total = base + ADAPTER_SCALE * delta[:, left:right]
            hold[rows, left:right] = total.astype(hold.dtype)
            left = right
        copies.append(pltpu.make_async_copy(hold.at[rows, :], out.at[rows, :], sem.at[i]))
        copies[-1].start()
    for copy in copies:
        copy.wait()


def finish(lengths, code_parts, base, up):
    many = base[0][0].shape[0]
    columns = up.shape[1]
    count = lengths.shape[1]
    parts = len(code_parts)
    tile = min(256, many // 2)
    shares = [len(share) for share in base]
    return pl.pallas_call(
        functools.partial(finish_kernel, count, parts, shares, tile),
        grid_spec=pltpu.PrefetchScalarGridSpec(
            num_scalar_prefetch=1,
            grid=(),
            in_specs=[VMEM] * (parts + sum(shares) + 1),
            out_specs=ANY,
            scratch_shapes=[
                pltpu.VMEM((many, columns), jnp.bfloat16),
                pltpu.SemaphoreType.DMA((many // tile,)),
            ],
        ),
        out_shape=jax.ShapeDtypeStruct((many, columns), jnp.bfloat16),
        compiler_params=pltpu.CompilerParams(vmem_limit_bytes=24 * MIB),
        name="finish",
    )(lengths, *code_parts, *[part for share in base for part in share], up)


def gathered(part, axis, size):
    held = [part]
    for step in range(1, size):
        held.append(lax.ppermute(part, axis, [(i, (i + step) % size) for i in range(size)]))
    return held


def route(table, down_pool, up_pool, n_dp, tokens, key_weight):
    rank = down_pool.shape[1]
    size = rank // 2
    half = up_pool.shape[2] // 2
    outer = [(i, i ^ 2) for i in range(n_dp)]
    middle = [(i, i + 2) for i in (2, 3)] + [(i, i - 2) for i in (4, 5)]
    over_x = [(i, i ^ 1) for i in range(n_dp)]
    got = [([], [], []), ([], [], [])]
    pieces = [(1, 0), (1, half), (0, 0), (0, half)]
    done = []
    for step in range(Z_STEPS):
        streams = [E_TABLE, O_TABLE] + ([X_TABLE] if step < X_STEPS else [])
        for part in range(2):
            known = [list(arrays) for arrays in got[part]]
            piece = pieces[step - 1] if part == 1 and 1 <= step <= len(pieces) else None
            sends, product = pick(
                step, part * size, size, streams, table, down_pool, up_pool, known, piece,
                tokens, key_weight,
            )
            done += product
            for stream, send in zip(streams, sends):
                pairs = (outer, middle, over_x)[stream]
                got[part][stream].append(lax.ppermute(send, "dp", pairs))
    return got, done


def shards(sizes, tokens, key_weight, down_pool, up_pool, adapter_ids, lengths, owner_map):
    n_groups, n_dp, n_tensor = sizes
    held, rank, width = down_pool.shape
    columns = up_pool.shape[2]

    def sent_on(part, step):
        pairs = [(i, (i + step) % n_tensor) for i in range(n_tensor)]
        return lax.ppermute(part, "tensor", pairs)

    def by_all_to_all():
        me = lax.axis_index("tensor")
        parts = []
        for step in range(n_tensor):
            first = lax.rem(me + step, n_tensor) * columns
            weight = lax.dynamic_slice_in_dim(key_weight, first, columns, 1)
            part = jnp.dot(tokens, weight, preferred_element_type=jnp.float32)
            parts.append(sent_on(part, step) if step else part)
        blocks = dense(adapter_ids, owner_map, down_pool, up_pool)
        member = lax.axis_index("dp")
        my_ids = lax.dynamic_index_in_dim(adapter_ids, member, 0, keepdims=False)
        index = (owner_map[my_ids] // held)[:, None]
        code, up, _ = codes(index, None, lengths, tokens, [("several", (blocks,))], rank, columns)
        return finish(lengths, gathered(code, "tensor", n_tensor), [parts], up)

    routable = n_dp == 8 and n_tensor == 2 and n_groups <= 2
    if not (routable and rank % 32 == 0 and adapter_ids.shape[1] == 4):
        return by_all_to_all()
    table = plan(held, adapter_ids, owner_map)
    got, done = route(table, down_pool, up_pool, n_dp, tokens, key_weight)
    base = [[here, sent_on(there, 1)] for there, here in zip(done[:2], done[2:])]
    others = gathered(table, "groups", n_groups)[-1]
    sources = [("pool", (in_hbm(down_pool), in_hbm(up_pool)))]
    for stream in (2, 0, 1):
        sources += [("block", pair) for pair in zip(got[0][stream], got[1][stream])]
    code, up, misfit = codes(table, others, lengths, tokens, sources, rank, columns)
    keys = finish(lengths, gathered(code, "tensor", n_tensor), base, up)
    return lax.cond(misfit[0] == 0, lambda: keys, by_all_to_all)


def solution(mesh):
    placed = (
        P(("groups", "dp"), "tensor"),
        P("tensor", None),
        P("dp", None, "tensor"),
        P("dp", None, "tensor"),
        P("groups", None),
        P(("groups", "dp"), None),
        P("groups"),
    )
    sizes = tuple(mesh.shape[name] for name in ("groups", "dp", "tensor"))
    return jax.shard_map(
        functools.partial(shards, sizes),
        mesh=mesh,
        in_specs=placed,
        out_specs=P(("groups", "dp"), "tensor"),
        check_vma=False,
    )
```

```python
import functools

import jax
import jax.numpy as jnp
from jax import lax
from jax.experimental import pallas as pl
from jax.experimental.pallas import tpu as pltpu
from jax.sharding import PartitionSpec as P

ADAPTER_SCALE = 2.0
MIB = 1 << 20
ANY = pl.BlockSpec(memory_space=pl.ANY)
VMEM = pl.BlockSpec(memory_space=pltpu.VMEM)


def in_vmem(x):
    return pltpu.with_memory_space_constraint(x, pltpu.VMEM)


def in_hbm(x):
    return pltpu.with_memory_space_constraint(x, pltpu.HBM)


X_STEPS = 4
Z_STEPS = 6
NEVER = 1000.0
E_TABLE, O_TABLE, X_TABLE, PLACE, MISFIT = range(5)


def plan_kernel(held, planes, req, ids, owner_map, out):
    n = planes * req
    member = lax.axis_index("dp")
    plane, column = member // 2, member % 2
    lane = lax.broadcasted_iota(jnp.int32, (n, 128), 1)
    sub = lax.broadcasted_iota(jnp.int32, (n, 128), 0)
    lane_f, sub_f = lane.astype(jnp.float32), sub.astype(jnp.float32)

    def row_of(at):
        return sum([(at >= q * req).astype(jnp.float32) for q in range(1, planes)])

    dest_i, dest_k = row_of(lane), row_of(sub)

    def entries(c):
        by_lane = [jnp.full((n, 128), -1.0, jnp.float32) for _ in range(5)]
        by_sub = [jnp.full((n, 128), -2.0, jnp.float32) for _ in range(5)]
        for i in range(n):
            slot = owner_map[ids[i % req, 2 * (i // req) + c]]
            owner = slot // held
            values = (slot, owner, owner // 2, owner % 2, slot - owner * held)
            for v, value in enumerate(values):
                value = value.astype(jnp.float32)
                by_lane[v] = jnp.where(lane == i, value, by_lane[v])
                by_sub[v] = jnp.where(sub == i, value, by_sub[v])
        return by_lane, by_sub

    def over_x(by_lane, by_sub, c):
        (slot_i, owner_i, src_i, col_i, _), (slot_k, owner_k, src_k, col_k, _) = by_lane, by_sub
        c = c.astype(jnp.float32)
        same = slot_i == slot_k
        key_i = jnp.where(col_i == c, -1.0, jnp.abs(dest_i - src_i) * n + (n - 1 - lane_f))
        key_k = jnp.where(col_k == c, -1.0, jnp.abs(dest_k - src_k) * n + (n - 1 - sub_f))
        best_i = jnp.max(jnp.where(same, key_k, -1.0), axis=0, keepdims=True)
        best_k = jnp.max(jnp.where(same, key_i, -1.0), axis=1, keepdims=True)
        ahead = (key_k == best_k) & (key_k >= 0) & (owner_k == owner_i) & (key_k > best_i)
        pos = jnp.sum(jnp.where(ahead, 1.0, 0.0), axis=0, keepdims=True)
        return pos, (key_i == best_i) & (key_i >= 0)

    row = lax.broadcasted_iota(jnp.int32, (8, 128), 0)
    lane8 = lax.broadcasted_iota(jnp.int32, (8, 128), 1).astype(jnp.float32)
    row_f = row.astype(jnp.float32)
    links = planes - 1
    up = row < links
    last = float(planes - 1)
    link = jnp.where(up, row_f, row_f - links)

    def top(x):
        return jnp.broadcast_to(x[0:1, :], (8, 128))

    def schedule(by_lane, by_sub, xpos, c):
        slot_i, _, src_i, col_i, _ = by_lane
        same = slot_i == by_sub[0]
        dest, src = top(dest_i), top(src_i)
        d_dest, d_src = jnp.where(up, dest, last - dest), jnp.where(up, src, last - src)

        def beyond(sign):
            more = same & ((dest_k - dest_i) * sign > 0)
            return top(jnp.max(jnp.where(more, 1.0, 0.0), axis=0, keepdims=True))

        farther = jnp.where(up, beyond(1.0), beyond(-1.0))
        valid = (row < 2 * links) & (lane8 < n)
        lead = valid & (farther == 0.0) & (d_dest > d_src)
        on = lead & (d_src <= link) & (d_dest > link)
        starts = d_src == link
        local = top(col_i) == c.astype(jnp.float32)
        first = jnp.where(local, 0.0, top(jnp.broadcast_to(xpos, (8, 128))) + 1)
        ready = jnp.where(starts, first, NEVER)
        pos = jnp.full((8, 128), NEVER, jnp.float32)
        for t in range(Z_STEPS):
            open_ = on & (ready <= t) & (pos >= NEVER)
            key = jnp.where(open_, d_dest * 128 + (127 - lane8), -1.0)
            chosen = open_ & (key == jnp.max(key, axis=1, keepdims=True))
            pos = jnp.where(chosen, float(t), pos)
            before = jnp.concatenate([pos[7:8, :], pos[0:7, :]], axis=0)
            ready = jnp.where(starts, first, before + 1)
        misfit = jnp.max(jnp.where(on & (pos >= NEVER), 1.0, 0.0), axis=1, keepdims=True)
        return same, dest, src, local, on, starts, pos, jnp.max(misfit, axis=0, keepdims=True)

    by_lane, by_sub = entries(column)
    within_i = by_lane[4]
    xpos, _ = over_x(by_lane, by_sub, column)
    same, dest, src, local, on, starts, pos, misfit = schedule(by_lane, by_sub, xpos, column)
    other_lane, other_sub = entries(1 - column)
    other_xpos, other_lead = over_x(other_lane, other_sub, 1 - column)
    other_misfit = schedule(other_lane, other_sub, other_xpos, 1 - column)[-1]
    misfit = jnp.maximum(misfit, other_misfit)

    from_x = float(held)
    from_e = from_x + X_STEPS
    from_o = from_e + Z_STEPS
    own = jnp.where(local, top(within_i), from_x + top(jnp.broadcast_to(xpos, (8, 128))))

    def table(hit, source):
        return jnp.sum(jnp.where(hit, source + 1, 0.0), axis=1, keepdims=True) - 1

    def only(which, x):
        return jnp.sum(jnp.where(row == which, x, 0.0), axis=0, keepdims=True)

    def sent(which, passing_from):
        hit = only(which, jnp.where(on, 1.0, 0.0)) == 1.0
        fresh = only(which, jnp.where(starts, 1.0, 0.0)) == 1.0
        at, earlier = only(which, pos), only(which - 1, pos)
        source = jnp.where(fresh, own, passing_from + earlier)
        return table(hit & (at == row_f), source)

    e_row = jnp.where(plane % 2 == 0, plane, links + (planes - 1 - plane))
    o_row = jnp.where(plane == 1, 1, jnp.where(plane == 2, links + 1, 7))
    e_table = sent(e_row, from_o)
    o_table = sent(o_row, from_e)
    (_, owner_o, _, _, within_o) = other_lane
    mine = top(owner_o) == member.astype(jnp.float32)
    other_lead8 = top(jnp.where(other_lead, 1.0, 0.0)) == 1.0
    other_xpos8 = top(jnp.broadcast_to(other_xpos, (8, 128)))
    x_table = table(mine & other_lead8 & (other_xpos8 == row_f), top(within_o))

    arrival = jnp.zeros((8, 128), jnp.float32)
    for which in range(2 * links):
        one = jnp.broadcast_to(pos[which : which + 1, :], (n, 128))
        one_on = jnp.broadcast_to(jnp.where(on, 1.0, 0.0)[which : which + 1, :], (n, 128))
        by_k = jnp.sum(jnp.where((lane == sub) & (one_on == 1.0), one + 1, 0.0), axis=1, keepdims=True)
        arrives = jnp.max(jnp.where(same, by_k, 0.0), axis=0, keepdims=True) - 1
        if which < links:
            hit = (dest > src) & (dest == which + 1)
        else:
            hit = (dest < src) & (last - dest == which - links + 1)
        arrival = jnp.where(hit, arrives, arrival)
    odd = dest - 2 * jnp.floor(dest * 0.5)
    outer = jnp.where(dest > src, odd, 1 - odd) == 1.0
    final = jnp.where(dest == src, own, jnp.where(outer, from_e, from_o) + arrival)
    my_rows = lane8 == (plane * req).astype(jnp.float32) + row_f
    place = jnp.sum(jnp.where(my_rows & (row < req), final, 0.0), axis=1, keepdims=True)
    place = jnp.where(misfit == 1.0, 0.0, place)
    result = jnp.zeros((8, 128), jnp.float32)
    for at, values in ((E_TABLE, e_table), (O_TABLE, o_table), (X_TABLE, x_table), (PLACE, place), (MISFIT, misfit)):
        result = jnp.where(lane8 == at, values, result)
    out[...] = result.astype(jnp.int32)


def plan(held, adapter_ids, owner_map):
    rows, req = adapter_ids.shape
    return pl.pallas_call(
        functools.partial(plan_kernel, held, rows // 2, req),
        grid_spec=pltpu.PrefetchScalarGridSpec(
            num_scalar_prefetch=2, grid=(), in_specs=[], out_specs=VMEM
        ),
        out_shape=jax.ShapeDtypeStruct((8, 128), jnp.int32),
        compiler_params=pltpu.CompilerParams(vmem_limit_bytes=4 * MIB),
        name="plan",
    )(adapter_ids.T, owner_map)


def pick_kernel(step, size, lo, streams, held, piece, table, down, up, *refs):
    at = 0
    got = []
    for many in held:
        got.append(refs[at : at + many])
        at += many
    refs = list(refs[at:])
    if piece is not None:
        tokens, weight = refs.pop(0), refs.pop(0)
        held_weight, weight_sem = refs.pop(-2), refs.pop(-1)
        distance, shift = piece
        columns, wide = up.shape[2], held_weight.shape[1]
        to = lax.rem(lax.axis_index("tensor") + distance, 2)
        first = pl.multiple_of(to * columns + shift, 128)
        load = pltpu.make_async_copy(weight.at[:, pl.ds(first, wide)], held_weight, weight_sem)
        load.start()
    outs, sem = refs[: len(streams)], refs[-1]
    slots, _, width = down.shape
    from_x, from_e, from_o = slots, slots + X_STEPS, slots + X_STEPS + Z_STEPS
    over_x = [(from_x + t, ref) for t, ref in enumerate(got[2])]
    outer = [(from_e + t, ref) for t, ref in enumerate(got[0])]
    middle = [(from_o + t, ref) for t, ref in enumerate(got[1])]
    sources = {E_TABLE: over_x + middle, O_TABLE: over_x + outer, X_TABLE: []}
    rows = pl.ds(lo, size)
    for i, stream in enumerate(streams):
        code, out = table[step, stream], outs[i]

        @pl.when((code >= 0) & (code < slots))
        def _(code=code, out=out, i=i):
            pltpu.make_async_copy(
                down.at[code, rows, :], out.at[:, pl.ds(0, width)], sem.at[i]
            ).start()
            pltpu.make_async_copy(
                up.at[code, rows, :], out.at[:, pl.ds(width, up.shape[2])], sem.at[i]
            ).start()

        for number, ref in sources[stream]:

            @pl.when(code == number)
            def _(ref=ref, out=out, i=i):
                pltpu.make_async_copy(ref, out, sem.at[i]).start()

    if piece is not None:
        load.wait()
        product = refs[len(streams)]
        tile = min(256, product.shape[0])
        for at in range(0, product.shape[0], tile):
            product[at : at + tile, :] = jnp.dot(
                tokens[at : at + tile, :],
                held_weight[...],
                preferred_element_type=jnp.float32,
            )

    for i, stream in enumerate(streams):

        @pl.when(table[step, stream] >= 0)
        def _(i=i):
            pltpu.make_async_copy(outs[i], outs[i], sem.at[i]).wait()


def pick(step, lo, size, streams, table, down_pool, up_pool, got, piece, tokens, key_weight):
    many = tokens.shape[0]
    columns = up_pool.shape[2]
    wide = down_pool.shape[2] + columns
    held = [len(arrays) for arrays in got]
    operands = [in_hbm(down_pool), in_hbm(up_pool)] + [a for arrays in got for a in arrays]
    in_specs = [ANY] * len(operands)
    out_specs = [ANY] * len(streams)
    out_shape = [pltpu.VMEM((size, wide), down_pool.dtype)] * len(streams)
    scratch = [pltpu.SemaphoreType.DMA((len(streams),))]
    if piece is not None:
        operands += [in_vmem(tokens), in_hbm(key_weight)]
        in_specs += [VMEM, ANY]
        out_specs.append(VMEM)
        out_shape.append(jax.ShapeDtypeStruct((many, columns // 2), jnp.float32))
        scratch += [
            pltpu.VMEM((tokens.shape[1], columns // 2), key_weight.dtype),
            pltpu.SemaphoreType.DMA,
        ]
    outs = pl.pallas_call(
        functools.partial(pick_kernel, step, size, lo, streams, held, piece),
        grid_spec=pltpu.PrefetchScalarGridSpec(
            num_scalar_prefetch=1,
            grid=(),
            in_specs=in_specs,
            out_specs=out_specs,
            scratch_shapes=scratch,
        ),
        out_shape=out_shape,
        compiler_params=pltpu.CompilerParams(vmem_limit_bytes=(4 if piece is None else 16) * MIB),
        name="pick",
    )(table, *operands)
    return outs[: len(streams)], outs[len(streams) :]


def dense_kernel(index, down, up, out):
    width = down.shape[2]
    out[:, :, :width] = down[...]
    out[:, :, width:] = up[...]


def dense(adapter_ids, owner_map, down_pool, up_pool):
    held, rank, width = down_pool.shape
    columns = up_pool.shape[2]
    slots = owner_map[adapter_ids] - lax.axis_index("dp") * held
    here = (slots >= 0) & (slots < held)
    index = jnp.sum(jnp.where(here, slots, 0), axis=1).astype(jnp.int32)
    many = index.shape[0]
    send = pl.pallas_call(
        dense_kernel,
        grid_spec=pltpu.PrefetchScalarGridSpec(
            num_scalar_prefetch=1,
            grid=(many,),
            in_specs=[
                pl.BlockSpec((1, rank, width), lambda j, index: (index[j], 0, 0)),
                pl.BlockSpec((1, rank, columns), lambda j, index: (index[j], 0, 0)),
            ],
            out_specs=pl.BlockSpec((1, rank, width + columns), lambda j, index: (j, 0, 0)),
        ),
        out_shape=jax.ShapeDtypeStruct((many, rank, width + columns), down_pool.dtype),
        name="pick_all",
    )(index, in_hbm(down_pool), in_hbm(up_pool))
    return lax.all_to_all(send, "dp", split_axis=0, concat_axis=0, tiled=True)


def stage_kernel(source, out, sem):
    copy = pltpu.make_async_copy(source, out, sem)
    copy.start()
    copy.wait()


def stage(x):
    return pl.pallas_call(
        stage_kernel,
        in_specs=[ANY],
        out_specs=VMEM,
        out_shape=pltpu.VMEM(x.shape, x.dtype),
        scratch_shapes=[pltpu.SemaphoreType.DMA],
        compiler_params=pltpu.CompilerParams(vmem_limit_bytes=4 * MIB),
        name="stage",
    )(in_hbm(x))


def request_of_rows(lengths, count, first, rows):
    at = first + lax.broadcasted_iota(jnp.int32, (rows, 1), 0)
    which = jnp.zeros((rows, 1), jnp.int32)
    end = 0
    for r in range(count - 1):
        end = end + lengths[0, r]
        which += (at >= end).astype(jnp.int32)
    return which


def code_kernel(count, kinds, routed, index, others, lengths, tokens, *refs):
    n = sum(many for _, many in kinds)
    arrays, refs = refs[:n], refs[n:]
    out, up, flag, down, sem, up_sem = refs
    rank, columns = out.shape[1] // 2, up.shape[1]
    features = tokens.shape[1]
    flag[0] = 0
    if routed:
        flag[0] = jnp.maximum(index[0, MISFIT], others[0, MISFIT])

    def source(r):
        return index[r, PLACE] if routed else index[r, 0]

    def load(r, kind, held):
        if kind == "pool":
            slot = source(r)
            parts = [(held[0].at[slot], held[1].at[slot])]
        elif kind == "several":
            block = held[0].at[source(r)]
            parts = [(block.at[:, pl.ds(0, features)], block.at[:, pl.ds(features, columns)])]
        else:
            parts = [
                (ref.at[:, pl.ds(0, features)], ref.at[:, pl.ds(features, columns)])
                for ref in held
            ]
        size = rank // len(parts)
        for p, (down_part, up_part) in enumerate(parts):
            mine = pl.ds(r * rank + p * size, size)
            pltpu.make_async_copy(down_part, down.at[mine, :], sem).start()
            pltpu.make_async_copy(up_part, up.at[mine, :], up_sem).start()

    for r in range(count):
        at, number = 0, 0
        for kind, many in kinds:
            held = arrays[at : at + many]
            at += many
            if kind == "several":
                load(r, kind, held)
            elif kind == "pool":
                number = held[0].shape[0]

                @pl.when(source(r) < number)
                def _(r=r, kind=kind, held=held):
                    load(r, kind, held)

            else:

                @pl.when(source(r) == number)
                def _(r=r, kind=kind, held=held):
                    load(r, kind, held)

                number += 1

    pltpu.make_async_copy(down, down, sem).wait()
    half = out.shape[0]
    tile = min(256, half)
    for i in range(half // tile):
        parts = []
        for side in range(2):
            first = side * half + i * tile
            full = lax.dot_general(
                tokens[first : first + tile, :],
                down[...],
                (((1,), (1,)), ((), ())),
                preferred_element_type=jnp.float32,
            )
            which = request_of_rows(lengths, count, first, tile)
            code = full[:, :rank]
            for r in range(1, count):
                code = jnp.where(which == r, full[:, r * rank : (r + 1) * rank], code)
            parts.append(code)
        out[i * tile : (i + 1) * tile, :] = jnp.concatenate(parts, axis=1)
    pltpu.make_async_copy(up, up, up_sem).wait()


def codes(index, others, lengths, tokens, sources, rank, columns):
    many, features = tokens.shape
    count = lengths.shape[1]
    routed = others is not None
    kinds = [(kind, len(held)) for kind, held in sources]
    arrays = [array for _, held in sources for array in held]
    return pl.pallas_call(
        functools.partial(code_kernel, count, kinds, routed),
        grid_spec=pltpu.PrefetchScalarGridSpec(
            num_scalar_prefetch=3,
            grid=(),
            in_specs=[VMEM] + [ANY] * len(arrays),
            out_specs=[VMEM, VMEM, pl.BlockSpec(memory_space=pltpu.SMEM)],
            scratch_shapes=[
                pltpu.VMEM((count * rank, features), tokens.dtype),
                pltpu.SemaphoreType.DMA,
                pltpu.SemaphoreType.DMA,
            ],
        ),
        out_shape=[
            jax.ShapeDtypeStruct((many // 2, 2 * rank), jnp.float32),
            jax.ShapeDtypeStruct((count * rank, columns), tokens.dtype),
            jax.ShapeDtypeStruct((1,), jnp.int32),
        ],
        compiler_params=pltpu.CompilerParams(vmem_limit_bytes=(16 if routed else 40) * MIB),
        name="codes",
    )(index, others if routed else index, lengths, in_vmem(tokens) if routed else tokens, *arrays)


def finish_kernel(count, parts, shares, tile, lengths, *refs):
    code_parts, base_parts = refs[:parts], refs[parts : parts + sum(shares)]
    up, out, hold, sem = refs[parts + sum(shares) :]
    rank = up.shape[0] // count
    code = code_parts[0][...]
    for p in range(1, parts):
        code = code + code_parts[p][...]
    half = code.shape[0]
    copies = []
    for i in range(out.shape[0] // tile):
        first = i * tile
        side, at = first // half, first % half
        mine = code[at : at + tile, side * rank : (side + 1) * rank]
        which = request_of_rows(lengths, count, first, tile)
        zero = jnp.zeros_like(mine)
        wide = jnp.concatenate([jnp.where(which == r, mine, zero) for r in range(count)], axis=1)
        delta = None
        for _ in range(3):
            part = wide.astype(jnp.bfloat16)
            wide = wide - part.astype(jnp.float32)
            term = jnp.dot(part, up[...], preferred_element_type=jnp.float32)
            delta = term if delta is None else delta + term
        rows = pl.ds(first, tile)
        left, number = 0, 0
        for share in shares:
            base = base_parts[number][rows, :]
            for p in range(1, share):
                base = base + base_parts[number + p][rows, :]
            number += share
            right = left + base.shape[1]
            total = base + ADAPTER_SCALE * delta[:, left:right]
            hold[rows, left:right] = total.astype(hold.dtype)
            left = right
        copies.append(pltpu.make_async_copy(hold.at[rows, :], out.at[rows, :], sem.at[i]))
        copies[-1].start()
    for copy in copies:
        copy.wait()


def finish(lengths, code_parts, base, up):
    many = base[0][0].shape[0]
    columns = up.shape[1]
    count = lengths.shape[1]
    parts = len(code_parts)
    tile = min(256, many // 2)
    shares = [len(share) for share in base]
    return pl.pallas_call(
        functools.partial(finish_kernel, count, parts, shares, tile),
        grid_spec=pltpu.PrefetchScalarGridSpec(
            num_scalar_prefetch=1,
            grid=(),
            in_specs=[VMEM] * (parts + sum(shares) + 1),
            out_specs=ANY,
            scratch_shapes=[
                pltpu.VMEM((many, columns), jnp.bfloat16),
                pltpu.SemaphoreType.DMA((many // tile,)),
            ],
        ),
        out_shape=jax.ShapeDtypeStruct((many, columns), jnp.bfloat16),
        compiler_params=pltpu.CompilerParams(vmem_limit_bytes=24 * MIB),
        name="finish",
    )(lengths, *code_parts, *[part for share in base for part in share], up)


def gathered(part, axis, size):
    held = [part]
    for step in range(1, size):
        held.append(lax.ppermute(part, axis, [(i, (i + step) % size) for i in range(size)]))
    return held


def route(table, down_pool, up_pool, n_dp, tokens, key_weight):
    rank = down_pool.shape[1]
    size = rank // 2
    half = up_pool.shape[2] // 2
    outer = [(i, i ^ 2) for i in range(n_dp)]
    middle = [(i, i + 2) for i in (2, 3)] + [(i, i - 2) for i in (4, 5)]
    over_x = [(i, i ^ 1) for i in range(n_dp)]
    got = [([], [], []), ([], [], [])]
    pieces = [(1, 0), (1, half), (0, 0), (0, half)]
    done = []
    for step in range(Z_STEPS):
        streams = [E_TABLE, O_TABLE] + ([X_TABLE] if step < X_STEPS else [])
        for part in range(2):
            known = [list(arrays) for arrays in got[part]]
            piece = pieces[step - 1] if part == 1 and 1 <= step <= len(pieces) else None
            sends, product = pick(
                step, part * size, size, streams, table, down_pool, up_pool, known, piece,
                tokens, key_weight,
            )
            done += product
            for stream, send in zip(streams, sends):
                pairs = (outer, middle, over_x)[stream]
                got[part][stream].append(lax.ppermute(send, "dp", pairs))
    return got, done


def shards(sizes, tokens, key_weight, down_pool, up_pool, adapter_ids, lengths, owner_map):
    n_groups, n_dp, n_tensor = sizes
    held, rank, width = down_pool.shape
    columns = up_pool.shape[2]

    def sent_on(part, step):
        pairs = [(i, (i + step) % n_tensor) for i in range(n_tensor)]
        return lax.ppermute(part, "tensor", pairs)

    def by_all_to_all():
        me = lax.axis_index("tensor")
        parts = []
        for step in range(n_tensor):
            first = lax.rem(me + step, n_tensor) * columns
            weight = lax.dynamic_slice_in_dim(key_weight, first, columns, 1)
            part = jnp.dot(tokens, weight, preferred_element_type=jnp.float32)
            parts.append(sent_on(part, step) if step else part)
        blocks = dense(adapter_ids, owner_map, down_pool, up_pool)
        member = lax.axis_index("dp")
        my_ids = lax.dynamic_index_in_dim(adapter_ids, member, 0, keepdims=False)
        index = (owner_map[my_ids] // held)[:, None]
        code, up, _ = codes(index, None, lengths, tokens, [("several", (blocks,))], rank, columns)
        return finish(lengths, gathered(code, "tensor", n_tensor), [parts], up)

    routable = n_dp == 8 and n_tensor == 2 and n_groups <= 2
    if not (routable and rank % 32 == 0 and adapter_ids.shape[1] == 4):
        return by_all_to_all()
    table = plan(held, adapter_ids, owner_map)
    at_hand = stage(tokens)
    got, done = route(table, down_pool, up_pool, n_dp, at_hand, key_weight)
    base = [[here, sent_on(there, 1)] for there, here in zip(done[:2], done[2:])]
    others = gathered(table, "groups", n_groups)[-1]
    sources = [("pool", (in_hbm(down_pool), in_hbm(up_pool)))]
    for stream in (2, 0, 1):
        sources += [("block", pair) for pair in zip(got[0][stream], got[1][stream])]
    code, up, misfit = codes(table, others, lengths, at_hand, sources, rank, columns)
    keys = finish(lengths, gathered(code, "tensor", n_tensor), base, up)
    return lax.cond(misfit[0] == 0, lambda: keys, by_all_to_all)


def solution(mesh):
    placed = (
        P(("groups", "dp"), "tensor"),
        P("tensor", None),
        P("dp", None, "tensor"),
        P("dp", None, "tensor"),
        P("groups", None),
        P(("groups", "dp"), None),
        P("groups"),
    )
    sizes = tuple(mesh.shape[name] for name in ("groups", "dp", "tensor"))
    return jax.shard_map(
        functools.partial(shards, sizes),
        mesh=mesh,
        in_specs=placed,
        out_specs=P(("groups", "dp"), "tensor"),
        check_vma=False,
    )
```

```python
import functools

import jax
import jax.numpy as jnp
from jax import lax
from jax.experimental import pallas as pl
from jax.experimental.pallas import tpu as pltpu
from jax.sharding import PartitionSpec as P

ADAPTER_SCALE = 2.0
MIB = 1 << 20
ANY = pl.BlockSpec(memory_space=pl.ANY)
VMEM = pl.BlockSpec(memory_space=pltpu.VMEM)


def in_vmem(x):
    return pltpu.with_memory_space_constraint(x, pltpu.VMEM)


def in_hbm(x):
    return pltpu.with_memory_space_constraint(x, pltpu.HBM)


X_STEPS = 4
Z_STEPS = 6
NEVER = 1000.0
E_TABLE, O_TABLE, X_TABLE, PLACE, MISFIT = range(5)


def plan_kernel(held, planes, req, ids, owner_map, out):
    n = planes * req
    member = lax.axis_index("dp")
    plane, column = member // 2, member % 2
    lane = lax.broadcasted_iota(jnp.int32, (n, 128), 1)
    sub = lax.broadcasted_iota(jnp.int32, (n, 128), 0)
    lane_f, sub_f = lane.astype(jnp.float32), sub.astype(jnp.float32)

    def row_of(at):
        return sum([(at >= q * req).astype(jnp.float32) for q in range(1, planes)])

    dest_i, dest_k = row_of(lane), row_of(sub)

    def entries(c):
        by_lane = [jnp.full((n, 128), -1.0, jnp.float32) for _ in range(5)]
        by_sub = [jnp.full((n, 128), -2.0, jnp.float32) for _ in range(5)]
        for i in range(n):
            slot = owner_map[ids[i % req, 2 * (i // req) + c]]
            owner = slot // held
            values = (slot, owner, owner // 2, owner % 2, slot - owner * held)
            for v, value in enumerate(values):
                value = value.astype(jnp.float32)
                by_lane[v] = jnp.where(lane == i, value, by_lane[v])
                by_sub[v] = jnp.where(sub == i, value, by_sub[v])
        return by_lane, by_sub

    def over_x(by_lane, by_sub, c):
        (slot_i, owner_i, src_i, col_i, _), (slot_k, owner_k, src_k, col_k, _) = by_lane, by_sub
        c = c.astype(jnp.float32)
        same = slot_i == slot_k
        key_i = jnp.where(col_i == c, -1.0, jnp.abs(dest_i - src_i) * n + (n - 1 - lane_f))
        key_k = jnp.where(col_k == c, -1.0, jnp.abs(dest_k - src_k) * n + (n - 1 - sub_f))
        best_i = jnp.max(jnp.where(same, key_k, -1.0), axis=0, keepdims=True)
        best_k = jnp.max(jnp.where(same, key_i, -1.0), axis=1, keepdims=True)
        ahead = (key_k == best_k) & (key_k >= 0) & (owner_k == owner_i) & (key_k > best_i)
        pos = jnp.sum(jnp.where(ahead, 1.0, 0.0), axis=0, keepdims=True)
        return pos, (key_i == best_i) & (key_i >= 0)

    row = lax.broadcasted_iota(jnp.int32, (8, 128), 0)
    lane8 = lax.broadcasted_iota(jnp.int32, (8, 128), 1).astype(jnp.float32)
    row_f = row.astype(jnp.float32)
    links = planes - 1
    up = row < links
    last = float(planes - 1)
    link = jnp.where(up, row_f, row_f - links)

    def top(x):
        return jnp.broadcast_to(x[0:1, :], (8, 128))

    def schedule(by_lane, by_sub, xpos, c):
        slot_i, _, src_i, col_i, _ = by_lane
        same = slot_i == by_sub[0]
        dest, src = top(dest_i), top(src_i)
        d_dest, d_src = jnp.where(up, dest, last - dest), jnp.where(up, src, last - src)

        def beyond(sign):
            more = same & ((dest_k - dest_i) * sign > 0)
            return top(jnp.max(jnp.where(more, 1.0, 0.0), axis=0, keepdims=True))

        farther = jnp.where(up, beyond(1.0), beyond(-1.0))
        valid = (row < 2 * links) & (lane8 < n)
        lead = valid & (farther == 0.0) & (d_dest > d_src)
        on = lead & (d_src <= link) & (d_dest > link)
        starts = d_src == link
        local = top(col_i) == c.astype(jnp.float32)
        first = jnp.where(local, 0.0, top(jnp.broadcast_to(xpos, (8, 128))) + 1)
        ready = jnp.where(starts, first, NEVER)
        pos = jnp.full((8, 128), NEVER, jnp.float32)
        for t in range(Z_STEPS):
            open_ = on & (ready <= t) & (pos >= NEVER)
            key = jnp.where(open_, d_dest * 128 + (127 - lane8), -1.0)
            chosen = open_ & (key == jnp.max(key, axis=1, keepdims=True))
            pos = jnp.where(chosen, float(t), pos)
            before = jnp.concatenate([pos[7:8, :], pos[0:7, :]], axis=0)
            ready = jnp.where(starts, first, before + 1)
        misfit = jnp.max(jnp.where(on & (pos >= NEVER), 1.0, 0.0), axis=1, keepdims=True)
        return same, dest, src, local, on, starts, pos, jnp.max(misfit, axis=0, keepdims=True)

    by_lane, by_sub = entries(column)
    within_i = by_lane[4]
    xpos, _ = over_x(by_lane, by_sub, column)
    same, dest, src, local, on, starts, pos, misfit = schedule(by_lane, by_sub, xpos, column)
    other_lane, other_sub = entries(1 - column)
    other_xpos, other_lead = over_x(other_lane, other_sub, 1 - column)
    other_misfit = schedule(other_lane, other_sub, other_xpos, 1 - column)[-1]
    misfit = jnp.maximum(misfit, other_misfit)

    from_x = float(held)
    from_e = from_x + X_STEPS
    from_o = from_e + Z_STEPS
    own = jnp.where(local, top(within_i), from_x + top(jnp.broadcast_to(xpos, (8, 128))))

    def table(hit, source):
        return jnp.sum(jnp.where(hit, source + 1, 0.0), axis=1, keepdims=True) - 1

    def only(which, x):
        return jnp.sum(jnp.where(row == which, x, 0.0), axis=0, keepdims=True)

    def sent(which, passing_from):
        hit = only(which, jnp.where(on, 1.0, 0.0)) == 1.0
        fresh = only(which, jnp.where(starts, 1.0, 0.0)) == 1.0
        at, earlier = only(which, pos), only(which - 1, pos)
        source = jnp.where(fresh, own, passing_from + earlier)
        return table(hit & (at == row_f), source)

    e_row = jnp.where(plane % 2 == 0, plane, links + (planes - 1 - plane))
    o_row = jnp.where(plane == 1, 1, jnp.where(plane == 2, links + 1, 7))
    e_table = sent(e_row, from_o)
    o_table = sent(o_row, from_e)
    (_, owner_o, _, _, within_o) = other_lane
    mine = top(owner_o) == member.astype(jnp.float32)
    other_lead8 = top(jnp.where(other_lead, 1.0, 0.0)) == 1.0
    other_xpos8 = top(jnp.broadcast_to(other_xpos, (8, 128)))
    x_table = table(mine & other_lead8 & (other_xpos8 == row_f), top(within_o))

    arrival = jnp.zeros((8, 128), jnp.float32)
    for which in range(2 * links):
        one = jnp.broadcast_to(pos[which : which + 1, :], (n, 128))
        one_on = jnp.broadcast_to(jnp.where(on, 1.0, 0.0)[which : which + 1, :], (n, 128))
        by_k = jnp.sum(jnp.where((lane == sub) & (one_on == 1.0), one + 1, 0.0), axis=1, keepdims=True)
        arrives = jnp.max(jnp.where(same, by_k, 0.0), axis=0, keepdims=True) - 1
        if which < links:
            hit = (dest > src) & (dest == which + 1)
        else:
            hit = (dest < src) & (last - dest == which - links + 1)
        arrival = jnp.where(hit, arrives, arrival)
    odd = dest - 2 * jnp.floor(dest * 0.5)
    outer = jnp.where(dest > src, odd, 1 - odd) == 1.0
    final = jnp.where(dest == src, own, jnp.where(outer, from_e, from_o) + arrival)
    my_rows = lane8 == (plane * req).astype(jnp.float32) + row_f
    place = jnp.sum(jnp.where(my_rows & (row < req), final, 0.0), axis=1, keepdims=True)
    place = jnp.where(misfit == 1.0, 0.0, place)
    result = jnp.zeros((8, 128), jnp.float32)
    for at, values in ((E_TABLE, e_table), (O_TABLE, o_table), (X_TABLE, x_table), (PLACE, place), (MISFIT, misfit)):
        result = jnp.where(lane8 == at, values, result)
    out[...] = result.astype(jnp.int32)


def plan(held, adapter_ids, owner_map):
    rows, req = adapter_ids.shape
    return pl.pallas_call(
        functools.partial(plan_kernel, held, rows // 2, req),
        grid_spec=pltpu.PrefetchScalarGridSpec(
            num_scalar_prefetch=2, grid=(), in_specs=[], out_specs=VMEM
        ),
        out_shape=jax.ShapeDtypeStruct((8, 128), jnp.int32),
        compiler_params=pltpu.CompilerParams(vmem_limit_bytes=4 * MIB),
        name="plan",
    )(adapter_ids.T, owner_map)


def pick_kernel(step, size, lo, streams, held, piece, staging, table, down, up, *refs):
    at = 0
    got = []
    for many in held:
        got.append(refs[at : at + many])
        at += many
    refs = list(refs[at:])
    if piece is not None:
        tokens, weight = refs.pop(0), refs.pop(0)
        row_sem = refs.pop(-1) if staging else None
        held_weight, weight_sem = refs.pop(-2), refs.pop(-1)
        distance, shift = piece
        columns, wide = up.shape[2], held_weight.shape[1]
        to = lax.rem(lax.axis_index("tensor") + distance, 2)
        first = pl.multiple_of(to * columns + shift, 128)
        load = pltpu.make_async_copy(weight.at[:, pl.ds(first, wide)], held_weight, weight_sem)
        load.start()
        if staging:
            at_hand, brought = refs[len(streams) + 1], []
            tile = min(256, tokens.shape[0])
            for at in range(0, tokens.shape[0], tile):
                some = pl.ds(at, tile)
                brought.append(
                    pltpu.make_async_copy(
                        tokens.at[some, :], at_hand.at[some, :], row_sem.at[at // tile]
                    )
                )
                brought[-1].start()
            tokens = at_hand
    outs, sem = refs[: len(streams)], refs[-1]
    slots, _, width = down.shape
    from_x, from_e, from_o = slots, slots + X_STEPS, slots + X_STEPS + Z_STEPS
    over_x = [(from_x + t, ref) for t, ref in enumerate(got[2])]
    outer = [(from_e + t, ref) for t, ref in enumerate(got[0])]
    middle = [(from_o + t, ref) for t, ref in enumerate(got[1])]
    sources = {E_TABLE: over_x + middle, O_TABLE: over_x + outer, X_TABLE: []}
    rows = pl.ds(lo, size)
    for i, stream in enumerate(streams):
        code, out = table[step, stream], outs[i]

        @pl.when((code >= 0) & (code < slots))
        def _(code=code, out=out, i=i):
            pltpu.make_async_copy(
                down.at[code, rows, :], out.at[:, pl.ds(0, width)], sem.at[i]
            ).start()
            pltpu.make_async_copy(
                up.at[code, rows, :], out.at[:, pl.ds(width, up.shape[2])], sem.at[i]
            ).start()

        for number, ref in sources[stream]:

            @pl.when(code == number)
            def _(ref=ref, out=out, i=i):
                pltpu.make_async_copy(ref, out, sem.at[i]).start()

    if piece is not None:
        load.wait()
        product = refs[len(streams)]
        tile = min(256, product.shape[0])
        for at in range(0, product.shape[0], tile):
            if staging:
                brought[at // tile].wait()
            product[at : at + tile, :] = jnp.dot(
                tokens[at : at + tile, :],
                held_weight[...],
                preferred_element_type=jnp.float32,
            )

    for i, stream in enumerate(streams):

        @pl.when(table[step, stream] >= 0)
        def _(i=i):
            pltpu.make_async_copy(outs[i], outs[i], sem.at[i]).wait()


def pick(
    step, lo, size, streams, table, down_pool, up_pool, got, piece, staging, tokens, key_weight
):
    many = tokens.shape[0]
    columns = up_pool.shape[2]
    wide = down_pool.shape[2] + columns
    held = [len(arrays) for arrays in got]
    operands = [in_hbm(down_pool), in_hbm(up_pool)] + [a for arrays in got for a in arrays]
    in_specs = [ANY] * len(operands)
    out_specs = [ANY] * len(streams)
    out_shape = [pltpu.VMEM((size, wide), down_pool.dtype)] * len(streams)
    scratch = [pltpu.SemaphoreType.DMA((len(streams),))]
    if piece is not None:
        operands += [in_hbm(tokens) if staging else in_vmem(tokens), in_hbm(key_weight)]
        in_specs += [ANY if staging else VMEM, ANY]
        out_specs.append(VMEM)
        out_shape.append(jax.ShapeDtypeStruct((many, columns // 2), jnp.float32))
        scratch += [
            pltpu.VMEM((tokens.shape[1], columns // 2), key_weight.dtype),
            pltpu.SemaphoreType.DMA,
        ]
        if staging:
            out_specs.append(VMEM)
            out_shape.append(pltpu.VMEM(tokens.shape, tokens.dtype))
            scratch.append(pltpu.SemaphoreType.DMA((-(-many // min(256, many)),)))
    outs = pl.pallas_call(
        functools.partial(pick_kernel, step, size, lo, streams, held, piece, staging),
        grid_spec=pltpu.PrefetchScalarGridSpec(
            num_scalar_prefetch=1,
            grid=(),
            in_specs=in_specs,
            out_specs=out_specs,
            scratch_shapes=scratch,
        ),
        out_shape=out_shape,
        compiler_params=pltpu.CompilerParams(vmem_limit_bytes=(4 if piece is None else 16) * MIB),
        cost_estimate=pl.CostEstimate(flops=0, bytes_accessed=1024, transcendentals=0),
        name="pick",
    )(table, *operands)
    return outs[: len(streams)], list(outs[len(streams) :])


def dense_kernel(index, down, up, out):
    width = down.shape[2]
    out[:, :, :width] = down[...]
    out[:, :, width:] = up[...]


def dense(adapter_ids, owner_map, down_pool, up_pool):
    held, rank, width = down_pool.shape
    columns = up_pool.shape[2]
    slots = owner_map[adapter_ids] - lax.axis_index("dp") * held
    here = (slots >= 0) & (slots < held)
    index = jnp.sum(jnp.where(here, slots, 0), axis=1).astype(jnp.int32)
    many = index.shape[0]
    send = pl.pallas_call(
        dense_kernel,
        grid_spec=pltpu.PrefetchScalarGridSpec(
            num_scalar_prefetch=1,
            grid=(many,),
            in_specs=[
                pl.BlockSpec((1, rank, width), lambda j, index: (index[j], 0, 0)),
                pl.BlockSpec((1, rank, columns), lambda j, index: (index[j], 0, 0)),
            ],
            out_specs=pl.BlockSpec((1, rank, width + columns), lambda j, index: (j, 0, 0)),
        ),
        out_shape=jax.ShapeDtypeStruct((many, rank, width + columns), down_pool.dtype),
        name="pick_all",
    )(index, in_hbm(down_pool), in_hbm(up_pool))
    return lax.all_to_all(send, "dp", split_axis=0, concat_axis=0, tiled=True)


def request_of_rows(lengths, count, first, rows):
    at = first + lax.broadcasted_iota(jnp.int32, (rows, 1), 0)
    which = jnp.zeros((rows, 1), jnp.int32)
    end = 0
    for r in range(count - 1):
        end = end + lengths[0, r]
        which += (at >= end).astype(jnp.int32)
    return which


def code_kernel(count, kinds, routed, index, others, lengths, tokens, *refs):
    n = sum(many for _, many in kinds)
    arrays, refs = refs[:n], refs[n:]
    out, up, flag, down, sem, up_sem = refs
    rank, columns = out.shape[1] // 2, up.shape[1]
    features = tokens.shape[1]
    flag[0] = 0
    if routed:
        flag[0] = jnp.maximum(index[0, MISFIT], others[0, MISFIT])

    def source(r):
        return index[r, PLACE] if routed else index[r, 0]

    def load(r, kind, held):
        if kind == "pool":
            slot = source(r)
            parts = [(held[0].at[slot], held[1].at[slot])]
        elif kind == "several":
            block = held[0].at[source(r)]
            parts = [(block.at[:, pl.ds(0, features)], block.at[:, pl.ds(features, columns)])]
        else:
            parts = [
                (ref.at[:, pl.ds(0, features)], ref.at[:, pl.ds(features, columns)])
                for ref in held
            ]
        size = rank // len(parts)
        for p, (down_part, up_part) in enumerate(parts):
            mine = pl.ds(r * rank + p * size, size)
            pltpu.make_async_copy(down_part, down.at[mine, :], sem).start()
            pltpu.make_async_copy(up_part, up.at[mine, :], up_sem).start()

    for r in range(count):
        at, number = 0, 0
        for kind, many in kinds:
            held = arrays[at : at + many]
            at += many
            if kind == "several":
                load(r, kind, held)
            elif kind == "pool":
                number = held[0].shape[0]

                @pl.when(source(r) < number)
                def _(r=r, kind=kind, held=held):
                    load(r, kind, held)

            else:

                @pl.when(source(r) == number)
                def _(r=r, kind=kind, held=held):
                    load(r, kind, held)

                number += 1

    pltpu.make_async_copy(down, down, sem).wait()
    half = out.shape[0]
    tile = min(256, half)
    for i in range(half // tile):
        parts = []
        for side in range(2):
            first = side * half + i * tile
            full = lax.dot_general(
                tokens[first : first + tile, :],
                down[...],
                (((1,), (1,)), ((), ())),
                preferred_element_type=jnp.float32,
            )
            which = request_of_rows(lengths, count, first, tile)
            code = full[:, :rank]
            for r in range(1, count):
                code = jnp.where(which == r, full[:, r * rank : (r + 1) * rank], code)
            parts.append(code)
        out[i * tile : (i + 1) * tile, :] = jnp.concatenate(parts, axis=1)
    pltpu.make_async_copy(up, up, up_sem).wait()


def codes(index, others, lengths, tokens, sources, rank, columns):
    many, features = tokens.shape
    count = lengths.shape[1]
    routed = others is not None
    kinds = [(kind, len(held)) for kind, held in sources]
    arrays = [array for _, held in sources for array in held]
    return pl.pallas_call(
        functools.partial(code_kernel, count, kinds, routed),
        grid_spec=pltpu.PrefetchScalarGridSpec(
            num_scalar_prefetch=3,
            grid=(),
            in_specs=[VMEM] + [ANY] * len(arrays),
            out_specs=[VMEM, VMEM, pl.BlockSpec(memory_space=pltpu.SMEM)],
            scratch_shapes=[
                pltpu.VMEM((count * rank, features), tokens.dtype),
                pltpu.SemaphoreType.DMA,
                pltpu.SemaphoreType.DMA,
            ],
        ),
        out_shape=[
            jax.ShapeDtypeStruct((many // 2, 2 * rank), jnp.float32),
            jax.ShapeDtypeStruct((count * rank, columns), tokens.dtype),
            jax.ShapeDtypeStruct((1,), jnp.int32),
        ],
        compiler_params=pltpu.CompilerParams(vmem_limit_bytes=(16 if routed else 40) * MIB),
        name="codes",
    )(index, others if routed else index, lengths, in_vmem(tokens) if routed else tokens, *arrays)


def finish_kernel(count, parts, shares, tile, lengths, *refs):
    code_parts, base_parts = refs[:parts], refs[parts : parts + sum(shares)]
    up, out, hold, sem = refs[parts + sum(shares) :]
    rank = up.shape[0] // count
    code = code_parts[0][...]
    for p in range(1, parts):
        code = code + code_parts[p][...]
    half = code.shape[0]
    copies = []
    for i in range(out.shape[0] // tile):
        first = i * tile
        side, at = first // half, first % half
        mine = code[at : at + tile, side * rank : (side + 1) * rank]
        which = request_of_rows(lengths, count, first, tile)
        zero = jnp.zeros_like(mine)
        wide = jnp.concatenate([jnp.where(which == r, mine, zero) for r in range(count)], axis=1)
        delta = None
        for _ in range(3):
            part = wide.astype(jnp.bfloat16)
            wide = wide - part.astype(jnp.float32)
            term = jnp.dot(part, up[...], preferred_element_type=jnp.float32)
            delta = term if delta is None else delta + term
        rows = pl.ds(first, tile)
        left, number = 0, 0
        for share in shares:
            base = base_parts[number][rows, :]
            for p in range(1, share):
                base = base + base_parts[number + p][rows, :]
            number += share
            right = left + base.shape[1]
            total = base + ADAPTER_SCALE * delta[:, left:right]
            hold[rows, left:right] = total.astype(hold.dtype)
            left = right
        copies.append(pltpu.make_async_copy(hold.at[rows, :], out.at[rows, :], sem.at[i]))
        copies[-1].start()
    for copy in copies:
        copy.wait()


def finish(lengths, code_parts, base, up):
    many = base[0][0].shape[0]
    columns = up.shape[1]
    count = lengths.shape[1]
    parts = len(code_parts)
    tile = min(256, many // 2)
    shares = [len(share) for share in base]
    return pl.pallas_call(
        functools.partial(finish_kernel, count, parts, shares, tile),
        grid_spec=pltpu.PrefetchScalarGridSpec(
            num_scalar_prefetch=1,
            grid=(),
            in_specs=[VMEM] * (parts + sum(shares) + 1),
            out_specs=ANY,
            scratch_shapes=[
                pltpu.VMEM((many, columns), jnp.bfloat16),
                pltpu.SemaphoreType.DMA((many // tile,)),
            ],
        ),
        out_shape=jax.ShapeDtypeStruct((many, columns), jnp.bfloat16),
        compiler_params=pltpu.CompilerParams(vmem_limit_bytes=24 * MIB),
        name="finish",
    )(lengths, *code_parts, *[part for share in base for part in share], up)


def gathered(part, axis, size):
    held = [part]
    for step in range(1, size):
        held.append(lax.ppermute(part, axis, [(i, (i + step) % size) for i in range(size)]))
    return held


def route(table, down_pool, up_pool, n_dp, tokens, key_weight, swap_plans):
    rank = down_pool.shape[1]
    size = rank // 2
    half = up_pool.shape[2] // 2
    outer = [(i, i ^ 2) for i in range(n_dp)]
    middle = [(i, i + 2) for i in (2, 3)] + [(i, i - 2) for i in (4, 5)]
    over_x = [(i, i ^ 1) for i in range(n_dp)]
    got = [([], [], []), ([], [], [])]
    pieces = [(1, 0), (1, half), (0, 0), (0, half)]
    done = []
    for step in range(Z_STEPS):
        streams = [E_TABLE, O_TABLE] + ([X_TABLE] if step < X_STEPS else [])
        if step == Z_STEPS - 2:
            table, others = lax.optimization_barrier((table, swap_plans(table)))
        for part in range(2):
            known = [list(arrays) for arrays in got[part]]
            piece = pieces[step - 1] if part == 1 and 1 <= step <= len(pieces) else None
            staging = piece is not None and not done
            sends, product = pick(
                step, part * size, size, streams, table, down_pool, up_pool, known, piece,
                staging, tokens, key_weight,
            )
            if staging:
                tokens = product.pop()
            done += product
            for stream, send in zip(streams, sends):
                pairs = (outer, middle, over_x)[stream]
                got[part][stream].append(lax.ppermute(send, "dp", pairs))
    *theirs, got[1][0][-2] = lax.optimization_barrier((*done[:2], got[1][0][-2]))
    return got, theirs, done[2:], others, tokens


def shards(sizes, tokens, key_weight, down_pool, up_pool, adapter_ids, lengths, owner_map):
    n_groups, n_dp, n_tensor = sizes
    held, rank, width = down_pool.shape
    columns = up_pool.shape[2]

    def sent_on(part, step):
        pairs = [(i, (i + step) % n_tensor) for i in range(n_tensor)]
        return lax.ppermute(part, "tensor", pairs)

    def by_all_to_all():
        me = lax.axis_index("tensor")
        parts = []
        for step in range(n_tensor):
            first = lax.rem(me + step, n_tensor) * columns
            weight = lax.dynamic_slice_in_dim(key_weight, first, columns, 1)
            part = jnp.dot(tokens, weight, preferred_element_type=jnp.float32)
            parts.append(sent_on(part, step) if step else part)
        blocks = dense(adapter_ids, owner_map, down_pool, up_pool)
        member = lax.axis_index("dp")
        my_ids = lax.dynamic_index_in_dim(adapter_ids, member, 0, keepdims=False)
        index = (owner_map[my_ids] // held)[:, None]
        code, up, _ = codes(index, None, lengths, tokens, [("several", (blocks,))], rank, columns)
        return finish(lengths, gathered(code, "tensor", n_tensor), [parts], up)

    routable = n_dp == 8 and n_tensor == 2 and n_groups <= 2
    if not (routable and rank % 32 == 0 and adapter_ids.shape[1] == 4):
        return by_all_to_all()
    table = plan(held, adapter_ids, owner_map)

    def swap_plans(table):
        return gathered(table, "groups", n_groups)[-1]

    got, theirs, mine, others, at_hand = route(
        table, down_pool, up_pool, n_dp, tokens, key_weight, swap_plans
    )
    base = [[here, sent_on(there, 1)] for here, there in zip(mine, theirs)]
    sources = [("pool", (in_hbm(down_pool), in_hbm(up_pool)))]
    for stream in (2, 0, 1):
        sources += [("block", pair) for pair in zip(got[0][stream], got[1][stream])]
    code, up, misfit = codes(table, others, lengths, at_hand, sources, rank, columns)
    keys = finish(lengths, gathered(code, "tensor", n_tensor), base, up)
    return lax.cond(misfit[0] == 0, lambda: keys, by_all_to_all)


def solution(mesh):
    placed = (
        P(("groups", "dp"), "tensor"),
        P("tensor", None),
        P("dp", None, "tensor"),
        P("dp", None, "tensor"),
        P("groups", None),
        P(("groups", "dp"), None),
        P("groups"),
    )
    sizes = tuple(mesh.shape[name] for name in ("groups", "dp", "tensor"))
    return jax.shard_map(
        functools.partial(shards, sizes),
        mesh=mesh,
        in_specs=placed,
        out_specs=P(("groups", "dp"), "tensor"),
        check_vma=False,
    )
```

```python
import functools

import jax
import jax.numpy as jnp
from jax import lax
from jax.experimental import pallas as pl
from jax.experimental.pallas import tpu as pltpu
from jax.sharding import PartitionSpec as P

ADAPTER_SCALE = 2.0
MIB = 1 << 20
ANY = pl.BlockSpec(memory_space=pl.ANY)
VMEM = pl.BlockSpec(memory_space=pltpu.VMEM)


def in_vmem(x):
    return pltpu.with_memory_space_constraint(x, pltpu.VMEM)


def in_hbm(x):
    return pltpu.with_memory_space_constraint(x, pltpu.HBM)


X_STEPS = 4
Z_STEPS = 6
NEVER = 1000.0
E_TABLE, O_TABLE, X_TABLE, PLACE, MISFIT = range(5)


def plan_kernel(held, planes, req, ids, owner_map, out):
    n = planes * req
    member = lax.axis_index("dp")
    plane, column = member // 2, member % 2
    lane = lax.broadcasted_iota(jnp.int32, (n, 128), 1)
    sub = lax.broadcasted_iota(jnp.int32, (n, 128), 0)
    lane_f, sub_f = lane.astype(jnp.float32), sub.astype(jnp.float32)

    def row_of(at):
        return sum([(at >= q * req).astype(jnp.float32) for q in range(1, planes)])

    dest_i, dest_k = row_of(lane), row_of(sub)

    def entries(c):
        by_lane = [jnp.full((n, 128), -1.0, jnp.float32) for _ in range(5)]
        by_sub = [jnp.full((n, 128), -2.0, jnp.float32) for _ in range(5)]
        for i in range(n):
            slot = owner_map[ids[i % req, 2 * (i // req) + c]]
            owner = slot // held
            values = (slot, owner, owner // 2, owner % 2, slot - owner * held)
            for v, value in enumerate(values):
                value = value.astype(jnp.float32)
                by_lane[v] = jnp.where(lane == i, value, by_lane[v])
                by_sub[v] = jnp.where(sub == i, value, by_sub[v])
        return by_lane, by_sub

    def over_x(by_lane, by_sub, c):
        (slot_i, owner_i, src_i, col_i, _), (slot_k, owner_k, src_k, col_k, _) = by_lane, by_sub
        c = c.astype(jnp.float32)
        same = slot_i == slot_k
        key_i = jnp.where(col_i == c, -1.0, jnp.abs(dest_i - src_i) * n + (n - 1 - lane_f))
        key_k = jnp.where(col_k == c, -1.0, jnp.abs(dest_k - src_k) * n + (n - 1 - sub_f))
        best_i = jnp.max(jnp.where(same, key_k, -1.0), axis=0, keepdims=True)
        best_k = jnp.max(jnp.where(same, key_i, -1.0), axis=1, keepdims=True)
        ahead = (key_k == best_k) & (key_k >= 0) & (owner_k == owner_i) & (key_k > best_i)
        pos = jnp.sum(jnp.where(ahead, 1.0, 0.0), axis=0, keepdims=True)
        return pos, (key_i == best_i) & (key_i >= 0)

    row = lax.broadcasted_iota(jnp.int32, (8, 128), 0)
    lane8 = lax.broadcasted_iota(jnp.int32, (8, 128), 1).astype(jnp.float32)
    row_f = row.astype(jnp.float32)
    links = planes - 1
    up = row < links
    last = float(planes - 1)
    link = jnp.where(up, row_f, row_f - links)

    def top(x):
        return jnp.broadcast_to(x[0:1, :], (8, 128))

    def schedule(by_lane, by_sub, xpos, c):
        slot_i, _, src_i, col_i, _ = by_lane
        same = slot_i == by_sub[0]
        dest, src = top(dest_i), top(src_i)
        d_dest, d_src = jnp.where(up, dest, last - dest), jnp.where(up, src, last - src)

        def beyond(sign):
            more = same & ((dest_k - dest_i) * sign > 0)
            return top(jnp.max(jnp.where(more, 1.0, 0.0), axis=0, keepdims=True))

        farther = jnp.where(up, beyond(1.0), beyond(-1.0))
        valid = (row < 2 * links) & (lane8 < n)
        lead = valid & (farther == 0.0) & (d_dest > d_src)
        on = lead & (d_src <= link) & (d_dest > link)
        starts = d_src == link
        local = top(col_i) == c.astype(jnp.float32)
        first = jnp.where(local, 0.0, top(jnp.broadcast_to(xpos, (8, 128))) + 1)
        ready = jnp.where(starts, first, NEVER)
        pos = jnp.full((8, 128), NEVER, jnp.float32)
        for t in range(Z_STEPS):
            open_ = on & (ready <= t) & (pos >= NEVER)
            key = jnp.where(open_, d_dest * 128 + (127 - lane8), -1.0)
            chosen = open_ & (key == jnp.max(key, axis=1, keepdims=True))
            pos = jnp.where(chosen, float(t), pos)
            before = jnp.concatenate([pos[7:8, :], pos[0:7, :]], axis=0)
            ready = jnp.where(starts, first, before + 1)
        misfit = jnp.max(jnp.where(on & (pos >= NEVER), 1.0, 0.0), axis=1, keepdims=True)
        return same, dest, src, local, on, starts, pos, jnp.max(misfit, axis=0, keepdims=True)

    by_lane, by_sub = entries(column)
    within_i = by_lane[4]
    xpos, _ = over_x(by_lane, by_sub, column)
    same, dest, src, local, on, starts, pos, misfit = schedule(by_lane, by_sub, xpos, column)
    other_lane, other_sub = entries(1 - column)
    other_xpos, other_lead = over_x(other_lane, other_sub, 1 - column)
    other_misfit = schedule(other_lane, other_sub, other_xpos, 1 - column)[-1]
    misfit = jnp.maximum(misfit, other_misfit)

    from_x = float(held)
    from_e = from_x + X_STEPS
    from_o = from_e + Z_STEPS
    own = jnp.where(local, top(within_i), from_x + top(jnp.broadcast_to(xpos, (8, 128))))

    def table(hit, source):
        return jnp.sum(jnp.where(hit, source + 1, 0.0), axis=1, keepdims=True) - 1

    def only(which, x):
        return jnp.sum(jnp.where(row == which, x, 0.0), axis=0, keepdims=True)

    def sent(which, passing_from):
        hit = only(which, jnp.where(on, 1.0, 0.0)) == 1.0
        fresh = only(which, jnp.where(starts, 1.0, 0.0)) == 1.0
        at, earlier = only(which, pos), only(which - 1, pos)
        source = jnp.where(fresh, own, passing_from + earlier)
        return table(hit & (at == row_f), source)

    e_row = jnp.where(plane % 2 == 0, plane, links + (planes - 1 - plane))
    o_row = jnp.where(plane == 1, 1, jnp.where(plane == 2, links + 1, 7))
    e_table = sent(e_row, from_o)
    o_table = sent(o_row, from_e)
    (_, owner_o, _, _, within_o) = other_lane
    mine = top(owner_o) == member.astype(jnp.float32)
    other_lead8 = top(jnp.where(other_lead, 1.0, 0.0)) == 1.0
    other_xpos8 = top(jnp.broadcast_to(other_xpos, (8, 128)))
    x_table = table(mine & other_lead8 & (other_xpos8 == row_f), top(within_o))

    arrival = jnp.zeros((8, 128), jnp.float32)
    for which in range(2 * links):
        one = jnp.broadcast_to(pos[which : which + 1, :], (n, 128))
        one_on = jnp.broadcast_to(jnp.where(on, 1.0, 0.0)[which : which + 1, :], (n, 128))
        by_k = jnp.sum(jnp.where((lane == sub) & (one_on == 1.0), one + 1, 0.0), axis=1, keepdims=True)
        arrives = jnp.max(jnp.where(same, by_k, 0.0), axis=0, keepdims=True) - 1
        if which < links:
            hit = (dest > src) & (dest == which + 1)
        else:
            hit = (dest < src) & (last - dest == which - links + 1)
        arrival = jnp.where(hit, arrives, arrival)
    odd = dest - 2 * jnp.floor(dest * 0.5)
    outer = jnp.where(dest > src, odd, 1 - odd) == 1.0
    final = jnp.where(dest == src, own, jnp.where(outer, from_e, from_o) + arrival)
    my_rows = lane8 == (plane * req).astype(jnp.float32) + row_f
    place = jnp.sum(jnp.where(my_rows & (row < req), final, 0.0), axis=1, keepdims=True)
    place = jnp.where(misfit == 1.0, 0.0, place)
    result = jnp.zeros((8, 128), jnp.float32)
    for at, values in ((E_TABLE, e_table), (O_TABLE, o_table), (X_TABLE, x_table), (PLACE, place), (MISFIT, misfit)):
        result = jnp.where(lane8 == at, values, result)
    out[...] = result.astype(jnp.int32)


def plan(held, adapter_ids, owner_map):
    rows, req = adapter_ids.shape
    return pl.pallas_call(
        functools.partial(plan_kernel, held, rows // 2, req),
        grid_spec=pltpu.PrefetchScalarGridSpec(
            num_scalar_prefetch=2, grid=(), in_specs=[], out_specs=VMEM
        ),
        out_shape=jax.ShapeDtypeStruct((8, 128), jnp.int32),
        compiler_params=pltpu.CompilerParams(vmem_limit_bytes=4 * MIB),
        name="plan",
    )(adapter_ids.T, owner_map)


def pick_kernel(step, size, lo, streams, held, piece, table, down, up, *refs):
    at = 0
    got = []
    for many in held:
        got.append(refs[at : at + many])
        at += many
    refs = list(refs[at:])
    if piece is not None:
        tokens, weight = refs.pop(0), refs.pop(0)
        held_weight, weight_sem = refs.pop(-2), refs.pop(-1)
        distance, shift = piece
        columns, wide = up.shape[2], held_weight.shape[1]
        to = lax.rem(lax.axis_index("tensor") + distance, 2)
        first = pl.multiple_of(to * columns + shift, 128)
        load = pltpu.make_async_copy(weight.at[:, pl.ds(first, wide)], held_weight, weight_sem)
        load.start()
    outs, sem = refs[: len(streams)], refs[-1]
    slots, _, width = down.shape
    from_x, from_e, from_o = slots, slots + X_STEPS, slots + X_STEPS + Z_STEPS
    over_x = [(from_x + t, ref) for t, ref in enumerate(got[2])]
    outer = [(from_e + t, ref) for t, ref in enumerate(got[0])]
    middle = [(from_o + t, ref) for t, ref in enumerate(got[1])]
    sources = {E_TABLE: over_x + middle, O_TABLE: over_x + outer, X_TABLE: []}
    rows = pl.ds(lo, size)
    for i, stream in enumerate(streams):
        code, out = table[step, stream], outs[i]

        @pl.when((code >= 0) & (code < slots))
        def _(code=code, out=out, i=i):
            pltpu.make_async_copy(
                down.at[code, rows, :], out.at[:, pl.ds(0, width)], sem.at[i]
            ).start()
            pltpu.make_async_copy(
                up.at[code, rows, :], out.at[:, pl.ds(width, up.shape[2])], sem.at[i]
            ).start()

        for number, ref in sources[stream]:

            @pl.when(code == number)
            def _(ref=ref, out=out, i=i):
                pltpu.make_async_copy(ref, out, sem.at[i]).start()

    if piece is not None:
        load.wait()
        product = refs[len(streams)]
        tile = min(256, product.shape[0])
        for at in range(0, product.shape[0], tile):
            product[at : at + tile, :] = jnp.dot(
                tokens[at : at + tile, :],
                held_weight[...],
                preferred_element_type=jnp.float32,
            )

    for i, stream in enumerate(streams):

        @pl.when(table[step, stream] >= 0)
        def _(i=i):
            pltpu.make_async_copy(outs[i], outs[i], sem.at[i]).wait()


def pick(step, lo, size, streams, table, down_pool, up_pool, got, piece, tokens, key_weight):
    many = tokens.shape[0]
    columns = up_pool.shape[2]
    wide = down_pool.shape[2] + columns
    held = [len(arrays) for arrays in got]
    operands = [in_hbm(down_pool), in_hbm(up_pool)] + [a for arrays in got for a in arrays]
    in_specs = [ANY] * len(operands)
    out_specs = [ANY] * len(streams)
    out_shape = [pltpu.VMEM((size, wide), down_pool.dtype)] * len(streams)
    scratch = [pltpu.SemaphoreType.DMA((len(streams),))]
    if piece is not None:
        operands += [in_vmem(tokens), in_hbm(key_weight)]
        in_specs += [VMEM, ANY]
        out_specs.append(VMEM)
        out_shape.append(jax.ShapeDtypeStruct((many, columns // 2), jnp.float32))
        scratch += [
            pltpu.VMEM((tokens.shape[1], columns // 2), key_weight.dtype),
            pltpu.SemaphoreType.DMA,
        ]
    outs = pl.pallas_call(
        functools.partial(pick_kernel, step, size, lo, streams, held, piece),
        grid_spec=pltpu.PrefetchScalarGridSpec(
            num_scalar_prefetch=1,
            grid=(),
            in_specs=in_specs,
            out_specs=out_specs,
            scratch_shapes=scratch,
        ),
        out_shape=out_shape,
        compiler_params=pltpu.CompilerParams(vmem_limit_bytes=(4 if piece is None else 16) * MIB),
        name="pick",
    )(table, *operands)
    return outs[: len(streams)], outs[len(streams) :]


def dense_kernel(index, down, up, out):
    width = down.shape[2]
    out[:, :, :width] = down[...]
    out[:, :, width:] = up[...]


def dense(adapter_ids, owner_map, down_pool, up_pool):
    held, rank, width = down_pool.shape
    columns = up_pool.shape[2]
    slots = owner_map[adapter_ids] - lax.axis_index("dp") * held
    here = (slots >= 0) & (slots < held)
    index = jnp.sum(jnp.where(here, slots, 0), axis=1).astype(jnp.int32)
    many = index.shape[0]
    send = pl.pallas_call(
        dense_kernel,
        grid_spec=pltpu.PrefetchScalarGridSpec(
            num_scalar_prefetch=1,
            grid=(many,),
            in_specs=[
                pl.BlockSpec((1, rank, width), lambda j, index: (index[j], 0, 0)),
                pl.BlockSpec((1, rank, columns), lambda j, index: (index[j], 0, 0)),
            ],
            out_specs=pl.BlockSpec((1, rank, width + columns), lambda j, index: (j, 0, 0)),
        ),
        out_shape=jax.ShapeDtypeStruct((many, rank, width + columns), down_pool.dtype),
        name="pick_all",
    )(index, in_hbm(down_pool), in_hbm(up_pool))
    return lax.all_to_all(send, "dp", split_axis=0, concat_axis=0, tiled=True)


def stage_kernel(source, out, sem):
    copy = pltpu.make_async_copy(source, out, sem)
    copy.start()
    copy.wait()


def stage(x):
    return pl.pallas_call(
        stage_kernel,
        in_specs=[ANY],
        out_specs=VMEM,
        out_shape=pltpu.VMEM(x.shape, x.dtype),
        scratch_shapes=[pltpu.SemaphoreType.DMA],
        compiler_params=pltpu.CompilerParams(vmem_limit_bytes=4 * MIB),
        name="stage",
    )(in_hbm(x))


def request_of_rows(lengths, count, first, rows):
    at = first + lax.broadcasted_iota(jnp.int32, (rows, 1), 0)
    which = jnp.zeros((rows, 1), jnp.int32)
    end = 0
    for r in range(count - 1):
        end = end + lengths[0, r]
        which += (at >= end).astype(jnp.int32)
    return which


def code_kernel(count, kinds, routed, index, others, lengths, tokens, *refs):
    n = sum(many for _, many in kinds)
    arrays, refs = refs[:n], refs[n:]
    out, up, flag, down, sem, up_sem = refs
    rank, columns = out.shape[1] // 2, up.shape[1]
    features = tokens.shape[1]
    flag[0] = 0
    if routed:
        flag[0] = jnp.maximum(index[0, MISFIT], others[0, MISFIT])

    def source(r):
        return index[r, PLACE] if routed else index[r, 0]

    def load(r, kind, held):
        if kind == "pool":
            slot = source(r)
            parts = [(held[0].at[slot], held[1].at[slot])]
        elif kind == "several":
            block = held[0].at[source(r)]
            parts = [(block.at[:, pl.ds(0, features)], block.at[:, pl.ds(features, columns)])]
        else:
            parts = [
                (ref.at[:, pl.ds(0, features)], ref.at[:, pl.ds(features, columns)])
                for ref in held
            ]
        size = rank // len(parts)
        for p, (down_part, up_part) in enumerate(parts):
            mine = pl.ds(r * rank + p * size, size)
            pltpu.make_async_copy(down_part, down.at[mine, :], sem).start()
            pltpu.make_async_copy(up_part, up.at[mine, :], up_sem).start()

    for r in range(count):
        at, number = 0, 0
        for kind, many in kinds:
            held = arrays[at : at + many]
            at += many
            if kind == "several":
                load(r, kind, held)
            elif kind == "pool":
                number = held[0].shape[0]

                @pl.when(source(r) < number)
                def _(r=r, kind=kind, held=held):
                    load(r, kind, held)

            else:

                @pl.when(source(r) == number)
                def _(r=r, kind=kind, held=held):
                    load(r, kind, held)

                number += 1

    pltpu.make_async_copy(down, down, sem).wait()
    half = out.shape[0]
    tile = min(256, half)
    for i in range(half // tile):
        parts = []
        for side in range(2):
            first = side * half + i * tile
            full = lax.dot_general(
                tokens[first : first + tile, :],
                down[...],
                (((1,), (1,)), ((), ())),
                preferred_element_type=jnp.float32,
            )
            which = request_of_rows(lengths, count, first, tile)
            code = full[:, :rank]
            for r in range(1, count):
                code = jnp.where(which == r, full[:, r * rank : (r + 1) * rank], code)
            parts.append(code)
        out[i * tile : (i + 1) * tile, :] = jnp.concatenate(parts, axis=1)
    pltpu.make_async_copy(up, up, up_sem).wait()


def codes(index, others, lengths, tokens, sources, rank, columns):
    many, features = tokens.shape
    count = lengths.shape[1]
    routed = others is not None
    kinds = [(kind, len(held)) for kind, held in sources]
    arrays = [array for _, held in sources for array in held]
    return pl.pallas_call(
        functools.partial(code_kernel, count, kinds, routed),
        grid_spec=pltpu.PrefetchScalarGridSpec(
            num_scalar_prefetch=3,
            grid=(),
            in_specs=[VMEM] + [ANY] * len(arrays),
            out_specs=[VMEM, VMEM, pl.BlockSpec(memory_space=pltpu.SMEM)],
            scratch_shapes=[
                pltpu.VMEM((count * rank, features), tokens.dtype),
                pltpu.SemaphoreType.DMA,
                pltpu.SemaphoreType.DMA,
            ],
        ),
        out_shape=[
            jax.ShapeDtypeStruct((many // 2, 2 * rank), jnp.float32),
            jax.ShapeDtypeStruct((count * rank, columns), tokens.dtype),
            jax.ShapeDtypeStruct((1,), jnp.int32),
        ],
        compiler_params=pltpu.CompilerParams(vmem_limit_bytes=(16 if routed else 40) * MIB),
        name="codes",
    )(index, others if routed else index, lengths, in_vmem(tokens) if routed else tokens, *arrays)


def finish_kernel(count, parts, shares, tile, lengths, *refs):
    code_parts, base_parts = refs[:parts], refs[parts : parts + sum(shares)]
    up, out, hold, sem = refs[parts + sum(shares) :]
    rank = up.shape[0] // count
    code = code_parts[0][...]
    for p in range(1, parts):
        code = code + code_parts[p][...]
    half = code.shape[0]
    copies = []
    for i in range(out.shape[0] // tile):
        first = i * tile
        side, at = first // half, first % half
        mine = code[at : at + tile, side * rank : (side + 1) * rank]
        which = request_of_rows(lengths, count, first, tile)
        zero = jnp.zeros_like(mine)
        wide = jnp.concatenate([jnp.where(which == r, mine, zero) for r in range(count)], axis=1)
        delta = None
        for _ in range(3):
            part = wide.astype(jnp.bfloat16)
            wide = wide - part.astype(jnp.float32)
            term = jnp.dot(part, up[...], preferred_element_type=jnp.float32)
            delta = term if delta is None else delta + term
        rows = pl.ds(first, tile)
        left, number = 0, 0
        for share in shares:
            base = base_parts[number][rows, :]
            for p in range(1, share):
                base = base + base_parts[number + p][rows, :]
            number += share
            right = left + base.shape[1]
            total = base + ADAPTER_SCALE * delta[:, left:right]
            hold[rows, left:right] = total.astype(hold.dtype)
            left = right
        copies.append(pltpu.make_async_copy(hold.at[rows, :], out.at[rows, :], sem.at[i]))
        copies[-1].start()
    for copy in copies:
        copy.wait()


def finish(lengths, code_parts, base, up):
    many = base[0][0].shape[0]
    columns = up.shape[1]
    count = lengths.shape[1]
    parts = len(code_parts)
    tile = min(256, many // 2)
    shares = [len(share) for share in base]
    return pl.pallas_call(
        functools.partial(finish_kernel, count, parts, shares, tile),
        grid_spec=pltpu.PrefetchScalarGridSpec(
            num_scalar_prefetch=1,
            grid=(),
            in_specs=[VMEM] * (parts + sum(shares) + 1),
            out_specs=ANY,
            scratch_shapes=[
                pltpu.VMEM((many, columns), jnp.bfloat16),
                pltpu.SemaphoreType.DMA((many // tile,)),
            ],
        ),
        out_shape=jax.ShapeDtypeStruct((many, columns), jnp.bfloat16),
        compiler_params=pltpu.CompilerParams(vmem_limit_bytes=24 * MIB),
        name="finish",
    )(lengths, *code_parts, *[part for share in base for part in share], up)


def gathered(part, axis, size):
    held = [part]
    for step in range(1, size):
        held.append(lax.ppermute(part, axis, [(i, (i + step) % size) for i in range(size)]))
    return held


def route(table, down_pool, up_pool, n_dp, tokens, key_weight, swap_plans):
    rank = down_pool.shape[1]
    size = rank // 2
    half = up_pool.shape[2] // 2
    outer = [(i, i ^ 2) for i in range(n_dp)]
    middle = [(i, i + 2) for i in (2, 3)] + [(i, i - 2) for i in (4, 5)]
    over_x = [(i, i ^ 1) for i in range(n_dp)]
    got = [([], [], []), ([], [], [])]
    pieces = [(1, 0), (1, half), (0, 0), (0, half)]
    done = []
    for step in range(Z_STEPS):
        streams = [E_TABLE, O_TABLE] + ([X_TABLE] if step < X_STEPS else [])
        if step == Z_STEPS - 2:
            table, others = lax.optimization_barrier((table, swap_plans(table)))
        for part in range(2):
            known = [list(arrays) for arrays in got[part]]
            piece = pieces[step - 1] if part == 1 and 1 <= step <= len(pieces) else None
            sends, product = pick(
                step, part * size, size, streams, table, down_pool, up_pool, known, piece,
                tokens, key_weight,
            )
            done += product
            for stream, send in zip(streams, sends):
                pairs = (outer, middle, over_x)[stream]
                got[part][stream].append(lax.ppermute(send, "dp", pairs))
    return got, done, others


def shards(sizes, tokens, key_weight, down_pool, up_pool, adapter_ids, lengths, owner_map):
    n_groups, n_dp, n_tensor = sizes
    held, rank, width = down_pool.shape
    columns = up_pool.shape[2]

    def sent_on(part, step):
        pairs = [(i, (i + step) % n_tensor) for i in range(n_tensor)]
        return lax.ppermute(part, "tensor", pairs)

    def by_all_to_all():
        me = lax.axis_index("tensor")
        parts = []
        for step in range(n_tensor):
            first = lax.rem(me + step, n_tensor) * columns
            weight = lax.dynamic_slice_in_dim(key_weight, first, columns, 1)
            part = jnp.dot(tokens, weight, preferred_element_type=jnp.float32)
            parts.append(sent_on(part, step) if step else part)
        blocks = dense(adapter_ids, owner_map, down_pool, up_pool)
        member = lax.axis_index("dp")
        my_ids = lax.dynamic_index_in_dim(adapter_ids, member, 0, keepdims=False)
        index = (owner_map[my_ids] // held)[:, None]
        code, up, _ = codes(index, None, lengths, tokens, [("several", (blocks,))], rank, columns)
        return finish(lengths, gathered(code, "tensor", n_tensor), [parts], up)

    routable = n_dp == 8 and n_tensor == 2 and n_groups <= 2
    if not (routable and rank % 32 == 0 and adapter_ids.shape[1] == 4):
        return by_all_to_all()
    table = plan(held, adapter_ids, owner_map)
    at_hand = stage(tokens)

    def swap_plans(table):
        return gathered(table, "groups", n_groups)[-1]

    got, done, others = route(
        table, down_pool, up_pool, n_dp, at_hand, key_weight, swap_plans
    )
    base = [[here, sent_on(there, 1)] for there, here in zip(done[:2], done[2:])]
    sources = [("pool", (in_hbm(down_pool), in_hbm(up_pool)))]
    for stream in (2, 0, 1):
        sources += [("block", pair) for pair in zip(got[0][stream], got[1][stream])]
    code, up, misfit = codes(table, others, lengths, at_hand, sources, rank, columns)
    keys = finish(lengths, gathered(code, "tensor", n_tensor), base, up)
    return lax.cond(misfit[0] == 0, lambda: keys, by_all_to_all)


def solution(mesh):
    placed = (
        P(("groups", "dp"), "tensor"),
        P("tensor", None),
        P("dp", None, "tensor"),
        P("dp", None, "tensor"),
        P("groups", None),
        P(("groups", "dp"), None),
        P("groups"),
    )
    sizes = tuple(mesh.shape[name] for name in ("groups", "dp", "tensor"))
    return jax.shard_map(
        functools.partial(shards, sizes),
        mesh=mesh,
        in_specs=placed,
        out_specs=P(("groups", "dp"), "tensor"),
        check_vma=False,
    )
```
